32 devices in a mesh: dp: 4 (over z), ctx: 8 (over y, x, core).
Axes of the slice: x: 2, y: 2, z: 4, core: 2. Of those that a mesh axis runs over, the one named last changes fastest.
Arguments:
- hidden: bfloat16 [4, 2048, 2048], P('dp', 'ctx'), may hold values from -6 to 6
- x_weight: bfloat16 [2048, 2048], replicated, may hold values from -0.125 to 0.125
- state_weight: bfloat16 [2048, 160], replicated, may hold values from -0.125 to 0.125
- log_rates: float32 [32], replicated, as said below
- step_bias: float32 [32], replicated, may hold values from -1 to 1
- out_gain: float32 [2048], replicated, may hold values from 0.5 to 1.5
- cotangent: bfloat16 [4, 2048, 2048], P('dp', 'ctx'), may hold values from -6 to 6
Outputs:
- mixed: bfloat16 [4, 2048, 2048], P('dp', 'ctx')
- grad_x: float32 [2048, 2048], P('ctx')
- grad_small: float32 [2048, 160], P('ctx')
The draws below stay inside these ranges and needn't reach their ends.
Inputs may be any that keep to these rules, and one draw needn't show every extreme that they name: Each head's rate exp(log_rates) lies between 0.05 / 2048 and 1 / 30.
All inputs are finite; a program needn't handle non-finite values.
Results may differ from the reference program's by a relative error of at most 0.0049.
Values may be sent and summed in bfloat16 or wider, within the bound.
No kernel may reach another device: no remote copies, remote signals or barrier semaphores. Data moves between devices by JAX's collectives and lax.ppermute only.
A program may use at most 192 MiB of HBM per device.

```python
import jax
import jax.numpy as jnp
from jax import lax

D = 2048
HEAD = 64
STATE = 64
ROWS = 256
HEADS = 32
SMALL_WIDTH = 160
LENGTH = 2048
SEQS = 4
N_CTX = 8


def draw_log_rates(key, part):
    key = jax.random.fold_in(key, 11)
    first_key, second_key, third_key, fourth_key = jax.random.split(key, 4)
    fast_count = HEADS // 4
    middle_count = HEADS // 4
    ranking = jax.random.permutation(first_key, HEADS)
    fast_rates = jnp.log(jax.random.uniform(second_key, (HEADS,), minval=1.0 / 50.0, maxval=1.0 / 30.0))
    middle_rates = jnp.log(jax.random.uniform(fourth_key, (HEADS,), minval=1.0 / 800.0, maxval=1.0 / 300.0))
    slow_rates = jnp.log(jax.random.uniform(third_key, (HEADS,), minval=0.05, maxval=0.5) / LENGTH)
    chosen = jnp.where(ranking < fast_count, fast_rates, jnp.where(ranking < fast_count + middle_count, middle_rates, slow_rates))
    return chosen.astype(jnp.float32)


def levels(rng, shape, shards, least, top_value):
    def one(dim, parts):
        steps = jax.random.uniform(jax.random.fold_in(jax.random.fold_in(rng, 6), dim), (parts,), jnp.float32, least / len(shards), top_value / len(shards))
        return jnp.repeat(jnp.exp(steps), shape[dim] // parts).reshape((-1,) + (1,) * (len(shape) - dim - 1))

    gain = one(*shards[0])
    for cut in shards[1:]:
        gain = gain * one(*cut)
    return gain


def bell_draw(own_key, extent, width, bound, cuts=(), kind=jnp.bfloat16):
    level = levels(own_key, extent, cuts, -0.22, 0.18) if cuts else 1.0
    entries = jax.random.normal(own_key, extent, jnp.float32) * width * level
    return jnp.minimum(jnp.maximum(entries, -bound), bound).astype(kind)


def setup_inputs(seed: int = 0) -> dict:
    key_list = jax.random.split(jax.random.key(seed), 8)
    hidden = bell_draw(key_list[0], (SEQS, LENGTH, D), 1.0, 6.0, ((0, 4), (1, 8)))
    x_weight = bell_draw(key_list[1], (D, D), D ** -0.5, 0.125)
    state_weight = bell_draw(key_list[2], (D, SMALL_WIDTH), D ** -0.5, 0.125)
    log_rates = draw_log_rates(jax.random.fold_in(key_list[7], 71), 0)
    step_bias = jnp.clip(jax.random.uniform(key_list[4], (HEADS,), jnp.float32, -1.0, 1.0), -1.0, 1.0)
    out_gain = jnp.clip(1.0 + 0.1 * jax.random.normal(key_list[5], (D,), jnp.float32), 0.5, 1.5)
    cotangent = bell_draw(key_list[6], (SEQS, LENGTH, D), 1.0, 6.0, ((0, 4), (1, 8)))
    return {"hidden": hidden, "x_weight": x_weight, "state_weight": state_weight, "log_rates": log_rates, "step_bias": step_bias, "out_gain": out_gain, "cotangent": cotangent}


precise = lax.Precision.HIGHEST

def split_small(projected, log_rates, step_bias):
    inputs_b = projected[:, :STATE]
    inputs_c = projected[:, STATE:2 * STATE]
    step_size = jax.nn.softplus(projected[:, 2 * STATE:] + step_bias[None, :])
    cumlog = jnp.cumsum(-jnp.exp(log_rates)[None, :] * step_size, axis=0)
    return (inputs_b, inputs_c, step_size, cumlog)

def block_state(values_in, projected, log_rates, step_bias):
    inputs_b, inputs_c, step_size, cumlog = split_small(projected, log_rates, step_bias)
    block_rows, channels = values_in.shape
    head_count = channels // HEAD
    per_head = values_in.reshape(block_rows, head_count, HEAD)
    weighting = jnp.exp(cumlog[-1][None, :] - cumlog) * step_size
    local_end = jnp.einsum('sh,shp,sn->hpn', weighting, per_head, inputs_b, precision=precise)
    return (jnp.exp(cumlog[-1]), local_end)

def forward_y(values_in, projected, state_in, log_rates, step_bias, out_gain):
    inputs_b, inputs_c, step_size, cumlog = split_small(projected, log_rates, step_bias)
    block_rows, channels = values_in.shape
    head_count = channels // HEAD
    per_head = values_in.reshape(block_rows, head_count, HEAD)
    log_heads = cumlog.T
    log_gap = log_heads[:, :, None] - log_heads[:, None, :]
    position = jnp.arange(block_rows)
    causal = position[:, None] >= position[None, :]
    decay_mat = jnp.exp(jnp.where(causal[None, :, :], log_gap, -jnp.inf)) * step_size.T[:, None, :]
    scores = jnp.dot(inputs_c, inputs_b.T, precision=precise)
    mixing = decay_mat * scores[None, :, :]
    inner = jnp.einsum('hts,shp->thp', mixing, per_head, precision=precise)
    readout = jnp.einsum('tn,hpn->thp', inputs_c, state_in, precision=precise) * jnp.exp(cumlog)[:, :, None]
    unnormed = (inner + readout).reshape(block_rows, channels)
    rescale = lax.rsqrt(lax.optimization_barrier(jnp.mean(unnormed * unnormed, axis=1, keepdims=True)) + 1e-05)
    return unnormed * rescale * out_gain[None, :]

def run_stream(values_all, projected_all, log_rates, step_bias, out_gain):
    head_count = D // HEAD

    def one_sequence(members):
        value_blocks = members[0].reshape(N_CTX, ROWS, D)
        proj_blocks = members[1].reshape(N_CTX, ROWS, members[1].shape[-1])

        def advance(carried, blocks):
            output = forward_y(blocks[0], blocks[1], carried, log_rates, step_bias, out_gain)
            totals, local_end = block_state(blocks[0], blocks[1], log_rates, step_bias)
            return (totals[:, None, None] * carried + local_end, output)
        initial = jnp.zeros((head_count, HEAD, STATE), jnp.float32)
        ignored, outputs = lax.scan(jax.checkpoint(advance), initial, (value_blocks, proj_blocks))
        return outputs.reshape(LENGTH, D)
    return lax.map(one_sequence, (values_all, projected_all))

def reference(hidden, x_weight, state_weight, log_rates, step_bias, out_gain, cotangent):
    rows_fwd = hidden.reshape(-1, D)
    rows_rc = hidden[:, ::-1, ::-1].reshape(-1, D)

    def project(rows_in):
        values = jnp.dot(rows_in, x_weight, preferred_element_type=jnp.float32).astype(jnp.bfloat16)
        projected = jnp.dot(rows_in, state_weight, preferred_element_type=jnp.float32)
        return (values.astype(jnp.float32).reshape(SEQS, LENGTH, D), projected.reshape(SEQS, LENGTH, -1))
    values_fwd, proj_fwd = project(rows_fwd)
    values_rc, proj_rc = project(rows_rc)

    def both_branches(first_values, first_proj, second_values, second_proj):
        return (run_stream(first_values, first_proj, log_rates, step_bias, out_gain), run_stream(second_values, second_proj, log_rates, step_bias, out_gain))
    outputs, pullback = jax.vjp(both_branches, values_fwd, proj_fwd, values_rc, proj_rc)
    back = outputs[1].astype(jnp.bfloat16)[:, ::-1, ::-1]
    mixed = (outputs[0] + back.astype(jnp.float32)).astype(jnp.bfloat16)
    cot_fwd = cotangent.astype(jnp.float32)
    cot_rc = cotangent[:, ::-1, ::-1].astype(jnp.float32)
    grad_vf, grad_pf, grad_vr, grad_pr = pullback((cot_fwd, cot_rc))
    grad_vf = grad_vf.astype(jnp.bfloat16).reshape(-1, D)
    grad_vr = grad_vr.astype(jnp.bfloat16).reshape(-1, D)
    grad_pf = grad_pf.astype(jnp.bfloat16).reshape(-1, grad_pf.shape[-1])
    grad_pr = grad_pr.astype(jnp.bfloat16).reshape(-1, grad_pr.shape[-1])
    grad_x = jnp.dot(rows_fwd.T, grad_vf, preferred_element_type=jnp.float32) + jnp.dot(rows_rc.T, grad_vr, preferred_element_type=jnp.float32)
    grad_small = jnp.dot(rows_fwd.T, grad_pf, preferred_element_type=jnp.float32) + jnp.dot(rows_rc.T, grad_pr, preferred_element_type=jnp.float32)
    return (mixed, grad_x, grad_small)
```

```python
import functools

import jax
import jax.numpy as jnp
from jax import lax
from jax.experimental import pallas as pl
from jax.experimental.pallas import tpu as pltpu
from jax.sharding import PartitionSpec as P

STATE = 64
GROUP = 256
LANES = 128
BF = jnp.bfloat16
F32 = jnp.float32
precise = lax.Precision.HIGHEST
ORDER = pl.BlockSpec(memory_space=pl.ANY)
SCALARS = pl.BlockSpec(memory_space=pltpu.SMEM)
PARAMS = pltpu.CompilerParams(vmem_limit_bytes=48 * 2**20)


def send(array, axis, mask):
    return lax.ppermute(array, axis, [(i, i ^ mask) for i in range(lax.axis_size(axis))])


def mm(a, b, ca=1, cb=0):
    return lax.dot_general(a, b, (((ca,), (cb,)), ((), ())), preferred_element_type=F32)


def exact(a, b, ca=1, cb=0):
    dims = (((ca,), (cb,)), ((), ()))
    return lax.dot_general(a, b, dims, precision=precise, preferred_element_type=F32)


def split(a):
    high = a.astype(BF)
    return high, (a - high.astype(F32)).astype(BF)


def split_three(a, axis):
    high, rest = split(a)
    middle, low = split(a - high.astype(F32))
    return jnp.concatenate([high, middle, low], axis=axis)


def iota(shape, axis):
    return lax.broadcasted_iota(jnp.int32, shape, axis)


def ordered(rows, branch, strict_after=False):
    t, s = iota((rows, rows), 0), iota((rows, rows), 1)
    return (t >= s) if (branch == 0) != strict_after else (t <= s)


def mirror(width):
    return (iota((width, width), 0) + iota((width, width), 1) == width - 1).astype(BF)


def spread(heads, channels, start, copies):
    head = iota((heads, GROUP if start is not None else channels), 0)
    lane = iota((heads, GROUP if start is not None else channels), 1)
    size = channels // heads
    first = 0 if start is None else start
    one = (head == lane // size + first).astype(BF)
    return jnp.concatenate([one] * copies, axis=0)


def flip_lanes(a, eye):
    parts = [mm(a[:, k : k + GROUP], eye).astype(BF) for k in range(0, a.shape[1], GROUP)]
    return jnp.concatenate(parts[::-1], axis=1)


def softplus(a):
    return jnp.maximum(a, 0.0) + jnp.log1p(jnp.exp(-jnp.abs(a)))


def whole(a):
    return pl.BlockSpec(a.shape, lambda *_: (0,) * a.ndim)


def padded(a):
    return jnp.concatenate([a, jnp.zeros((a.shape[0], LANES - a.shape[1]), a.dtype)], axis=1)


CUM, STEP = LANES, 2 * LANES


def small_kernel(
    h_ref, ws_ref, rate_ref, bias_ref,
    both_ref, nat_ref, lines_ref, cg3_ref, bf3_ref, bt_ref, weight3_ref, tot3_ref,
):
    rows, channels = h_ref.shape
    heads = rate_ref.shape[1]
    eye = mirror(GROUP)
    both_ref[:rows] = h_ref[...]
    for k in range(0, channels, GROUP):
        both_ref[rows:, channels - k - GROUP : channels - k] = mm(
            h_ref[:, k : k + GROUP], eye
        ).astype(BF)
    projected = mm(both_ref[...], ws_ref[...])
    for branch in range(2):
        p = projected[branch * rows : (branch + 1) * rows]
        b, c = p[:, :STATE], p[:, STATE : 2 * STATE]
        pre = p[:, 2 * STATE :] + bias_ref[...]
        step = softplus(pre)
        la = -jnp.exp(rate_ref[...]) * step
        cum = exact(ordered(rows, branch).astype(F32), la)
        tot = cum[rows - 1 :] if branch == 0 else cum[:1]
        fade = jnp.exp(tot - cum)
        wide_step, wide_cum = padded(step), padded(cum)
        nat_ref[branch, :, :CUM] = p[:, : 2 * STATE]
        nat_ref[branch, :, CUM:STEP] = wide_cum
        nat_ref[branch, :, STEP:] = padded(jnp.concatenate([step, pre], axis=1))
        lines_ref[branch, :heads] = wide_cum.T[:heads]
        lines_ref[branch, heads:] = wide_step.T[:heads]
        b_high, b_low = split(b)
        c_high, c_low = split(c)
        grow3 = split_three(jnp.exp(cum), 1)
        cg3_ref[branch] = jnp.concatenate(
            [c_high, c_low, c_high, grow3, jnp.zeros_like(grow3)], axis=1
        )
        bf3_ref[branch] = jnp.concatenate(
            [b_high, b_low, b_high, split_three(fade, 1), split_three(step, 1)], axis=1
        )
        bt_ref[branch] = jnp.concatenate([b_high, b_low], axis=1).T
        weight3_ref[branch] = split_three(fade * step, 1)
        tot3_ref[branch] = split_three(jnp.broadcast_to(tot, (8, heads)), 1)


def project_small(h, ws, log_rates, step_bias):
    rows, channels = h.shape
    heads = log_rates.shape[0]
    f32 = lambda *shape: jax.ShapeDtypeStruct(shape, F32)
    bf16 = lambda *shape: jax.ShapeDtypeStruct(shape, BF)
    return pl.pallas_call(
        small_kernel,
        out_shape=[
            bf16(2 * rows, channels),
            f32(2, rows, 3 * LANES),
            f32(2, 2 * heads, rows),
            bf16(2, rows, 3 * STATE + 6 * heads),
            bf16(2, rows, 3 * STATE + 6 * heads),
            bf16(2, 2 * STATE, rows),
            bf16(2, rows, 3 * heads),
            bf16(2, 8, 3 * heads),
        ],
        compiler_params=PARAMS,
        name="small",
    )(h, ws, log_rates[None], step_bias[None])


def project_kernel(both_ref, w_ref, bt_ref, weight3_ref, tot3_ref, x_ref, end_ref):
    at = pl.program_id(0)
    rows = x_ref.shape[1]
    heads = weight3_ref.shape[2] // 3
    channels = both_ref.shape[1]
    copier = spread(heads, channels, at * (GROUP * heads // channels), 3)
    values = mm(both_ref[...], w_ref[...]).astype(BF)
    for branch in range(2):
        x = values[branch * rows : (branch + 1) * rows]
        x_ref[branch] = x
        weighted = mm(weight3_ref[branch], copier) * x.astype(F32)
        both = mm(bt_ref[branch], weighted.astype(BF))
        end_ref[branch, :STATE] = both[:STATE] + both[STATE:]
        end_ref[branch, STATE:] = mm(tot3_ref[branch], copier)


def project(both, w, bt, weight3, tot3):
    rows, channels = both.shape[0] // 2, both.shape[1]
    return pl.pallas_call(
        project_kernel,
        grid=(channels // GROUP,),
        in_specs=[
            whole(both),
            pl.BlockSpec((channels, GROUP), lambda j: (0, j)),
            whole(bt),
            whole(weight3),
            whole(tot3),
        ],
        out_specs=[
            pl.BlockSpec((2, rows, GROUP), lambda j: (0, 0, j)),
            pl.BlockSpec((2, STATE + 8, GROUP), lambda j: (0, 0, j)),
        ],
        out_shape=[
            jax.ShapeDtypeStruct((2, rows, channels), BF),
            jax.ShapeDtypeStruct((2, STATE + 8, channels), F32),
        ],
        compiler_params=PARAMS,
        name="project",
    )(both, w, bt, weight3, tot3)


def own_lanes(a, k, size):
    lane = iota(a.shape, 1) // size
    return jnp.where(lane == k, a.astype(F32), 0.0).astype(BF)


def inner_kernel(x_ref, nat_ref, lines_ref, sent, left, raw_ref, score):
    at = pl.program_id(0)
    rows = x_ref.shape[1]
    heads = lines_ref.shape[1] // 2
    size = x_ref.shape[2] * pl.num_programs(0) // heads
    half = rows // 2
    per = GROUP // size

    @pl.when(at == 0)
    def _():
        for branch in range(2):
            b, c = nat_ref[branch, :, :STATE], nat_ref[branch, :, STATE : 2 * STATE]
            full = exact(c, b, 1, 1)
            score[branch] = jnp.where(ordered(rows, branch), full, 0.0)

    for branch in range(2):
        alone, later = (0, half) if branch == 0 else (half, 0)
        columns = pltpu.roll(nat_ref[branch, :, CUM:STEP], -(at * per) % LANES, 1)
        tops, bottoms = 0.0, 0.0
        for k in range(per):
            line = lines_ref[branch, pl.ds(at * per + k, 1), :]
            step = lines_ref[branch, pl.ds(heads + at * per + k, 1), :]
            xk = own_lanes(x_ref[branch], k, size)
            own = pl.ds(alone, half)
            gap = jnp.minimum(columns[alone : alone + half, k : k + 1] - line[:, alone : alone + half], 0.0)
            m = jnp.exp(gap) * score[branch, own, own] * step[:, alone : alone + half]
            tops = tops + mm(m.astype(BF), xk[alone : alone + half])
            gap = jnp.minimum(columns[later : later + half, k : k + 1] - line, 0.0)
            m = jnp.exp(gap) * score[branch, pl.ds(later, half), :] * step
            bottoms = bottoms + mm(m.astype(BF), xk)
        raw_ref[branch, pl.ds(alone, half), :] = tops
        raw_ref[branch, pl.ds(later, half), :] = bottoms


def inner(x, nat, lines, sent, left):
    _, rows, channels = x.shape
    block = pl.BlockSpec((2, rows, GROUP), lambda j: (0, 0, j))
    return pl.pallas_call(
        inner_kernel,
        grid=(channels // GROUP,),
        in_specs=[block, whole(nat), whole(lines), ORDER, ORDER],
        out_specs=block,
        out_shape=jax.ShapeDtypeStruct(x.shape, F32),
        scratch_shapes=[pltpu.VMEM((2, rows, rows), F32)],
        compiler_params=PARAMS,
        name="inner",
    )(x, nat, lines, sent, left)


class Scalars:
    def __init__(self, chips, ref=None):
        self.chips, self.ref = chips, ref
        self.bits = bits_of(chips)

    def made(self):
        place = lax.axis_index("ctx")
        chip, core = place // 2, place % 2
        at = chip ^ jnp.arange(1, self.chips)
        up = (chip ^ jnp.array(self.bits)) > chip
        reach = jnp.concatenate([at < chip, at > chip])
        left = (at[None] > at[:, None]) & (at[None] < chip)
        right = (at[None] > chip) & (at[None] < at[:, None])
        parts = [jnp.stack([core == 0, core == 1]), up, reach, left.ravel(), right.ravel()]
        return jnp.concatenate(parts).astype(F32)

    def first(self, slot):
        return self.ref[slot]

    def up(self, n):
        return self.ref[2 + n]

    def reach(self, slot, m):
        return self.ref[2 + len(self.bits) + slot * (self.chips - 1) + m]

    def between(self, slot, m, k):
        most = self.chips - 1
        return self.ref[2 + len(self.bits) + 2 * most + (slot * most + m) * most + k]


def merge_kernel(chips, turned, scalars_ref, *refs):
    scalars = Scalars(chips, scalars_ref)
    if turned:
        tots_ref, own_ref, near_ref, *outs = refs
    else:
        own_ref, near_ref, *outs = refs
    sums, tots = [], []
    for slot in range(2):
        if turned:
            own, other = tots_ref[1 - slot : 2 - slot], tots_ref[3 - slot : 4 - slot]
        else:
            own, other = (ref[slot, STATE : STATE + 1] for ref in (own_ref, near_ref))
            tots.append(own + other)
        first = scalars.first(slot)
        a = first * jnp.exp(other) + (1.0 - first)
        p = first + (1.0 - first) * jnp.exp(own)
        sums.append(a * own_ref[slot, :STATE] + p * near_ref[slot, :STATE])
    for n, out in enumerate(outs):
        up = scalars.up(n)
        out[:STATE] = (up * sums[0] + (1.0 - up) * sums[1]).astype(BF)
        if not turned:
            extra = jnp.concatenate(tots + [jnp.zeros((6, tots[0].shape[1]), F32)], axis=0)
            high, rest = split(extra)
            middle, low = split(extra - high.astype(F32))
            for k, part in enumerate((high, middle, low)):
                out[STATE + 16 * k : STATE + 16 * (k + 1)] = jnp.concatenate(
                    [part, jnp.zeros_like(part)], axis=0
                )


def merge(chips, scalars, own, near, tots=None):
    channels = own.shape[2]
    rows = STATE if tots is not None else STATE + 48
    given = [own, near] if tots is None else [tots, own, near]
    bits = bits_of(chips)
    return pl.pallas_call(
        functools.partial(merge_kernel, chips, tots is not None),
        in_specs=[SCALARS] + [pl.BlockSpec(memory_space=pltpu.VMEM)] * len(given),
        out_shape=[jax.ShapeDtypeStruct((rows, channels), BF) for _ in bits],
        compiler_params=PARAMS,
        name="merge",
    )(scalars, *given)


def exchange(chips, sums):
    return [send(sums[m.bit_length() - 1], "ctx", 2 * m) for m in range(1, chips)]


def gather_states(scalars, tot, near_ref, arrived, out):
    for slot in range(2):
        last = 1.0 - scalars.first(slot)
        total = last * near_ref[slot, :STATE]
        for m, ref in enumerate(arrived):
            weight = last * tot(1, slot)
            for k in range(len(arrived)):
                weight = weight + scalars.between(slot, m, k) * tot(2 + k, slot)
            weight = scalars.reach(slot, m) * jnp.exp(weight)
            total = total + weight * ref[:STATE].astype(F32)
        out(slot, total)


TILE = 128


def normed_kernel(count, heads, raw_ref, cg3_ref, gain_ref, cot_ref, scalars_ref, own_ref, near_ref, *refs):
    arrived, refs = refs[:count], refs[count:]
    mixed_ref, draw_ref, ry_ref, adj_ref, dc_ref, s_ref, tots_ref, s3 = refs
    at = pl.program_id(0)
    channels = raw_ref.shape[2]
    copier = spread(heads, channels, None, 3)

    @pl.when(at == 0)
    def _():
        rows = [own_ref[0, :1], own_ref[1, :1]]
        rows += [near_ref[0, STATE : STATE + 1], near_ref[1, STATE : STATE + 1]]
        for ref in arrived:
            parts = [ref[STATE + 16 * k : STATE + 16 * (k + 1)].astype(F32) for k in range(3)]
            both = parts[0] + parts[1] + parts[2]
            rows += [both[:1], both[1:2]]
        fill = tots_ref.shape[0] - len(rows)
        tots_ref[...] = jnp.concatenate(rows + [jnp.zeros((fill, channels), F32)], axis=0)

        def out(slot, total):
            s_ref[slot] = total
            high, low = split(total)
            s3[slot, :STATE] = high
            s3[slot, STATE : 2 * STATE] = high
            s3[slot, 2 * STATE :] = low

        scalars = Scalars(count + 1, scalars_ref)
        gather_states(scalars, lambda n, slot: rows[2 * n + slot], near_ref, arrived, out)
        adj_ref[...] = jnp.zeros_like(adj_ref)

    eye = mirror(GROUP)
    one = spread(heads, channels, None, 1)
    ys = []
    for branch in range(2):
        c3 = cg3_ref[branch, :, : 3 * STATE]
        grow = mm(cg3_ref[branch, :, 3 * STATE : 3 * STATE + 3 * heads], copier)
        r = raw_ref[branch] + grow * mm(c3, s3[branch])
        scale = lax.rsqrt(jnp.sum(r * r, axis=1, keepdims=True) * (1.0 / channels) + 1e-05)
        n = r * scale
        ys.append(n * gain_ref[...])
        cot = cot_ref[...] if branch == 0 else flip_lanes(cot_ref[...], eye)
        dz = cot.astype(F32) * gain_ref[...]
        mean = jnp.sum(dz * n, axis=1, keepdims=True) * (1.0 / channels)
        draw = scale * (dz - n * mean)
        draw_ref[branch] = draw.astype(BF)
        high, low = split(draw * r)
        ry_ref[branch] = mm(high, one, 1, 1) + mm(low, one, 1, 1)
        grown = (grow * draw).astype(BF)
        both = mm(c3[:, : 2 * STATE].T, grown)
        adj_ref[1 - branch] += both[:STATE] + both[STATE:]
        both = mm(grown, s3[branch, STATE:], 1, 1)
        dc_ref[branch] = both[:, :STATE] + both[:, STATE:]
    back = flip_lanes(ys[1].astype(BF), eye)
    mixed_ref[...] = (ys[0] + back.astype(F32)).astype(BF)


def normed(raw, cg3, gain, cot, scalars, ends, near, arrived):
    _, rows, channels = raw.shape
    heads = (cg3.shape[2] - 3 * STATE) // 6
    band = lambda n: pl.BlockSpec((2, TILE, n), lambda j: (0, j, 0))
    flat = pl.BlockSpec((TILE, channels), lambda j: (j, 0))
    gain = gain[None]
    state = pl.BlockSpec((2, STATE, channels), lambda j: (0, 0, 0))
    tots = -(-2 * (len(arrived) + 2) // 8) * 8
    return pl.pallas_call(
        functools.partial(normed_kernel, len(arrived), heads),
        grid=(rows // TILE,),
        in_specs=[band(channels), band(cg3.shape[2]), whole(gain), flat, SCALARS]
        + [pl.BlockSpec((2, 8, channels), lambda j: (0, STATE // 8, 0))]
        + [whole(a) for a in (near, *arrived)],
        out_specs=[flat, band(channels), band(heads), state, band(STATE), state]
        + [pl.BlockSpec((tots, channels), lambda j: (0, 0))],
        out_shape=[
            jax.ShapeDtypeStruct((rows, channels), BF),
            jax.ShapeDtypeStruct((2, rows, channels), BF),
            jax.ShapeDtypeStruct((2, rows, heads), F32),
            jax.ShapeDtypeStruct((2, STATE, channels), F32),
            jax.ShapeDtypeStruct((2, rows, STATE), F32),
            jax.ShapeDtypeStruct((2, STATE, channels), F32),
            jax.ShapeDtypeStruct((tots, channels), F32),
        ],
        scratch_shapes=[pltpu.VMEM((2, 3 * STATE, channels), BF)],
        compiler_params=PARAMS,
        name="normed",
    )(raw, cg3, gain, cot, scalars, ends, near, *arrived)


def inner_back_kernel(
    x_ref, draw_ref, nat_ref, lines_ref, after, u_ref, db_ref, dc_ref, score, ds_all, ds_own,
):
    at = pl.program_id(0)
    rows = x_ref.shape[1]
    heads = lines_ref.shape[1] // 2
    size = x_ref.shape[2] * pl.num_programs(0) // heads
    half = rows // 2
    per = GROUP // size

    @pl.when(at == 0)
    def _():
        for branch in range(2):
            b, c = nat_ref[branch, :, :STATE], nat_ref[branch, :, STATE : 2 * STATE]
            full = exact(b, c, 1, 1)
            score[branch] = jnp.where(ordered(rows, 1 - branch), full, 0.0)
        ds_all[...] = jnp.zeros_like(ds_all)
        ds_own[...] = jnp.zeros_like(ds_own)

    for branch in range(2):
        alone, first = (half, 0) if branch == 0 else (0, half)
        columns = pltpu.roll(nat_ref[branch, :, CUM:STEP], -(at * per) % LANES, 1)
        steps = pltpu.roll(nat_ref[branch, :, STEP:], -(at * per) % LANES, 1)
        draw = draw_ref[branch]
        tops, bottoms = 0.0, 0.0
        for k in range(per):
            line = lines_ref[branch, pl.ds(at * per + k, 1), :]
            dk = own_lanes(draw, k, size)
            xk = own_lanes(x_ref[branch], k, size)
            gap = line[:, alone : alone + half] - columns[alone : alone + half, k : k + 1]
            d = jnp.exp(jnp.minimum(gap, 0.0))
            m = d * score[branch, pl.ds(alone, half), pl.ds(alone, half)]
            bottoms = bottoms + mm(m.astype(BF), dk[alone : alone + half])
            xd = mm(xk[alone : alone + half], draw[alone : alone + half], 1, 1)
            ds_own[branch] += d * xd * steps[alone : alone + half, k : k + 1]
            gap = line - columns[first : first + half, k : k + 1]
            d = jnp.exp(jnp.minimum(gap, 0.0))
            m = d * score[branch, pl.ds(first, half), :]
            tops = tops + mm(m.astype(BF), dk)
            xd = mm(xk[first : first + half], draw, 1, 1)
            ds_all[branch] += d * xd * steps[first : first + half, k : k + 1]
        u_ref[branch, pl.ds(alone, half), :] = bottoms
        u_ref[branch, pl.ds(first, half), :] = tops

    @pl.when(at == pl.num_programs(0) - 1)
    def _():
        for branch in range(2):
            alone, first = (half, 0) if branch == 0 else (0, half)
            place, column = iota((half, rows), 0) + first, iota((half, rows), 1)
            seen = (place <= column) if branch == 0 else (place >= column)
            all_part = jnp.where(seen, ds_all[branch], 0.0)
            own_part = jnp.where(ordered(half, 1 - branch), ds_own[branch], 0.0)
            b, c = nat_ref[branch, :, :STATE], nat_ref[branch, :, STATE : 2 * STATE]
            db_ref[branch, pl.ds(first, half), :] = exact(all_part, c)
            db_ref[branch, pl.ds(alone, half), :] = exact(own_part, c[alone : alone + half])
            dc = exact(all_part.T, b[first : first + half])
            dc_own = dc[alone : alone + half] + exact(own_part.T, b[alone : alone + half])
            dc_ref[branch, pl.ds(first, half), :] = dc[first : first + half]
            dc_ref[branch, pl.ds(alone, half), :] = dc_own


def inner_back(x, draw, nat, lines, after):
    _, rows, channels = x.shape
    block = pl.BlockSpec((2, rows, GROUP), lambda j: (0, 0, j))
    return pl.pallas_call(
        inner_back_kernel,
        grid=(channels // GROUP,),
        in_specs=[block, block, whole(nat), whole(lines), ORDER],
        out_specs=[block] + [pl.BlockSpec((2, rows, STATE), lambda j: (0, 0, 0))] * 2,
        out_shape=[
            jax.ShapeDtypeStruct(x.shape, F32),
            jax.ShapeDtypeStruct((2, rows, STATE), F32),
            jax.ShapeDtypeStruct((2, rows, STATE), F32),
        ],
        scratch_shapes=[
            pltpu.VMEM((2, rows, rows), F32),
            pltpu.VMEM((2, rows // 2, rows), F32),
            pltpu.VMEM((2, rows // 2, rows // 2), F32),
        ],
        compiler_params=PARAMS,
        name="inner_back",
    )(x, draw, nat, lines, after)


def finish_kernel(first, count, last, heads, channels, *refs):
    x_ref, u_ref, bf3_ref, s_ref, end_ref, tots_ref, scalars_ref, near_ref, *refs = refs
    arrived, refs = refs[:count], refs[count:]
    if last:
        nat_ref, db_ref, dc_ref, dc0_ref, ry_ref, rate_ref, *refs = refs
        before, refs = refs[: len(refs) - 4], refs[len(refs) - 4 :]
    out_ref, dbs_ref, direct_ref, dtot_ref = refs
    at = pl.program_id(0)
    start = (first + at) * (GROUP * heads // channels)
    one = spread(heads, channels, start, 1)
    copier = spread(heads, channels, start, 3)
    columns = pl.ds(pl.multiple_of(at * GROUP, GROUP), GROUP)

    def per_head(a):
        high, low = split(a)
        return mm(high, one, 1, 1) + mm(low, one, 1, 1)

    @pl.when(at == 0)
    def _():
        dbs_ref[...] = jnp.zeros_like(dbs_ref)
        direct_ref[...] = jnp.zeros_like(direct_ref)
        dtot_ref[...] = jnp.zeros_like(dtot_ref)

    def tot(n, slot):
        at = 2 * n + 1 - slot
        return tots_ref[at : at + 1]

    def out(slot, g):
        branch = 1 - slot
        g_high, g_low = split(g)
        us = mm(bf3_ref[branch, :, : 3 * STATE], jnp.concatenate([g_high, g_high, g_low], axis=0))
        fade = mm(bf3_ref[branch, :, 3 * STATE : 3 * STATE + 3 * heads], copier)
        step = mm(bf3_ref[branch, :, 3 * STATE + 3 * heads :], copier)
        both = u_ref[branch] + fade * us
        xf = x_ref[branch].astype(F32)
        dx = (step * both).astype(BF)
        if last:
            out_ref[branch, :, columns] = dx
        else:
            out_ref[branch] = dx
        direct_ref[branch] += per_head(xf * both)
        weighted = (fade * step * xf).astype(BF)
        sums = mm(weighted, jnp.concatenate([g_high, g_low], axis=0), 1, 1)
        dbs_ref[branch] += sums[:, :STATE] + sums[:, STATE:]
        ended = jnp.exp(tot(0, slot)) * s_ref[branch] + end_ref[branch]
        kept = jnp.sum(g * ended, axis=0, keepdims=True)
        kept = jnp.concatenate([kept, jnp.zeros((7, GROUP), F32)], axis=0)
        dtot_ref[branch] += per_head(kept)[:1]

    gather_states(Scalars(count + 1, scalars_ref), tot, near_ref, arrived, out)

    if last:

        @pl.when(at == pl.num_programs(0) - 1)
        def _():
            rows, width = direct_ref.shape[1], out_ref.shape[2] - 2 * STATE - heads
            for branch in range(2):
                dbs, direct, dtot = dbs_ref[branch], direct_ref[branch], dtot_ref[branch]
                for n in range(0, len(before), 3):
                    dbs = dbs + before[n][branch]
                    direct = direct + before[n + 1][branch]
                    dtot = dtot + before[n + 2][branch]
                step = nat_ref[branch, :, STEP : STEP + heads]
                pre = nat_ref[branch, :, STEP + heads : STEP + 2 * heads]
                dcum = ry_ref[branch] - step * direct
                dla = exact(ordered(rows, 1 - branch).astype(F32), dcum) + dtot
                dpre = (direct - jnp.exp(rate_ref[...]) * dla) * jax.nn.sigmoid(pre)
                small = [db_ref[branch] + dbs, dc_ref[branch] + dc0_ref[branch], dpre]
                out_ref[branch, :, width:] = jnp.concatenate(small, axis=1).astype(BF)


def finish(piece, pieces, x, u, bf3, s_in, ends, tots, scalars, near, arrived, more, before):
    _, rows, channels = x.shape
    heads = (bf3.shape[2] - 3 * STATE) // 6
    last = piece == pieces - 1
    groups = channels // GROUP // pieces
    first = piece * groups
    block = pl.BlockSpec((2, rows, GROUP), lambda j: (0, 0, first + j))
    state = pl.BlockSpec((2, STATE, GROUP), lambda j: (0, 0, first + j))
    flat = lambda n: pl.BlockSpec((n, GROUP), lambda j: (0, first + j))
    extra = [*more, *before] if last else []
    width = groups * GROUP + (2 * STATE + heads if last else 0)
    sums = [(2, rows, STATE), (2, rows, heads), (2, 1, heads)]
    return pl.pallas_call(
        functools.partial(finish_kernel, first, len(arrived), last, heads, channels),
        grid=(groups,),
        in_specs=[block, block, whole(bf3), state, state, flat(tots.shape[0]), SCALARS, state]
        + [flat(STATE)] * len(arrived)
        + [whole(a) for a in extra],
        out_specs=[
            pl.BlockSpec((2, rows, width), lambda j: (0, 0, 0))
            if last
            else pl.BlockSpec((2, rows, GROUP), lambda j: (0, 0, j))
        ]
        + [pl.BlockSpec(shape, lambda j: (0, 0, 0)) for shape in sums],
        out_shape=[jax.ShapeDtypeStruct((2, rows, width), BF)]
        + [jax.ShapeDtypeStruct(shape, F32) for shape in sums],
        compiler_params=PARAMS,
        name="finish",
    )(x, u, bf3, s_in, ends, tots, scalars, near, *arrived, *extra)


def turned_kernel(
    chips, where_ref, own_ref, own_mirror_ref, peer_ref, peer_mirror_ref, after, out_ref, held
):
    parts = where_ref.shape[0] - chips
    wide, rows = held.shape[1], held.shape[2]
    thin = wide // parts
    eye = (iota((wide, wide), 0) == iota((wide, wide), 1)).astype(BF)
    back = mirror(wide)
    sources = [(own_ref, eye), (own_mirror_ref, back), (peer_ref, eye), (peer_mirror_ref, back)]
    for n, (ref, turn) in enumerate(sources):
        held[n] = mm(turn, ref[...], 1, 1).astype(BF)
    for n in range(4):
        for k in range(parts):
            start = pl.multiple_of(where_ref[chips + k] * thin, thin)
            out_ref[k * thin : (k + 1) * thin, n * rows : (n + 1) * rows] = held[
                n, pl.ds(start, thin), :
            ]


def turned(h, peer, where, chips, after):
    rows, channels = h.shape
    wide = channels // (2 * chips)
    plain = pl.BlockSpec((rows, wide), lambda m, where: (0, where[m]))
    other = pl.BlockSpec((rows, wide), lambda m, where: (0, 2 * chips - 1 - where[m]))
    return pl.pallas_call(
        functools.partial(turned_kernel, chips),
        grid_spec=pltpu.PrefetchScalarGridSpec(
            num_scalar_prefetch=1,
            grid=(chips,),
            in_specs=[plain, other, plain, other, ORDER],
            out_specs=pl.BlockSpec((wide, 4 * rows), lambda m, where: (m, 0)),
            scratch_shapes=[pltpu.VMEM((4, wide, rows), BF)],
        ),
        out_shape=jax.ShapeDtypeStruct((chips * wide, 4 * rows), BF),
        compiler_params=PARAMS,
        name="turned",
    )(where, h, h, peer, peer, after)


def by_bits(size, bits):
    return sorted(range(size), key=lambda k: [k & bit for bit in bits])


def bits_of(size):
    return [1 << k for k in range(size.bit_length() - 1)]


def term_kernel(orders, cuts, left_ref, own_ref, peer_ref, *outs):
    depth = own_ref.shape[0]
    wide = left_ref.shape[0] // len(orders[0])
    for part, (order, (low, high)) in enumerate(zip(orders, cuts)):
        stay_ref, go_ref = outs[2 * part : 2 * part + 2]
        half = len(order) // 2
        for n, block in enumerate(order):
            left = left_ref[block * wide : (block + 1) * wide]
            term = mm(left[:, :depth], own_ref[:, low:high])
            term = term + mm(left[:, depth:], peer_ref[:, low:high])
            if n < half:
                stay_ref[n * wide : (n + 1) * wide] = term
            else:
                go_ref[(n - half) * wide : (n - half + 1) * wide] = term.astype(BF)


def weight_terms(left, own, peer, orders, cuts):
    rows = left.shape[0] // 2
    shape = lambda cut, kind: jax.ShapeDtypeStruct((rows, cut[1] - cut[0]), kind)
    outs = pl.pallas_call(
        functools.partial(term_kernel, orders, cuts),
        out_shape=[shape(cut, kind) for cut in cuts for kind in (F32, BF)],
        compiler_params=PARAMS,
        name="terms",
    )(left, own, peer)
    return [outs[n : n + 2] for n in range(0, len(outs), 2)]


def fold_kernel(count, final, *refs):
    given, outs = refs[: 2 * count], refs[2 * count :]
    joined = len(outs) < 2 * count
    column = 0
    for n in range(count):
        stay_ref, got_ref = given[2 * n : 2 * n + 2]
        rows, width = stay_ref.shape
        total = stay_ref[...] + got_ref[...].astype(F32)
        columns = slice(column, column + width)
        if final:
            outs[0][:, columns] = total.astype(BF)
        else:
            keep, go = outs[:2] if joined else outs[2 * n : 2 * n + 2]
            keep[:, columns] = total[: rows // 2]
            go[:, columns] = total[rows // 2 :].astype(BF)
        column = column + width if joined else 0


def fold(parts, join=False, final=False):
    rows = parts[0][0].shape[0] if final else parts[0][0].shape[0] // 2
    widths = [stay.shape[1] for stay, _ in parts]
    widths = [sum(widths)] if join else widths
    kinds = [BF] if final else [F32, BF]
    outs = pl.pallas_call(
        functools.partial(fold_kernel, len(parts), final),
        out_shape=[jax.ShapeDtypeStruct((rows, w), kind) for w in widths for kind in kinds],
        compiler_params=PARAMS,
        name="fold",
    )(*[a for part in parts for a in part])
    return outs[0] if final else [outs[n : n + 2] for n in range(0, len(outs), 2)]


def summed(parts, orders):
    dps = lax.axis_size("dp")
    dp_bits = bits_of(dps)
    for n in range(len(orders[0])):
        sent = [send(go, "ctx", 2 * bits[n]) for (_, go), bits in zip(parts, orders)]
        got = [(stay, came) for (stay, _), came in zip(parts, sent)]
        parts = fold(got, join=n == len(orders[0]) - 1)
    for n, bit in enumerate(dp_bits):
        stay, go = parts[0]
        last = n == len(dp_bits) - 1
        parts = fold([(stay, send(go, "dp", bit))], join=True, final=last)
    held, came = parts, None
    for bit in dp_bits[::-1]:
        if came is not None:
            held = jnp.concatenate([held, came])
        came = send(held, "dp", bit)
    return held, came


def place_kernel(chips, where_ref, *refs):
    given, (grad_x_ref, grad_small_ref) = refs[:-2], refs[-2:]
    dps = where_ref.shape[0] - chips
    thin = grad_x_ref.shape[0] // dps
    columns = grad_x_ref.shape[1]
    for k in range(dps):
        target = pl.ds(pl.multiple_of(where_ref[chips + k] * thin, thin), thin)
        column = 0
        for n in range(0, len(given), 2):
            ref, at = (given[n], k) if k < dps // 2 else (given[n + 1], k - dps // 2)
            piece = ref[at * thin : (at + 1) * thin].astype(F32)
            width = min(piece.shape[1], columns - column)
            grad_x_ref[target, column : column + width] = piece[:, :width]
            column += width
            if piece.shape[1] > width:
                grad_small_ref[target, :] = piece[:, width:]


def placed(chips, where, given, wide, channels, small):
    vmem = pl.BlockSpec(memory_space=pltpu.VMEM)
    return pl.pallas_call(
        functools.partial(place_kernel, chips),
        in_specs=[SCALARS] + [vmem] * len(given),
        out_shape=[
            jax.ShapeDtypeStruct((wide, channels), F32),
            jax.ShapeDtypeStruct((wide, small), F32),
        ],
        compiler_params=PARAMS,
        name="placed",
    )(where, *given)


PIECES = 2


def shards(hidden, x_weight, state_weight, log_rates, step_bias, out_gain, cotangent):
    h, cot = hidden[0], cotangent[0]
    rows, channels = h.shape
    chips = lax.axis_size("ctx") // 2
    place = lax.axis_index("ctx")
    dps, dp_place = lax.axis_size("dp"), lax.axis_index("dp")
    scalars = Scalars(chips).made()
    where = (place ^ (2 * jnp.arange(chips)), dp_place ^ jnp.array(by_bits(dps, bits_of(dps))))
    where = jnp.concatenate(where).astype(jnp.int32)
    peer_h = send(h, "ctx", 1)
    both, nat, lines, cg3, bf3, bt, weight3, tot3 = project_small(
        h, state_weight, log_rates, step_bias
    )
    x, ends = project(both, x_weight, bt, weight3, tot3)
    near = send(ends, "ctx", 1)
    left = turned(h, peer_h, where, chips, ends)
    sums = merge(chips, scalars, ends, near)
    arrived = exchange(chips, sums)
    raw = inner(x, nat, lines, sums[0], left)
    mixed, draw, ry, adj, dc0, s_in, tots = normed(
        raw, cg3, out_gain, cot, scalars, ends, near, arrived
    )
    near = send(adj, "ctx", 1)
    sums = merge(chips, scalars, adj, near, tots)
    arrived = exchange(chips, sums)
    u, db, dc = inner_back(x, draw, nat, lines, sums[0])
    bits = bits_of(chips)
    orders = [bits[n:] + bits[:n] for n in range(2)]
    blocks = [by_bits(chips, order) for order in orders]
    done, before = [], []
    more = [nat, db, dc, dc0, ry, log_rates[None]]
    for n in range(PIECES):
        own, *partial = finish(
            n, PIECES, x, u, bf3, s_in, ends, tots, scalars, near, arrived, more, before
        )
        before = before + partial
        own = own.reshape(2 * rows, -1)
        peer = send(own, "ctx", 1)
        middle = channels // PIECES // 2
        cuts = [(0, middle), (middle, own.shape[1])]
        done += summed(weight_terms(left, own, peer, blocks, cuts), orders)
    wide = channels // (2 * chips)
    grad_x, grad_small = placed(chips, where, done, wide, channels, state_weight.shape[1])
    return (mixed[None], grad_x, grad_small)


def solution(mesh):
    return jax.shard_map(
        shards,
        mesh=mesh,
        in_specs=(P("dp", "ctx", None), P(), P(), P(), P(), P(), P("dp", "ctx", None)),
        out_specs=(P("dp", "ctx", None), P("ctx", None), P("ctx", None)),
        check_vma=False,
    )
```

```python
import functools

import jax
import jax.numpy as jnp
from jax import lax
from jax.experimental import pallas as pl
from jax.experimental.pallas import tpu as pltpu
from jax.sharding import PartitionSpec as P

STATE = 64
GROUP = 256
LANES = 128
BF = jnp.bfloat16
F32 = jnp.float32
precise = lax.Precision.HIGHEST
ORDER = pl.BlockSpec(memory_space=pl.ANY)
SCALARS = pl.BlockSpec(memory_space=pltpu.SMEM)
PARAMS = pltpu.CompilerParams(vmem_limit_bytes=48 * 2**20)


def send(array, axis, mask):
    return lax.ppermute(array, axis, [(i, i ^ mask) for i in range(lax.axis_size(axis))])


def mm(a, b, ca=1, cb=0):
    return lax.dot_general(a, b, (((ca,), (cb,)), ((), ())), preferred_element_type=F32)


def exact(a, b, ca=1, cb=0):
    dims = (((ca,), (cb,)), ((), ()))
    return lax.dot_general(a, b, dims, precision=precise, preferred_element_type=F32)


def split(a):
    high = a.astype(BF)
    return high, (a - high.astype(F32)).astype(BF)


def split_three(a, axis):
    high, rest = split(a)
    middle, low = split(a - high.astype(F32))
    return jnp.concatenate([high, middle, low], axis=axis)


def iota(shape, axis):
    return lax.broadcasted_iota(jnp.int32, shape, axis)


def ordered(rows, branch, strict_after=False):
    t, s = iota((rows, rows), 0), iota((rows, rows), 1)
    return (t >= s) if (branch == 0) != strict_after else (t <= s)


def mirror(width):
    return (iota((width, width), 0) + iota((width, width), 1) == width - 1).astype(BF)


def spread(heads, channels, start, copies):
    head = iota((heads, GROUP if start is not None else channels), 0)
    lane = iota((heads, GROUP if start is not None else channels), 1)
    size = channels // heads
    first = 0 if start is None else start
    one = (head == lane // size + first).astype(BF)
    return jnp.concatenate([one] * copies, axis=0)


def flip_lanes(a, eye):
    parts = [mm(a[:, k : k + GROUP], eye).astype(BF) for k in range(0, a.shape[1], GROUP)]
    return jnp.concatenate(parts[::-1], axis=1)


def softplus(a):
    return jnp.maximum(a, 0.0) + jnp.log1p(jnp.exp(-jnp.abs(a)))


def whole(a):
    return pl.BlockSpec(a.shape, lambda *_: (0,) * a.ndim)


def padded(a):
    return jnp.concatenate([a, jnp.zeros((a.shape[0], LANES - a.shape[1]), a.dtype)], axis=1)


CUM, STEP = LANES, 2 * LANES


def small_kernel(
    h_ref, ws_ref, rate_ref, bias_ref,
    both_ref, nat_ref, lines_ref, cg3_ref, bf3_ref, bt_ref, weight3_ref, tot3_ref,
):
    rows, channels = h_ref.shape
    heads = rate_ref.shape[1]
    eye = mirror(GROUP)
    both_ref[:rows] = h_ref[...]
    for k in range(0, channels, GROUP):
        both_ref[rows:, channels - k - GROUP : channels - k] = mm(
            h_ref[:, k : k + GROUP], eye
        ).astype(BF)
    projected = mm(both_ref[...], ws_ref[...])
    for branch in range(2):
        p = projected[branch * rows : (branch + 1) * rows]
        b, c = p[:, :STATE], p[:, STATE : 2 * STATE]
        pre = p[:, 2 * STATE :] + bias_ref[...]
        step = softplus(pre)
        la = -jnp.exp(rate_ref[...]) * step
        cum = exact(ordered(rows, branch).astype(F32), la)
        tot = cum[rows - 1 :] if branch == 0 else cum[:1]
        fade = jnp.exp(tot - cum)
        wide_step, wide_cum = padded(step), padded(cum)
        nat_ref[branch, :, :CUM] = p[:, : 2 * STATE]
        nat_ref[branch, :, CUM:STEP] = wide_cum
        nat_ref[branch, :, STEP:] = padded(jnp.concatenate([step, pre], axis=1))
        lines_ref[branch, :heads] = wide_cum.T[:heads]
        lines_ref[branch, heads:] = wide_step.T[:heads]
        b_high, b_low = split(b)
        c_high, c_low = split(c)
        grow3 = split_three(jnp.exp(cum), 1)
        cg3_ref[branch] = jnp.concatenate(
            [c_high, c_low, c_high, grow3, jnp.zeros_like(grow3)], axis=1
        )
        bf3_ref[branch] = jnp.concatenate(
            [b_high, b_low, b_high, split_three(fade, 1), split_three(step, 1)], axis=1
        )
        bt_ref[branch] = jnp.concatenate([b_high, b_low], axis=1).T
        weight3_ref[branch] = split_three(fade * step, 1)
        tot3_ref[branch] = split_three(jnp.broadcast_to(tot, (8, heads)), 1)


def project_small(h, ws, log_rates, step_bias):
    rows, channels = h.shape
    heads = log_rates.shape[0]
    f32 = lambda *shape: jax.ShapeDtypeStruct(shape, F32)
    bf16 = lambda *shape: jax.ShapeDtypeStruct(shape, BF)
    return pl.pallas_call(
        small_kernel,
        out_shape=[
            bf16(2 * rows, channels),
            f32(2, rows, 3 * LANES),
            f32(2, 2 * heads, rows),
            bf16(2, rows, 3 * STATE + 6 * heads),
            bf16(2, rows, 3 * STATE + 6 * heads),
            bf16(2, 2 * STATE, rows),
            bf16(2, rows, 3 * heads),
            bf16(2, 8, 3 * heads),
        ],
        compiler_params=PARAMS,
        name="small",
    )(h, ws, log_rates[None], step_bias[None])


def project_kernel(both_ref, w_ref, bt_ref, weight3_ref, tot3_ref, x_ref, end_ref):
    at = pl.program_id(0)
    rows = x_ref.shape[1]
    heads = weight3_ref.shape[2] // 3
    channels = both_ref.shape[1]
    copier = spread(heads, channels, at * (GROUP * heads // channels), 3)
    values = mm(both_ref[...], w_ref[...]).astype(BF)
    for branch in range(2):
        x = values[branch * rows : (branch + 1) * rows]
        x_ref[branch] = x
        weighted = mm(weight3_ref[branch], copier) * x.astype(F32)
        both = mm(bt_ref[branch], weighted.astype(BF))
        end_ref[branch, :STATE] = both[:STATE] + both[STATE:]
        end_ref[branch, STATE:] = mm(tot3_ref[branch], copier)


def project(both, w, bt, weight3, tot3):
    rows, channels = both.shape[0] // 2, both.shape[1]
    return pl.pallas_call(
        project_kernel,
        grid=(channels // GROUP,),
        in_specs=[
            whole(both),
            pl.BlockSpec((channels, GROUP), lambda j: (0, j)),
            whole(bt),
            whole(weight3),
            whole(tot3),
        ],
        out_specs=[
            pl.BlockSpec((2, rows, GROUP), lambda j: (0, 0, j)),
            pl.BlockSpec((2, STATE + 8, GROUP), lambda j: (0, 0, j)),
        ],
        out_shape=[
            jax.ShapeDtypeStruct((2, rows, channels), BF),
            jax.ShapeDtypeStruct((2, STATE + 8, channels), F32),
        ],
        compiler_params=PARAMS,
        name="project",
    )(both, w, bt, weight3, tot3)


def own_lanes(a, k, size):
    lane = iota(a.shape, 1) // size
    return jnp.where(lane == k, a.astype(F32), 0.0).astype(BF)


def inner_kernel(branch, x_ref, nat_ref, lines_ref, after, raw_ref, score):
    at = pl.program_id(0)
    rows = x_ref.shape[1]
    heads = lines_ref.shape[1] // 2
    size = x_ref.shape[2] * pl.num_programs(0) // heads
    half = rows // 2
    per = GROUP // size

    @pl.when(at == 0)
    def _():
        b, c = nat_ref[0, :, :STATE], nat_ref[0, :, STATE : 2 * STATE]
        score[...] = jnp.where(ordered(rows, branch), exact(c, b, 1, 1), 0.0)

    alone, later = (0, half) if branch == 0 else (half, 0)
    columns = pltpu.roll(nat_ref[0, :, CUM:STEP], -(at * per) % LANES, 1)
    tops, bottoms = 0.0, 0.0
    for k in range(per):
        line = lines_ref[0, pl.ds(at * per + k, 1), :]
        step = lines_ref[0, pl.ds(heads + at * per + k, 1), :]
        xk = own_lanes(x_ref[0], k, size)
        own = pl.ds(alone, half)
        gap = columns[alone : alone + half, k : k + 1] - line[:, alone : alone + half]
        m = jnp.exp(jnp.minimum(gap, 0.0)) * score[own, own] * step[:, alone : alone + half]
        tops = tops + mm(m.astype(BF), xk[alone : alone + half])
        gap = columns[later : later + half, k : k + 1] - line
        m = jnp.exp(jnp.minimum(gap, 0.0)) * score[pl.ds(later, half), :] * step
        bottoms = bottoms + mm(m.astype(BF), xk)
    raw_ref[pl.ds(alone, half), :] = tops
    raw_ref[pl.ds(later, half), :] = bottoms


def inner(branch, x, nat, lines, after):
    _, rows, channels = x.shape
    one = lambda a: pl.BlockSpec((1, *a.shape[1:]), lambda j: (branch, 0, 0))
    return pl.pallas_call(
        functools.partial(inner_kernel, branch),
        grid=(channels // GROUP,),
        in_specs=[
            pl.BlockSpec((1, rows, GROUP), lambda j: (branch, 0, j)),
            one(nat),
            one(lines),
            ORDER,
        ],
        out_specs=pl.BlockSpec((rows, GROUP), lambda j: (0, j)),
        out_shape=jax.ShapeDtypeStruct((rows, channels), F32),
        scratch_shapes=[pltpu.VMEM((rows, rows), F32)],
        compiler_params=PARAMS,
        name="inner",
    )(x, nat, lines, after)


class Scalars:
    def __init__(self, chips, ref=None):
        self.chips, self.ref = chips, ref
        self.bits = bits_of(chips)

    def made(self):
        place = lax.axis_index("ctx")
        chip, core = place // 2, place % 2
        at = chip ^ jnp.arange(1, self.chips)
        up = (chip ^ jnp.array(self.bits)) > chip
        reach = jnp.concatenate([at < chip, at > chip])
        left = (at[None] > at[:, None]) & (at[None] < chip)
        right = (at[None] > chip) & (at[None] < at[:, None])
        parts = [jnp.stack([core == 0, core == 1]), up, reach, left.ravel(), right.ravel()]
        return jnp.concatenate(parts).astype(F32)

    def first(self, slot):
        return self.ref[slot]

    def up(self, n):
        return self.ref[2 + n]

    def reach(self, slot, m):
        return self.ref[2 + len(self.bits) + slot * (self.chips - 1) + m]

    def between(self, slot, m, k):
        most = self.chips - 1
        return self.ref[2 + len(self.bits) + 2 * most + (slot * most + m) * most + k]


def merge_kernel(chips, turned, scalars_ref, after, *refs):
    scalars = Scalars(chips, scalars_ref)
    if turned:
        tots_ref, own_ref, near_ref, *outs = refs
    else:
        own_ref, near_ref, *outs = refs
    sums, tots = [], []
    for slot in range(2):
        if turned:
            own, other = tots_ref[1 - slot : 2 - slot], tots_ref[3 - slot : 4 - slot]
        else:
            own, other = (ref[slot, STATE : STATE + 1] for ref in (own_ref, near_ref))
            tots.append(own + other)
        first = scalars.first(slot)
        a = first * jnp.exp(other) + (1.0 - first)
        p = first + (1.0 - first) * jnp.exp(own)
        sums.append(a * own_ref[slot, :STATE] + p * near_ref[slot, :STATE])
    for n, out in enumerate(outs):
        up = scalars.up(n)
        out[:STATE] = (up * sums[0] + (1.0 - up) * sums[1]).astype(BF)
        if not turned:
            rows = []
            for tot in tots:
                high, rest = split(tot)
                middle, low = split(tot - high.astype(F32))
                rows += [part.astype(F32) for part in (high, middle, low)]
            rows.append(jnp.zeros((16 - len(rows), rows[0].shape[1]), F32))
            out[STATE:] = jnp.concatenate(rows, axis=0).astype(BF)


def merge(chips, scalars, after, own, near, tots=None):
    channels = own.shape[2]
    rows = STATE if tots is not None else STATE + 16
    given = [own, near] if tots is None else [tots, own, near]
    bits = bits_of(chips)
    return pl.pallas_call(
        functools.partial(merge_kernel, chips, tots is not None),
        in_specs=[SCALARS, ORDER] + [pl.BlockSpec(memory_space=pltpu.VMEM)] * len(given),
        out_shape=[jax.ShapeDtypeStruct((rows, channels), BF) for _ in bits],
        compiler_params=PARAMS,
        name="merge",
    )(scalars, after, *given)


def exchange(chips, sums):
    return [send(sums[m.bit_length() - 1], "ctx", 2 * m) for m in range(1, chips)]


def gather_states(scalars, tot, near_ref, arrived, out):
    for slot in range(2):
        last = 1.0 - scalars.first(slot)
        total = last * near_ref[slot, :STATE]
        for m, ref in enumerate(arrived):
            weight = last * tot(1, slot)
            for k in range(len(arrived)):
                weight = weight + scalars.between(slot, m, k) * tot(2 + k, slot)
            weight = scalars.reach(slot, m) * jnp.exp(weight)
            total = total + weight * ref[:STATE].astype(F32)
        out(slot, total)


TILE = 128


def normed_kernel(
    count, heads, raw_fwd_ref, raw_rc_ref, cg3_ref, gain_ref, cot_ref, scalars_ref,
    x_fwd_ref, x_rc_ref, nat_fwd_ref, nat_rc_ref, own_ref, near_ref, *refs,
):
    arrived, refs = refs[:count], refs[count:]
    mixed_ref, draw_ref, ry_ref, adj_ref, dc_ref, s_ref, tots_ref, start_ref, s3 = refs
    at = pl.program_id(0)
    channels = raw_fwd_ref.shape[1]
    copier = spread(heads, channels, None, 3)

    @pl.when(at == 0)
    def _():
        rows = [own_ref[0, :1], own_ref[1, :1]]
        rows += [near_ref[0, STATE : STATE + 1], near_ref[1, STATE : STATE + 1]]
        for ref in arrived:
            parts = ref[STATE:].astype(F32)
            rows += [parts[n : n + 1] + parts[n + 1 : n + 2] + parts[n + 2 : n + 3] for n in (0, 3)]
        fill = tots_ref.shape[0] - len(rows)
        tots_ref[...] = jnp.concatenate(rows + [jnp.zeros((fill, channels), F32)], axis=0)

        def out(slot, total):
            s_ref[slot] = total
            high, low = split(total)
            s3[slot, :STATE] = high
            s3[slot, STATE : 2 * STATE] = high
            s3[slot, 2 * STATE :] = low

        scalars = Scalars(count + 1, scalars_ref)
        gather_states(scalars, lambda n, slot: rows[2 * n + slot], near_ref, arrived, out)
        adj_ref[...] = jnp.zeros_like(adj_ref)

    eye = mirror(GROUP)
    one = spread(heads, channels, None, 1)
    ys = []
    for branch in range(2):
        c3 = cg3_ref[branch, :, : 3 * STATE]
        grow = mm(cg3_ref[branch, :, 3 * STATE : 3 * STATE + 3 * heads], copier)
        raw_ref = raw_fwd_ref if branch == 0 else raw_rc_ref
        r = raw_ref[...] + grow * mm(c3, s3[branch])
        scale = lax.rsqrt(jnp.sum(r * r, axis=1, keepdims=True) * (1.0 / channels) + 1e-05)
        n = r * scale
        ys.append(n * gain_ref[...])
        cot = cot_ref[...] if branch == 0 else flip_lanes(cot_ref[...], eye)
        dz = cot.astype(F32) * gain_ref[...]
        mean = jnp.sum(dz * n, axis=1, keepdims=True) * (1.0 / channels)
        draw = scale * (dz - n * mean)
        draw_ref[branch] = draw.astype(BF)

        x_ref, nat_ref = ((x_fwd_ref, nat_fwd_ref), (x_rc_ref, nat_rc_ref))[branch]
        row, edge = (0, 0) if branch == 0 else (TILE - 1, x_ref.shape[1] - 1)

        @pl.when(at == (0 if branch == 0 else pl.num_programs(0) - 1))
        def _(branch=branch, x_ref=x_ref, nat_ref=nat_ref, row=row, edge=edge, scale=scale, dz=dz):
            step = mm(split_three(nat_ref[0, :, STEP : STEP + heads], 1), copier)
            step = step[0:1] if branch == 0 else step[7:8]
            x = x_ref[0].astype(F32)[edge : edge + 1]
            total = jnp.sum(step * x * dz[row : row + 1], axis=1, keepdims=True)
            value = 1e-05 * scale[row : row + 1] ** 3 * total
            start_ref[branch] = jnp.broadcast_to(value, start_ref.shape[1:])

        high, low = split(draw * r)
        ry_ref[branch] = mm(high, one, 1, 1) + mm(low, one, 1, 1)
        grown = (grow * draw).astype(BF)
        both = mm(c3[:, : 2 * STATE].T, grown)
        adj_ref[1 - branch] += both[:STATE] + both[STATE:]
        both = mm(grown, s3[branch, STATE:], 1, 1)
        dc_ref[branch] = both[:, :STATE] + both[:, STATE:]
    back = flip_lanes(ys[1].astype(BF), eye)
    mixed_ref[...] = (ys[0] + back.astype(F32)).astype(BF)


def normed(raws, x, nat, cg3, gain, cot, scalars, ends, near, arrived):
    rows, channels = raws[0].shape
    heads = (cg3.shape[2] - 3 * STATE) // 6
    band = lambda n: pl.BlockSpec((2, TILE, n), lambda j: (0, j, 0))
    flat = pl.BlockSpec((TILE, channels), lambda j: (j, 0))
    gain = gain[None]
    state = pl.BlockSpec((2, STATE, channels), lambda j: (0, 0, 0))
    tots = -(-2 * (len(arrived) + 2) // 8) * 8
    return pl.pallas_call(
        functools.partial(normed_kernel, len(arrived), heads),
        grid=(rows // TILE,),
        in_specs=[flat, flat, band(cg3.shape[2]), whole(gain), flat, SCALARS]
        + [
            pl.BlockSpec((1, 16, channels), lambda j: (0, 0, 0)),
            pl.BlockSpec((1, 16, channels), lambda j: (1, rows // 16 - 1, 0)),
            pl.BlockSpec((1, 8, nat.shape[2]), lambda j: (0, 0, 0)),
            pl.BlockSpec((1, 8, nat.shape[2]), lambda j: (1, rows // 8 - 1, 0)),
            pl.BlockSpec((2, 8, channels), lambda j: (0, STATE // 8, 0)),
        ]
        + [whole(a) for a in (near, *arrived)],
        out_specs=[flat, band(channels), band(heads), state, band(STATE), state]
        + [
            pl.BlockSpec((tots, channels), lambda j: (0, 0)),
            pl.BlockSpec((2, 8, LANES), lambda j: (0, 0, 0)),
        ],
        out_shape=[
            jax.ShapeDtypeStruct((rows, channels), BF),
            jax.ShapeDtypeStruct((2, rows, channels), BF),
            jax.ShapeDtypeStruct((2, rows, heads), F32),
            jax.ShapeDtypeStruct((2, STATE, channels), F32),
            jax.ShapeDtypeStruct((2, rows, STATE), F32),
            jax.ShapeDtypeStruct((2, STATE, channels), F32),
            jax.ShapeDtypeStruct((tots, channels), F32),
            jax.ShapeDtypeStruct((2, 8, LANES), F32),
        ],
        scratch_shapes=[pltpu.VMEM((2, 3 * STATE, channels), BF)],
        compiler_params=PARAMS,
        name="normed",
    )(*raws, cg3, gain, cot, scalars, x, x, nat, nat, ends, near, *arrived)


def inner_back_kernel(
    x_ref, draw_ref, nat_ref, lines_ref, start_ref, edges_ref, after, u_ref, db_ref, dc_ref, score, ds_all, ds_own,
):
    at = pl.program_id(0)
    rows = x_ref.shape[1]
    heads = lines_ref.shape[1] // 2
    size = x_ref.shape[2] * pl.num_programs(0) // heads
    half = rows // 2
    per = GROUP // size

    @pl.when(at == 0)
    def _():
        for branch in range(2):
            b, c = nat_ref[branch, :, :STATE], nat_ref[branch, :, STATE : 2 * STATE]
            full = exact(b, c, 1, 1)
            score[branch] = jnp.where(ordered(rows, 1 - branch), full, 0.0)
        ds_all[...] = jnp.zeros_like(ds_all)
        ds_own[...] = jnp.zeros_like(ds_own)

    for branch in range(2):
        alone, first = (half, 0) if branch == 0 else (0, half)
        columns = pltpu.roll(nat_ref[branch, :, CUM:STEP], -(at * per) % LANES, 1)
        steps = pltpu.roll(nat_ref[branch, :, STEP:], -(at * per) % LANES, 1)
        draw = draw_ref[branch]
        tops, bottoms = 0.0, 0.0
        for k in range(per):
            line = lines_ref[branch, pl.ds(at * per + k, 1), :]
            dk = own_lanes(draw, k, size)
            xk = own_lanes(x_ref[branch], k, size)
            gap = line[:, alone : alone + half] - columns[alone : alone + half, k : k + 1]
            d = jnp.exp(jnp.minimum(gap, 0.0))
            m = d * score[branch, pl.ds(alone, half), pl.ds(alone, half)]
            bottoms = bottoms + mm(m.astype(BF), dk[alone : alone + half])
            xd = mm(xk[alone : alone + half], draw[alone : alone + half], 1, 1)
            ds_own[branch] += d * xd * steps[alone : alone + half, k : k + 1]
            gap = line - columns[first : first + half, k : k + 1]
            d = jnp.exp(jnp.minimum(gap, 0.0))
            m = d * score[branch, pl.ds(first, half), :]
            tops = tops + mm(m.astype(BF), dk)
            xd = mm(xk[first : first + half], draw, 1, 1)
            ds_all[branch] += d * xd * steps[first : first + half, k : k + 1]
        u_ref[branch, pl.ds(alone, half), :] = bottoms
        u_ref[branch, pl.ds(first, half), :] = tops

    @pl.when(at == pl.num_programs(0) - 1)
    def _():
        for branch in range(2):
            alone, first = (half, 0) if branch == 0 else (0, half)
            place, column = iota((half, rows), 0) + first, iota((half, rows), 1)
            seen = (place <= column) if branch == 0 else (place >= column)
            corner = 0 if branch == 0 else rows - 1
            corner = (place == corner) & (column == corner) & (edges_ref[branch] > 0)
            all_part = jnp.where(corner, start_ref[branch, :1, :1], ds_all[branch])
            all_part = jnp.where(seen, all_part, 0.0)
            own_part = jnp.where(ordered(half, 1 - branch), ds_own[branch], 0.0)
            b, c = nat_ref[branch, :, :STATE], nat_ref[branch, :, STATE : 2 * STATE]
            db_ref[branch, pl.ds(first, half), :] = exact(all_part, c)
            db_ref[branch, pl.ds(alone, half), :] = exact(own_part, c[alone : alone + half])
            dc = exact(all_part.T, b[first : first + half])
            dc_own = dc[alone : alone + half] + exact(own_part.T, b[alone : alone + half])
            dc_ref[branch, pl.ds(first, half), :] = dc[first : first + half]
            dc_ref[branch, pl.ds(alone, half), :] = dc_own


def inner_back(x, draw, nat, lines, starts, edges, after):
    _, rows, channels = x.shape
    block = pl.BlockSpec((2, rows, GROUP), lambda j: (0, 0, j))
    return pl.pallas_call(
        inner_back_kernel,
        grid=(channels // GROUP,),
        in_specs=[block, block, whole(nat), whole(lines), whole(starts), SCALARS, ORDER],
        out_specs=[block] + [pl.BlockSpec((2, rows, STATE), lambda j: (0, 0, 0))] * 2,
        out_shape=[
            jax.ShapeDtypeStruct(x.shape, F32),
            jax.ShapeDtypeStruct((2, rows, STATE), F32),
            jax.ShapeDtypeStruct((2, rows, STATE), F32),
        ],
        scratch_shapes=[
            pltpu.VMEM((2, rows, rows), F32),
            pltpu.VMEM((2, rows // 2, rows), F32),
            pltpu.VMEM((2, rows // 2, rows // 2), F32),
        ],
        compiler_params=PARAMS,
        name="inner_back",
    )(x, draw, nat, lines, starts, edges, after)


def finish_kernel(first, count, last, heads, channels, *refs):
    x_ref, u_ref, bf3_ref, s_ref, end_ref, tots_ref, scalars_ref, near_ref, *refs = refs
    arrived, refs = refs[:count], refs[count + 1 :]
    if last:
        nat_ref, db_ref, dc_ref, dc0_ref, ry_ref, rate_ref, *refs = refs
        before, refs = refs[: len(refs) - 4], refs[len(refs) - 4 :]
    out_ref, dbs_ref, direct_ref, dtot_ref = refs
    at = pl.program_id(0)
    start = (first + at) * (GROUP * heads // channels)
    one = spread(heads, channels, start, 1)
    copier = spread(heads, channels, start, 3)
    columns = pl.ds(pl.multiple_of(at * GROUP, GROUP), GROUP)
    rows = x_ref.shape[1]

    def per_head(a):
        high, low = split(a)
        return mm(high, one, 1, 1) + mm(low, one, 1, 1)

    @pl.when(at == 0)
    def _():
        dbs_ref[...] = jnp.zeros_like(dbs_ref)
        direct_ref[...] = jnp.zeros_like(direct_ref)
        dtot_ref[...] = jnp.zeros_like(dtot_ref)

    def tot(n, slot):
        at = 2 * n + 1 - slot
        return tots_ref[at : at + 1]

    def out(slot, g):
        branch = 1 - slot
        g_high, g_low = split(g)
        us = mm(bf3_ref[branch, :, : 3 * STATE], jnp.concatenate([g_high, g_high, g_low], axis=0))
        fade = mm(bf3_ref[branch, :, 3 * STATE : 3 * STATE + 3 * heads], copier)
        step = mm(bf3_ref[branch, :, 3 * STATE + 3 * heads :], copier)
        both = u_ref[branch] + fade * us
        xf = x_ref[branch].astype(F32)
        dx = (step * both).astype(BF)
        band = slice(branch * rows, (branch + 1) * rows)
        if last:
            out_ref[band, columns] = dx
        else:
            out_ref[band] = dx
        direct_ref[branch] += per_head(xf * both)
        weighted = (fade * step * xf).astype(BF)
        sums = mm(weighted, jnp.concatenate([g_high, g_low], axis=0), 1, 1)
        dbs_ref[branch] += sums[:, :STATE] + sums[:, STATE:]
        ended = jnp.exp(tot(0, slot)) * s_ref[branch] + end_ref[branch]
        kept = jnp.sum(g * ended, axis=0, keepdims=True)
        kept = jnp.concatenate([kept, jnp.zeros((7, GROUP), F32)], axis=0)
        dtot_ref[branch] += per_head(kept)[:1]

    gather_states(Scalars(count + 1, scalars_ref), tot, near_ref, arrived, out)

    if last:

        @pl.when(at == pl.num_programs(0) - 1)
        def _():
            width = out_ref.shape[1] - GROUP
            for branch in range(2):
                dbs, direct, dtot = dbs_ref[branch], direct_ref[branch], dtot_ref[branch]
                for n in range(0, len(before), 3):
                    dbs = dbs + before[n][branch]
                    direct = direct + before[n + 1][branch]
                    dtot = dtot + before[n + 2][branch]
                step = nat_ref[branch, :, STEP : STEP + heads]
                pre = nat_ref[branch, :, STEP + heads : STEP + 2 * heads]
                dcum = ry_ref[branch] - step * direct
                dla = exact(ordered(rows, 1 - branch).astype(F32), dcum) + dtot
                dpre = (direct - jnp.exp(rate_ref[...]) * dla) * jax.nn.sigmoid(pre)
                fill = jnp.zeros((rows, GROUP - 2 * STATE - heads), F32)
                small = [db_ref[branch] + dbs, dc_ref[branch] + dc0_ref[branch], dpre, fill]
                small = jnp.concatenate(small, axis=1).astype(BF)
                out_ref[branch * rows : (branch + 1) * rows, width:] = small


def finish(first, groups, x, u, bf3, s_in, ends, tots, scalars, near, arrived, after, more, before):
    _, rows, channels = x.shape
    heads = (bf3.shape[2] - 3 * STATE) // 6
    last = (first + groups) * GROUP == channels
    block = pl.BlockSpec((2, rows, GROUP), lambda j: (0, 0, first + j))
    state = pl.BlockSpec((2, STATE, GROUP), lambda j: (0, 0, first + j))
    flat = lambda n: pl.BlockSpec((n, GROUP), lambda j: (0, first + j))
    extra = [*more, *before] if last else []
    width = (groups + 1 if last else groups) * GROUP
    sums = [(2, rows, STATE), (2, rows, heads), (2, 1, heads)]
    return pl.pallas_call(
        functools.partial(finish_kernel, first, len(arrived), last, heads, channels),
        grid=(groups,),
        in_specs=[block, block, whole(bf3), state, state, flat(tots.shape[0]), SCALARS, state]
        + [flat(STATE)] * len(arrived)
        + [ORDER]
        + [whole(a) for a in extra],
        out_specs=[
            pl.BlockSpec((2 * rows, width), lambda j: (0, 0))
            if last
            else pl.BlockSpec((2 * rows, GROUP), lambda j: (0, j))
        ]
        + [pl.BlockSpec(shape, lambda j: (0, 0, 0)) for shape in sums],
        out_shape=[jax.ShapeDtypeStruct((2 * rows, width), BF)]
        + [jax.ShapeDtypeStruct(shape, F32) for shape in sums],
        compiler_params=PARAMS,
        name="finish",
    )(x, u, bf3, s_in, ends, tots, scalars, near, *arrived, after, *extra)


def turned_kernel(
    chips, where_ref, own_ref, own_mirror_ref, peer_ref, peer_mirror_ref, after, out_ref, held
):
    parts = where_ref.shape[0] - chips
    wide, rows = held.shape[1], held.shape[2]
    thin = wide // parts
    eye = (iota((wide, wide), 0) == iota((wide, wide), 1)).astype(BF)
    back = mirror(wide)
    sources = [(own_ref, eye), (own_mirror_ref, back), (peer_ref, eye), (peer_mirror_ref, back)]
    for n, (ref, turn) in enumerate(sources):
        held[n] = mm(turn, ref[...], 1, 1).astype(BF)
    for n in range(4):
        for k in range(parts):
            start = pl.multiple_of(where_ref[chips + k] * thin, thin)
            out_ref[k * thin : (k + 1) * thin, n * rows : (n + 1) * rows] = held[
                n, pl.ds(start, thin), :
            ]


def turned(h, peer, where, chips, after):
    rows, channels = h.shape
    wide = channels // (2 * chips)
    plain = pl.BlockSpec((rows, wide), lambda m, where: (0, where[m]))
    other = pl.BlockSpec((rows, wide), lambda m, where: (0, 2 * chips - 1 - where[m]))
    return pl.pallas_call(
        functools.partial(turned_kernel, chips),
        grid_spec=pltpu.PrefetchScalarGridSpec(
            num_scalar_prefetch=1,
            grid=(chips,),
            in_specs=[plain, other, plain, other, ORDER],
            out_specs=pl.BlockSpec((wide, 4 * rows), lambda m, where: (m, 0)),
            scratch_shapes=[pltpu.VMEM((4, wide, rows), BF)],
        ),
        out_shape=jax.ShapeDtypeStruct((chips * wide, 4 * rows), BF),
        compiler_params=PARAMS,
        name="turned",
    )(where, h, h, peer, peer, after)


def by_bits(size, bits):
    return sorted(range(size), key=lambda k: [k & bit for bit in bits])


def bits_of(size):
    return [1 << k for k in range(size.bit_length() - 1)]


def tile(rows, start=0, count=None):
    if count is None:
        return pl.BlockSpec((rows, GROUP), lambda j: (0, j))
    return pl.BlockSpec((rows, GROUP), lambda j: (0, jnp.clip(j - start, 0, count - 1)))


def spans(widths):
    counts = [width // GROUP for width in widths]
    return [(sum(counts[:n]), count) for n, count in enumerate(counts)]


def in_span(span):
    at = pl.program_id(0)
    return (at >= span[0]) & (at < span[0] + span[1])


def term_kernel(picked, pieces, left_ref, own_ref, peer_ref, after, *outs):
    depth = own_ref.shape[0]
    for out, blocks, span in zip(outs, picked, pieces):

        @pl.when(in_span(span))
        def _(out=out, blocks=blocks):
            wide = out.shape[0] // len(blocks)
            for n, block in enumerate(blocks):
                left = left_ref[block * wide : (block + 1) * wide]
                term = mm(left[:, :depth], own_ref[...]) + mm(left[:, depth:], peer_ref[...])
                out[n * wide : (n + 1) * wide] = term.astype(out.dtype)


def weight_terms(left, own, peer, picked, widths, kind, after):
    rows, pieces = left.shape[0] // 2, spans(widths)
    return pl.pallas_call(
        functools.partial(term_kernel, picked, pieces),
        grid=(own.shape[1] // GROUP,),
        in_specs=[whole(left), tile(own.shape[0]), tile(own.shape[0]), ORDER],
        out_specs=[tile(rows, *span) for span in pieces],
        out_shape=[jax.ShapeDtypeStruct((rows, width), kind) for width in widths],
        compiler_params=PARAMS,
        name="terms",
    )(left, own, peer, after)


def fold_kernel(pieces, join, final, after, *refs):
    given, outs = refs[: 2 * len(pieces)], refs[2 * len(pieces) :]
    for n, span in enumerate(pieces):
        stay_ref, got_ref = given[2 * n : 2 * n + 2]
        mine = outs if join else outs[2 * n : 2 * n + 2]

        @pl.when(in_span(span))
        def _(stay_ref=stay_ref, got_ref=got_ref, mine=mine):
            total = stay_ref[...] + got_ref[...].astype(F32)
            if final:
                mine[0][...] = total.astype(BF)
            else:
                rows = stay_ref.shape[0] // 2
                mine[0][...] = total[:rows]
                mine[1][...] = total[rows:].astype(BF)


def fold(parts, turn, join=False, final=False):
    height = parts[0][0].shape[0]
    rows = height if final else height // 2
    widths = [stay.shape[1] for stay, _ in parts]
    pieces = spans(widths)
    kinds = [BF] if final else [F32, BF]
    total = sum(widths)
    outs = pl.pallas_call(
        functools.partial(fold_kernel, pieces, join, final),
        grid=(total // GROUP,),
        in_specs=[ORDER] + [tile(height, *span) for span in pieces for _ in range(2)],
        out_specs=[tile(rows) for _ in kinds]
        if join
        else [tile(rows, *span) for span in pieces for _ in kinds],
        out_shape=[
            jax.ShapeDtypeStruct((rows, width), kind)
            for width in ([total] if join else widths)
            for kind in kinds
        ],
        compiler_params=PARAMS,
        name="fold",
    )(turn[0], *[a for part in parts for a in part])
    turn[0] = outs[0]
    return outs[0] if final else [outs[n : n + 2] for n in range(0, len(outs), 2)]


def summing(stays, came, orders, turn):
    dps = lax.axis_size("dp")
    dp_bits = bits_of(dps)
    for n in range(1, len(orders[0])):
        parts = fold(list(zip(stays, came)), turn)
        stays = [stay for stay, _ in parts]
        came = yield [send(go, "ctx", 2 * bits[n]) for (_, go), bits in zip(parts, orders)]
    parts = fold(list(zip(stays, came)), turn, join=True)
    for n, bit in enumerate(dp_bits):
        stay, go = parts[0]
        came = yield [send(go, "dp", bit)]
        parts = fold([(stay, came[0])], turn, join=True, final=n == len(dp_bits) - 1)
    held, came = parts, []
    for bit in dp_bits[::-1]:
        held = jnp.concatenate([held, *came])
        came = yield [send(held, "dp", bit)]
    yield (held, *came)


def together(*groups):
    flat = lax.optimization_barrier([part for group in groups for part in group])
    return [[flat.pop(0) for _ in group] for group in groups]


def place_kernel(chips, where_ref, *refs):
    given, (grad_x_ref, grad_small_ref) = refs[:-2], refs[-2:]
    dps = where_ref.shape[0] - chips
    thin = grad_x_ref.shape[0] // dps
    columns = grad_x_ref.shape[1]
    for k in range(dps):
        target = pl.ds(pl.multiple_of(where_ref[chips + k] * thin, thin), thin)
        column = 0
        for n in range(0, len(given), 2):
            ref, at = (given[n], k) if k < dps // 2 else (given[n + 1], k - dps // 2)
            piece = ref[at * thin : (at + 1) * thin].astype(F32)
            width = min(piece.shape[1], columns - column)
            grad_x_ref[target, column : column + width] = piece[:, :width]
            column += width
            if piece.shape[1] > width:
                grad_small_ref[target, :] = piece[:, width : width + grad_small_ref.shape[1]]


def placed(chips, where, given, wide, channels, small):
    vmem = pl.BlockSpec(memory_space=pltpu.VMEM)
    return pl.pallas_call(
        functools.partial(place_kernel, chips),
        in_specs=[SCALARS] + [vmem] * len(given),
        out_shape=[
            jax.ShapeDtypeStruct((wide, channels), F32),
            jax.ShapeDtypeStruct((wide, small), F32),
        ],
        compiler_params=PARAMS,
        name="placed",
    )(where, *given)


def cut_groups(groups):
    sizes = [groups // 2, groups - groups // 2]
    return [(sum(sizes[:n]), size) for n, size in enumerate(sizes)]


def shards(hidden, x_weight, state_weight, log_rates, step_bias, out_gain, cotangent):
    h, cot = hidden[0], cotangent[0]
    rows, channels = h.shape
    chips = lax.axis_size("ctx") // 2
    place = lax.axis_index("ctx")
    dps, dp_place = lax.axis_size("dp"), lax.axis_index("dp")
    scalars = Scalars(chips).made()
    where = (place ^ (2 * jnp.arange(chips)), dp_place ^ jnp.array(by_bits(dps, bits_of(dps))))
    where = jnp.concatenate(where).astype(jnp.int32)
    peer_h = send(h, "ctx", 1)
    both, nat, lines, cg3, bf3, bt, weight3, tot3 = project_small(
        h, state_weight, log_rates, step_bias
    )
    x, ends = project(both, x_weight, bt, weight3, tot3)
    near = send(ends, "ctx", 1)
    raw_fwd = inner(0, x, nat, lines, ends)
    sums = merge(chips, scalars, raw_fwd, ends, near)
    arrived = exchange(chips, sums)
    left = turned(h, peer_h, where, chips, sums[0])
    raw_rc = inner(1, x, nat, lines, left)
    mixed, draw, ry, adj, dc0, s_in, tots, starts = normed(
        (raw_fwd, raw_rc), x, nat, cg3, out_gain, cot, scalars, ends, near, arrived
    )
    near = send(adj, "ctx", 1)
    sums = merge(chips, scalars, adj, adj, near, tots)
    arrived = exchange(chips, sums)
    edges = jnp.stack([place == 0, place == 2 * chips - 1]).astype(jnp.int32)
    u, db, dc = inner_back(x, draw, nat, lines, starts, edges, sums[0])

    bits = bits_of(chips)
    orders = [bits[n:] + bits[:n] for n in range(2)]
    blocks = [by_bits(chips, order) for order in orders]
    staying, going = [b[: chips // 2] for b in blocks], [b[chips // 2 :] for b in blocks]
    more = [nat, db, dc, dc0, ry, log_rates[None]]
    before = []

    def finished(first, groups, after):
        own, *partial = finish(
            first, groups, x, u, bf3, s_in, ends, tots, scalars, near, arrived, after, more, before
        )
        before.extend(partial)
        return own

    def terms(own, peer, size, picked, kind):
        cuts = [size * GROUP // 2, own.shape[1] - size * GROUP // 2]
        outs = weight_terms(left, own, peer, picked, cuts, kind, turn[0])
        turn[0] = outs[0]
        return outs

    def first_hop(go):
        return [send(part, "ctx", 2 * order[0]) for part, order in zip(go, orders)]

    (start, size), (start_next, size_next) = cut_groups(channels // GROUP)
    own = finished(start, size, db)
    turn = [before[-1]]
    peer = send(own, "ctx", 1)
    came = first_hop(terms(own, peer, size, going, BF))
    own_next = finished(start_next, size_next, turn[0])
    (own_next,), came = together([own_next], came)
    turn[0] = own_next
    peer_next = send(own_next, "ctx", 1)
    ahead = summing(terms(own, peer, size, staying, F32), came, orders, turn)
    hop = next(ahead)
    go, hop = together(terms(own_next, peer_next, size_next, going, BF), hop)
    came = first_hop(go)
    hop = ahead.send(hop)
    stay = terms(own_next, peer_next, size_next, staying, F32)
    hop, came = together(hop, came)
    behind = summing(stay, came, orders, turn)
    hop, hop_next = ahead.send(hop), next(behind)
    while isinstance(hop, list):
        hop, hop_next = together(hop, hop_next)
        hop, hop_next = ahead.send(hop), behind.send(hop_next)
    while isinstance(hop_next, list):
        hop_next = behind.send(hop_next)
    done = [*hop, *hop_next]
    wide = channels // (2 * chips)
    grad_x, grad_small = placed(chips, where, done, wide, channels, state_weight.shape[1])
    return (mixed[None], grad_x, grad_small)


def solution(mesh):
    return jax.shard_map(
        shards,
        mesh=mesh,
        in_specs=(P("dp", "ctx", None), P(), P(), P(), P(), P(), P("dp", "ctx", None)),
        out_specs=(P("dp", "ctx", None), P("ctx", None), P("ctx", None)),
        check_vma=False,
    )
```

```python
import functools

import jax
import jax.numpy as jnp
from jax import lax
from jax.experimental import pallas as pl
from jax.experimental.pallas import tpu as pltpu
from jax.sharding import PartitionSpec as P

STATE = 64
GROUP = 256
LANES = 128
PROJECTED = 512
BF = jnp.bfloat16
F32 = jnp.float32
precise = lax.Precision.HIGHEST
ORDER = pl.BlockSpec(memory_space=pl.ANY)
SCALARS = pl.BlockSpec(memory_space=pltpu.SMEM)
PARAMS = pltpu.CompilerParams(vmem_limit_bytes=48 * 2**20)


def send(array, axis, mask):
    return lax.ppermute(array, axis, [(i, i ^ mask) for i in range(lax.axis_size(axis))])


def mm(a, b, ca=1, cb=0):
    return lax.dot_general(a, b, (((ca,), (cb,)), ((), ())), preferred_element_type=F32)


def exact(a, b, ca=1, cb=0):
    dims = (((ca,), (cb,)), ((), ()))
    return lax.dot_general(a, b, dims, precision=precise, preferred_element_type=F32)


def split(a):
    high = a.astype(BF)
    return high, (a - high.astype(F32)).astype(BF)


def split_three(a, axis):
    high, rest = split(a)
    middle, low = split(a - high.astype(F32))
    return jnp.concatenate([high, middle, low], axis=axis)


def iota(shape, axis):
    return lax.broadcasted_iota(jnp.int32, shape, axis)


def ordered(rows, branch, strict_after=False):
    t, s = iota((rows, rows), 0), iota((rows, rows), 1)
    return (t >= s) if (branch == 0) != strict_after else (t <= s)


def mirror(width):
    return (iota((width, width), 0) + iota((width, width), 1) == width - 1).astype(BF)


def spread(heads, channels, start, copies):
    head = iota((heads, GROUP if start is not None else channels), 0)
    lane = iota((heads, GROUP if start is not None else channels), 1)
    size = channels // heads
    first = 0 if start is None else start
    one = (head == lane // size + first).astype(BF)
    return jnp.concatenate([one] * copies, axis=0)


def flip_lanes(a, eye):
    parts = [mm(a[:, k : k + GROUP], eye).astype(BF) for k in range(0, a.shape[1], GROUP)]
    return jnp.concatenate(parts[::-1], axis=1)


def softplus(a):
    return jnp.maximum(a, 0.0) + jnp.log1p(jnp.exp(-jnp.abs(a)))


def whole(a):
    return pl.BlockSpec(a.shape, lambda *_: (0,) * a.ndim)


def padded(a):
    return jnp.concatenate([a, jnp.zeros((a.shape[0], LANES - a.shape[1]), a.dtype)], axis=1)


CUM, STEP = LANES, 2 * LANES


def small_kernel(
    h_ref, ws_ref, rate_ref, bias_ref,
    both_ref, nat_ref, lines_ref, cg3_ref, bf3_ref, bt_ref, weight3_ref, tot3_ref,
):
    rows, channels = h_ref.shape
    heads = rate_ref.shape[1]
    eye = mirror(GROUP)
    both_ref[:rows] = h_ref[...]
    for k in range(0, channels, GROUP):
        both_ref[rows:, channels - k - GROUP : channels - k] = mm(
            h_ref[:, k : k + GROUP], eye
        ).astype(BF)
    projected = mm(both_ref[...], ws_ref[...], 1, 1)
    for branch in range(2):
        p = projected[branch * rows : (branch + 1) * rows]
        b, c = p[:, :STATE], p[:, STATE : 2 * STATE]
        pre = p[:, 2 * STATE :] + bias_ref[...]
        step = softplus(pre)
        la = -jnp.exp(rate_ref[...]) * step
        cum = exact(ordered(rows, branch).astype(F32), la)
        tot = cum[rows - 1 :] if branch == 0 else cum[:1]
        fade = jnp.exp(tot - cum)
        wide_step, wide_cum = padded(step), padded(cum)
        nat_ref[branch, :, :CUM] = p[:, : 2 * STATE]
        nat_ref[branch, :, CUM:STEP] = wide_cum
        nat_ref[branch, :, STEP:] = padded(jnp.concatenate([step, pre], axis=1))
        lines_ref[branch, :heads] = wide_cum.T[:heads]
        lines_ref[branch, heads:] = wide_step.T[:heads]
        b_high, b_low = split(b)
        c_high, c_low = split(c)
        grow3 = split_three(jnp.exp(cum), 1)
        cg3_ref[branch] = jnp.concatenate(
            [c_high, c_low, c_high, grow3, jnp.zeros_like(grow3)], axis=1
        )
        bf3_ref[branch] = jnp.concatenate(
            [b_high, b_low, b_high, split_three(fade, 1), split_three(step, 1)], axis=1
        )
        bt_ref[branch] = jnp.concatenate([b_high, b_low], axis=1).T
        weight3_ref[branch] = split_three(fade * step, 1)
        tot3_ref[branch] = split_three(jnp.broadcast_to(tot, (8, heads)), 1)


def project_small(h, ws, log_rates, step_bias):
    rows, channels = h.shape
    heads = log_rates.shape[0]
    f32 = lambda *shape: jax.ShapeDtypeStruct(shape, F32)
    bf16 = lambda *shape: jax.ShapeDtypeStruct(shape, BF)
    return pl.pallas_call(
        small_kernel,
        out_shape=[
            bf16(2 * rows, channels),
            f32(2, rows, 3 * LANES),
            f32(2, 2 * heads, rows),
            bf16(2, rows, 3 * STATE + 6 * heads),
            bf16(2, rows, 3 * STATE + 6 * heads),
            bf16(2, 2 * STATE, rows),
            bf16(2, rows, 3 * heads),
            bf16(2, 8, 3 * heads),
        ],
        compiler_params=PARAMS,
        name="small",
    )(h, ws.T, log_rates[None], step_bias[None])


def project_kernel(both_ref, w_ref, bt_ref, weight3_ref, tot3_ref, x_ref, end_ref):
    at = pl.program_id(0)
    rows = x_ref.shape[1]
    heads = weight3_ref.shape[2] // 3
    channels = both_ref.shape[1]
    values = mm(both_ref[...], w_ref[...]).astype(BF)
    for part in range(PROJECTED // GROUP):
        here = slice(part * GROUP, (part + 1) * GROUP)
        group = at * (PROJECTED // GROUP) + part
        copier = spread(heads, channels, group * (GROUP * heads // channels), 3)
        for branch in range(2):
            x = values[branch * rows : (branch + 1) * rows, here]
            x_ref[branch, :, here] = x
            weighted = mm(weight3_ref[branch], copier) * x.astype(F32)
            both = mm(bt_ref[branch], weighted.astype(BF))
            end_ref[branch, :STATE, here] = both[:STATE] + both[STATE:]
            end_ref[branch, STATE:, here] = mm(tot3_ref[branch], copier)


def project(both, w, bt, weight3, tot3):
    rows, channels = both.shape[0] // 2, both.shape[1]
    return pl.pallas_call(
        project_kernel,
        grid=(channels // PROJECTED,),
        in_specs=[
            whole(both),
            pl.BlockSpec((channels, PROJECTED), lambda j: (0, j)),
            whole(bt),
            whole(weight3),
            whole(tot3),
        ],
        out_specs=[
            pl.BlockSpec((2, rows, PROJECTED), lambda j: (0, 0, j)),
            pl.BlockSpec((2, STATE + 8, PROJECTED), lambda j: (0, 0, j)),
        ],
        out_shape=[
            jax.ShapeDtypeStruct((2, rows, channels), BF),
            jax.ShapeDtypeStruct((2, STATE + 8, channels), F32),
        ],
        compiler_params=PARAMS,
        name="project",
    )(both, w, bt, weight3, tot3)


def own_lanes(a, k, size):
    lane = iota(a.shape, 1) // size
    return jnp.where(lane == k, a.astype(F32), 0.0).astype(BF)


def inner_kernel(branch, x_ref, nat_ref, lines_ref, after, raw_ref, score):
    at = pl.program_id(0)
    rows = x_ref.shape[1]
    heads = lines_ref.shape[1] // 2
    size = x_ref.shape[2] * pl.num_programs(0) // heads
    half = rows // 2
    per = GROUP // size

    @pl.when(at == 0)
    def _():
        b, c = nat_ref[0, :, :STATE], nat_ref[0, :, STATE : 2 * STATE]
        score[...] = jnp.where(ordered(rows, branch), exact(c, b, 1, 1), 0.0)

    alone, later = (0, half) if branch == 0 else (half, 0)
    columns = pltpu.roll(nat_ref[0, :, CUM:STEP], -(at * per) % LANES, 1)
    tops, bottoms = 0.0, 0.0
    for k in range(per):
        line = lines_ref[0, pl.ds(at * per + k, 1), :]
        step = lines_ref[0, pl.ds(heads + at * per + k, 1), :]
        xk = own_lanes(x_ref[0], k, size)
        own = pl.ds(alone, half)
        gap = columns[alone : alone + half, k : k + 1] - line[:, alone : alone + half]
        m = jnp.exp(jnp.minimum(gap, 0.0)) * score[own, own] * step[:, alone : alone + half]
        tops = tops + mm(m.astype(BF), xk[alone : alone + half])
        gap = columns[later : later + half, k : k + 1] - line
        m = jnp.exp(jnp.minimum(gap, 0.0)) * score[pl.ds(later, half), :] * step
        bottoms = bottoms + mm(m.astype(BF), xk)
    raw_ref[pl.ds(alone, half), :] = tops
    raw_ref[pl.ds(later, half), :] = bottoms


def inner(branch, x, nat, lines, after):
    _, rows, channels = x.shape
    one = lambda a: pl.BlockSpec((1, *a.shape[1:]), lambda j: (branch, 0, 0))
    return pl.pallas_call(
        functools.partial(inner_kernel, branch),
        grid=(channels // GROUP,),
        in_specs=[
            pl.BlockSpec((1, rows, GROUP), lambda j: (branch, 0, j)),
            one(nat),
            one(lines),
            ORDER,
        ],
        out_specs=pl.BlockSpec((rows, GROUP), lambda j: (0, j)),
        out_shape=jax.ShapeDtypeStruct((rows, channels), F32),
        scratch_shapes=[pltpu.VMEM((rows, rows), F32)],
        compiler_params=PARAMS,
        name="inner",
    )(x, nat, lines, after)


class Scalars:
    def __init__(self, chips, ref=None):
        self.chips, self.ref = chips, ref
        self.bits = bits_of(chips)

    def made(self):
        place = lax.axis_index("ctx")
        chip, core = place // 2, place % 2
        at = chip ^ jnp.arange(1, self.chips)
        up = (chip ^ jnp.array(self.bits)) > chip
        reach = jnp.concatenate([at < chip, at > chip])
        left = (at[None] > at[:, None]) & (at[None] < chip)
        right = (at[None] > chip) & (at[None] < at[:, None])
        parts = [jnp.stack([core == 0, core == 1]), up, reach, left.ravel(), right.ravel()]
        return jnp.concatenate(parts).astype(F32)

    def first(self, slot):
        return self.ref[slot]

    def up(self, n):
        return self.ref[2 + n]

    def reach(self, slot, m):
        return self.ref[2 + len(self.bits) + slot * (self.chips - 1) + m]

    def between(self, slot, m, k):
        most = self.chips - 1
        return self.ref[2 + len(self.bits) + 2 * most + (slot * most + m) * most + k]


def merge_kernel(chips, turned, scalars_ref, after, *refs):
    scalars = Scalars(chips, scalars_ref)
    if turned:
        tots_ref, own_ref, near_ref, *outs = refs
    else:
        own_ref, near_ref, *outs = refs
    sums, tots = [], []
    for slot in range(2):
        if turned:
            own, other = tots_ref[1 - slot : 2 - slot], tots_ref[3 - slot : 4 - slot]
        else:
            own, other = (ref[slot, STATE : STATE + 1] for ref in (own_ref, near_ref))
            tots.append(own + other)
        first = scalars.first(slot)
        a = first * jnp.exp(other) + (1.0 - first)
        p = first + (1.0 - first) * jnp.exp(own)
        sums.append(a * own_ref[slot, :STATE] + p * near_ref[slot, :STATE])
    for n, out in enumerate(outs):
        up = scalars.up(n)
        out[:STATE] = (up * sums[0] + (1.0 - up) * sums[1]).astype(BF)
        if not turned:
            rows = []
            for tot in tots:
                high, rest = split(tot)
                middle, low = split(tot - high.astype(F32))
                rows += [part.astype(F32) for part in (high, middle, low)]
            rows.append(jnp.zeros((16 - len(rows), rows[0].shape[1]), F32))
            out[STATE:] = jnp.concatenate(rows, axis=0).astype(BF)


def merge(chips, scalars, after, own, near, tots=None):
    channels = own.shape[2]
    rows = STATE if tots is not None else STATE + 16
    given = [own, near] if tots is None else [tots, own, near]
    bits = bits_of(chips)
    return pl.pallas_call(
        functools.partial(merge_kernel, chips, tots is not None),
        in_specs=[SCALARS, ORDER] + [pl.BlockSpec(memory_space=pltpu.VMEM)] * len(given),
        out_shape=[jax.ShapeDtypeStruct((rows, channels), BF) for _ in bits],
        compiler_params=PARAMS,
        name="merge",
    )(scalars, after, *given)


def exchange(chips, sums):
    return [send(sums[m.bit_length() - 1], "ctx", 2 * m) for m in range(1, chips)]


def gather_states(scalars, tot, near_ref, arrived, out):
    for slot in range(2):
        last = 1.0 - scalars.first(slot)
        total = last * near_ref[slot, :STATE]
        for m, ref in enumerate(arrived):
            weight = last * tot(1, slot)
            for k in range(len(arrived)):
                weight = weight + scalars.between(slot, m, k) * tot(2 + k, slot)
            weight = scalars.reach(slot, m) * jnp.exp(weight)
            total = total + weight * ref[:STATE].astype(F32)
        out(slot, total)


TILE = 128


def normed_kernel(
    count, heads, raw_fwd_ref, raw_rc_ref, cg3_ref, gain_ref, cot_ref, scalars_ref,
    x_fwd_ref, x_rc_ref, nat_fwd_ref, nat_rc_ref, own_ref, near_ref, *refs,
):
    arrived, refs = refs[:count], refs[count:]
    mixed_ref, draw_ref, ry_ref, adj_ref, dc_ref, s_ref, tots_ref, start_ref, s3 = refs
    at = pl.program_id(0)
    channels = raw_fwd_ref.shape[1]
    copier = spread(heads, channels, None, 3)

    @pl.when(at == 0)
    def _():
        rows = [own_ref[0, :1], own_ref[1, :1]]
        rows += [near_ref[0, STATE : STATE + 1], near_ref[1, STATE : STATE + 1]]
        for ref in arrived:
            parts = ref[STATE:].astype(F32)
            rows += [parts[n : n + 1] + parts[n + 1 : n + 2] + parts[n + 2 : n + 3] for n in (0, 3)]
        fill = tots_ref.shape[0] - len(rows)
        tots_ref[...] = jnp.concatenate(rows + [jnp.zeros((fill, channels), F32)], axis=0)

        def out(slot, total):
            s_ref[slot] = total
            high, low = split(total)
            s3[slot, :STATE] = high
            s3[slot, STATE : 2 * STATE] = high
            s3[slot, 2 * STATE :] = low

        scalars = Scalars(count + 1, scalars_ref)
        gather_states(scalars, lambda n, slot: rows[2 * n + slot], near_ref, arrived, out)
        adj_ref[...] = jnp.zeros_like(adj_ref)

    eye = mirror(GROUP)
    one = spread(heads, channels, None, 1)
    ys = []
    for branch in range(2):
        c3 = cg3_ref[branch, :, : 3 * STATE]
        grow = mm(cg3_ref[branch, :, 3 * STATE : 3 * STATE + 3 * heads], copier)
        raw_ref = raw_fwd_ref if branch == 0 else raw_rc_ref
        r = raw_ref[...] + grow * mm(c3, s3[branch])
        scale = lax.rsqrt(jnp.sum(r * r, axis=1, keepdims=True) * (1.0 / channels) + 1e-05)
        n = r * scale
        ys.append(n * gain_ref[...])
        cot = cot_ref[...] if branch == 0 else flip_lanes(cot_ref[...], eye)
        dz = cot.astype(F32) * gain_ref[...]
        mean = jnp.sum(dz * n, axis=1, keepdims=True) * (1.0 / channels)
        draw = scale * (dz - n * mean)
        draw_ref[branch] = draw.astype(BF)

        x_ref, nat_ref = ((x_fwd_ref, nat_fwd_ref), (x_rc_ref, nat_rc_ref))[branch]
        row, edge = (0, 0) if branch == 0 else (TILE - 1, x_ref.shape[1] - 1)

        @pl.when(at == (0 if branch == 0 else pl.num_programs(0) - 1))
        def _(branch=branch, x_ref=x_ref, nat_ref=nat_ref, row=row, edge=edge, scale=scale, dz=dz):
            step = mm(split_three(nat_ref[0, :, STEP : STEP + heads], 1), copier)
            step = step[0:1] if branch == 0 else step[7:8]
            x = x_ref[0].astype(F32)[edge : edge + 1]
            total = jnp.sum(step * x * dz[row : row + 1], axis=1, keepdims=True)
            value = 1e-05 * scale[row : row + 1] ** 3 * total
            start_ref[branch] = jnp.broadcast_to(value, start_ref.shape[1:])

        high, low = split(draw * r)
        ry_ref[branch] = mm(high, one, 1, 1) + mm(low, one, 1, 1)
        grown = (grow * draw).astype(BF)
        both = mm(c3[:, : 2 * STATE].T, grown)
        adj_ref[1 - branch] += both[:STATE] + both[STATE:]
        both = mm(grown, s3[branch, STATE:], 1, 1)
        dc_ref[branch] = both[:, :STATE] + both[:, STATE:]
    back = flip_lanes(ys[1].astype(BF), eye)
    mixed_ref[...] = (ys[0] + back.astype(F32)).astype(BF)


def normed(raws, x, nat, cg3, gain, cot, scalars, ends, near, arrived):
    rows, channels = raws[0].shape
    heads = (cg3.shape[2] - 3 * STATE) // 6
    band = lambda n: pl.BlockSpec((2, TILE, n), lambda j: (0, j, 0))
    flat = pl.BlockSpec((TILE, channels), lambda j: (j, 0))
    gain = gain[None]
    state = pl.BlockSpec((2, STATE, channels), lambda j: (0, 0, 0))
    tots = -(-2 * (len(arrived) + 2) // 8) * 8
    return pl.pallas_call(
        functools.partial(normed_kernel, len(arrived), heads),
        grid=(rows // TILE,),
        in_specs=[flat, flat, band(cg3.shape[2]), whole(gain), flat, SCALARS]
        + [
            pl.BlockSpec((1, 16, channels), lambda j: (0, 0, 0)),
            pl.BlockSpec((1, 16, channels), lambda j: (1, rows // 16 - 1, 0)),
            pl.BlockSpec((1, 8, nat.shape[2]), lambda j: (0, 0, 0)),
            pl.BlockSpec((1, 8, nat.shape[2]), lambda j: (1, rows // 8 - 1, 0)),
            pl.BlockSpec((2, 8, channels), lambda j: (0, STATE // 8, 0)),
        ]
        + [whole(a) for a in (near, *arrived)],
        out_specs=[flat, band(channels), band(heads), state, band(STATE), state]
        + [
            pl.BlockSpec((tots, channels), lambda j: (0, 0)),
            pl.BlockSpec((2, 8, LANES), lambda j: (0, 0, 0)),
        ],
        out_shape=[
            jax.ShapeDtypeStruct((rows, channels), BF),
            jax.ShapeDtypeStruct((2, rows, channels), BF),
            jax.ShapeDtypeStruct((2, rows, heads), F32),
            jax.ShapeDtypeStruct((2, STATE, channels), F32),
            jax.ShapeDtypeStruct((2, rows, STATE), F32),
            jax.ShapeDtypeStruct((2, STATE, channels), F32),
            jax.ShapeDtypeStruct((tots, channels), F32),
            jax.ShapeDtypeStruct((2, 8, LANES), F32),
        ],
        scratch_shapes=[pltpu.VMEM((2, 3 * STATE, channels), BF)],
        compiler_params=PARAMS,
        name="normed",
    )(*raws, cg3, gain, cot, scalars, x, x, nat, nat, ends, near, *arrived)


def inner_back_kernel(
    x_ref, draw_ref, nat_ref, lines_ref, start_ref, edges_ref, after, u_ref, db_ref, dc_ref, score, ds_all, ds_own,
):
    at = pl.program_id(0)
    rows = x_ref.shape[1]
    heads = lines_ref.shape[1] // 2
    size = x_ref.shape[2] * pl.num_programs(0) // heads
    half = rows // 2
    per = GROUP // size

    @pl.when(at == 0)
    def _():
        for branch in range(2):
            b, c = nat_ref[branch, :, :STATE], nat_ref[branch, :, STATE : 2 * STATE]
            full = exact(b, c, 1, 1)
            score[branch] = jnp.where(ordered(rows, 1 - branch), full, 0.0)
        ds_all[...] = jnp.zeros_like(ds_all)
        ds_own[...] = jnp.zeros_like(ds_own)

    for branch in range(2):
        alone, first = (half, 0) if branch == 0 else (0, half)
        columns = pltpu.roll(nat_ref[branch, :, CUM:STEP], -(at * per) % LANES, 1)
        steps = pltpu.roll(nat_ref[branch, :, STEP:], -(at * per) % LANES, 1)
        draw = draw_ref[branch]
        tops, bottoms = 0.0, 0.0
        for k in range(per):
            line = lines_ref[branch, pl.ds(at * per + k, 1), :]
            dk = own_lanes(draw, k, size)
            xk = own_lanes(x_ref[branch], k, size)
            gap = line[:, alone : alone + half] - columns[alone : alone + half, k : k + 1]
            d = jnp.exp(jnp.minimum(gap, 0.0))
            m = d * score[branch, pl.ds(alone, half), pl.ds(alone, half)]
            bottoms = bottoms + mm(m.astype(BF), dk[alone : alone + half])
            xd = mm(xk[alone : alone + half], draw[alone : alone + half], 1, 1)
            ds_own[branch] += d * xd * steps[alone : alone + half, k : k + 1]
            gap = line - columns[first : first + half, k : k + 1]
            d = jnp.exp(jnp.minimum(gap, 0.0))
            m = d * score[branch, pl.ds(first, half), :]
            tops = tops + mm(m.astype(BF), dk)
            xd = mm(xk[first : first + half], draw, 1, 1)
            ds_all[branch] += d * xd * steps[first : first + half, k : k + 1]
        u_ref[branch, pl.ds(alone, half), :] = bottoms
        u_ref[branch, pl.ds(first, half), :] = tops

    @pl.when(at == pl.num_programs(0) - 1)
    def _():
        for branch in range(2):
            alone, first = (half, 0) if branch == 0 else (0, half)
            place, column = iota((half, rows), 0) + first, iota((half, rows), 1)
            seen = (place <= column) if branch == 0 else (place >= column)
            corner = 0 if branch == 0 else rows - 1
            corner = (place == corner) & (column == corner) & (edges_ref[branch] > 0)
            all_part = jnp.where(corner, start_ref[branch, :1, :1], ds_all[branch])
            all_part = jnp.where(seen, all_part, 0.0)
            own_part = jnp.where(ordered(half, 1 - branch), ds_own[branch], 0.0)
            b, c = nat_ref[branch, :, :STATE], nat_ref[branch, :, STATE : 2 * STATE]
            db_ref[branch, pl.ds(first, half), :] = exact(all_part, c)
            db_ref[branch, pl.ds(alone, half), :] = exact(own_part, c[alone : alone + half])
            dc = exact(all_part.T, b[first : first + half])
            dc_own = dc[alone : alone + half] + exact(own_part.T, b[alone : alone + half])
            dc_ref[branch, pl.ds(first, half), :] = dc[first : first + half]
            dc_ref[branch, pl.ds(alone, half), :] = dc_own


def inner_back(x, draw, nat, lines, starts, edges, after):
    _, rows, channels = x.shape
    block = pl.BlockSpec((2, rows, GROUP), lambda j: (0, 0, j))
    return pl.pallas_call(
        inner_back_kernel,
        grid=(channels // GROUP,),
        in_specs=[block, block, whole(nat), whole(lines), whole(starts), SCALARS, ORDER],
        out_specs=[block] + [pl.BlockSpec((2, rows, STATE), lambda j: (0, 0, 0))] * 2,
        out_shape=[
            jax.ShapeDtypeStruct(x.shape, F32),
            jax.ShapeDtypeStruct((2, rows, STATE), F32),
            jax.ShapeDtypeStruct((2, rows, STATE), F32),
        ],
        scratch_shapes=[
            pltpu.VMEM((2, rows, rows), F32),
            pltpu.VMEM((2, rows // 2, rows), F32),
            pltpu.VMEM((2, rows // 2, rows // 2), F32),
        ],
        compiler_params=PARAMS,
        name="inner_back",
    )(x, draw, nat, lines, starts, edges, after)


def finish_kernel(first, count, last, heads, channels, *refs):
    x_ref, u_ref, bf3_ref, s_ref, end_ref, tots_ref, scalars_ref, near_ref, *refs = refs
    arrived, refs = refs[:count], refs[count + 1 :]
    if last:
        nat_ref, db_ref, dc_ref, dc0_ref, ry_ref, rate_ref, *refs = refs
        before, refs = refs[: len(refs) - 4], refs[len(refs) - 4 :]
    out_ref, dbs_ref, direct_ref, dtot_ref = refs
    at = pl.program_id(0)
    start = (first + at) * (GROUP * heads // channels)
    one = spread(heads, channels, start, 1)
    copier = spread(heads, channels, start, 3)
    columns = pl.ds(pl.multiple_of(at * GROUP, GROUP), GROUP)
    rows = x_ref.shape[1]

    def per_head(a):
        high, low = split(a)
        return mm(high, one, 1, 1) + mm(low, one, 1, 1)

    @pl.when(at == 0)
    def _():
        dbs_ref[...] = jnp.zeros_like(dbs_ref)
        direct_ref[...] = jnp.zeros_like(direct_ref)
        dtot_ref[...] = jnp.zeros_like(dtot_ref)

    def tot(n, slot):
        at = 2 * n + 1 - slot
        return tots_ref[at : at + 1]

    def out(slot, g):
        branch = 1 - slot
        g_high, g_low = split(g)
        us = mm(bf3_ref[branch, :, : 3 * STATE], jnp.concatenate([g_high, g_high, g_low], axis=0))
        fade = mm(bf3_ref[branch, :, 3 * STATE : 3 * STATE + 3 * heads], copier)
        step = mm(bf3_ref[branch, :, 3 * STATE + 3 * heads :], copier)
        both = u_ref[branch] + fade * us
        xf = x_ref[branch].astype(F32)
        dx = (step * both).astype(BF)
        band = slice(branch * rows, (branch + 1) * rows)
        if last:
            out_ref[band, columns] = dx
        else:
            out_ref[band] = dx
        direct_ref[branch] += per_head(xf * both)
        weighted = (fade * step * xf).astype(BF)
        sums = mm(weighted, jnp.concatenate([g_high, g_low], axis=0), 1, 1)
        dbs_ref[branch] += sums[:, :STATE] + sums[:, STATE:]
        ended = jnp.exp(tot(0, slot)) * s_ref[branch] + end_ref[branch]
        kept = jnp.sum(g * ended, axis=0, keepdims=True)
        kept = jnp.concatenate([kept, jnp.zeros((7, GROUP), F32)], axis=0)
        dtot_ref[branch] += per_head(kept)[:1]

    gather_states(Scalars(count + 1, scalars_ref), tot, near_ref, arrived, out)

    if last:

        @pl.when(at == pl.num_programs(0) - 1)
        def _():
            width = out_ref.shape[1] - GROUP
            for branch in range(2):
                dbs, direct, dtot = dbs_ref[branch], direct_ref[branch], dtot_ref[branch]
                for n in range(0, len(before), 3):
                    dbs = dbs + before[n][branch]
                    direct = direct + before[n + 1][branch]
                    dtot = dtot + before[n + 2][branch]
                step = nat_ref[branch, :, STEP : STEP + heads]
                pre = nat_ref[branch, :, STEP + heads : STEP + 2 * heads]
                dcum = ry_ref[branch] - step * direct
                dla = exact(ordered(rows, 1 - branch).astype(F32), dcum) + dtot
                dpre = (direct - jnp.exp(rate_ref[...]) * dla) * jax.nn.sigmoid(pre)
                fill = jnp.zeros((rows, GROUP - 2 * STATE - heads), F32)
                small = [db_ref[branch] + dbs, dc_ref[branch] + dc0_ref[branch], dpre, fill]
                small = jnp.concatenate(small, axis=1).astype(BF)
                out_ref[branch * rows : (branch + 1) * rows, width:] = small


def finish(first, groups, x, u, bf3, s_in, ends, tots, scalars, near, arrived, after, more, before):
    _, rows, channels = x.shape
    heads = (bf3.shape[2] - 3 * STATE) // 6
    last = (first + groups) * GROUP == channels
    block = pl.BlockSpec((2, rows, GROUP), lambda j: (0, 0, first + j))
    state = pl.BlockSpec((2, STATE, GROUP), lambda j: (0, 0, first + j))
    flat = lambda n: pl.BlockSpec((n, GROUP), lambda j: (0, first + j))
    extra = [*more, *before] if last else []
    width = (groups + 1 if last else groups) * GROUP
    sums = [(2, rows, STATE), (2, rows, heads), (2, 1, heads)]
    return pl.pallas_call(
        functools.partial(finish_kernel, first, len(arrived), last, heads, channels),
        grid=(groups,),
        in_specs=[block, block, whole(bf3), state, state, flat(tots.shape[0]), SCALARS, state]
        + [flat(STATE)] * len(arrived)
        + [ORDER]
        + [whole(a) for a in extra],
        out_specs=[
            pl.BlockSpec((2 * rows, width), lambda j: (0, 0))
            if last
            else pl.BlockSpec((2 * rows, GROUP), lambda j: (0, j))
        ]
        + [pl.BlockSpec(shape, lambda j: (0, 0, 0)) for shape in sums],
        out_shape=[jax.ShapeDtypeStruct((2 * rows, width), BF)]
        + [jax.ShapeDtypeStruct(shape, F32) for shape in sums],
        compiler_params=PARAMS,
        name="finish",
    )(x, u, bf3, s_in, ends, tots, scalars, near, *arrived, after, *extra)


def turned_kernel(
    chips, where_ref, own_ref, own_mirror_ref, peer_ref, peer_mirror_ref, after, out_ref, held
):
    parts = where_ref.shape[0] - chips
    wide, rows = held.shape[1], held.shape[2]
    thin = wide // parts
    eye = (iota((wide, wide), 0) == iota((wide, wide), 1)).astype(BF)
    back = mirror(wide)
    sources = [(own_ref, eye), (own_mirror_ref, back), (peer_ref, eye), (peer_mirror_ref, back)]
    for n, (ref, turn) in enumerate(sources):
        held[n] = mm(turn, ref[...], 1, 1).astype(BF)
    for n in range(4):
        for k in range(parts):
            start = pl.multiple_of(where_ref[chips + k] * thin, thin)
            out_ref[k * thin : (k + 1) * thin, n * rows : (n + 1) * rows] = held[
                n, pl.ds(start, thin), :
            ]


def turned(h, peer, where, chips, after):
    rows, channels = h.shape
    wide = channels // (2 * chips)
    plain = pl.BlockSpec((rows, wide), lambda m, where: (0, where[m]))
    other = pl.BlockSpec((rows, wide), lambda m, where: (0, 2 * chips - 1 - where[m]))
    return pl.pallas_call(
        functools.partial(turned_kernel, chips),
        grid_spec=pltpu.PrefetchScalarGridSpec(
            num_scalar_prefetch=1,
            grid=(chips,),
            in_specs=[plain, other, plain, other, ORDER],
            out_specs=pl.BlockSpec((wide, 4 * rows), lambda m, where: (m, 0)),
            scratch_shapes=[pltpu.VMEM((4, wide, rows), BF)],
        ),
        out_shape=jax.ShapeDtypeStruct((chips * wide, 4 * rows), BF),
        compiler_params=PARAMS,
        name="turned",
    )(where, h, h, peer, peer, after)


def by_bits(size, bits):
    return sorted(range(size), key=lambda k: [k & bit for bit in bits])


def bits_of(size):
    return [1 << k for k in range(size.bit_length() - 1)]


def tile(rows, start=0, count=None):
    if count is None:
        return pl.BlockSpec((rows, GROUP), lambda j: (0, j))
    return pl.BlockSpec((rows, GROUP), lambda j: (0, jnp.clip(j - start, 0, count - 1)))


def spans(widths):
    counts = [width // GROUP for width in widths]
    return [(sum(counts[:n]), count) for n, count in enumerate(counts)]


def in_span(span):
    at = pl.program_id(0)
    return (at >= span[0]) & (at < span[0] + span[1])


def term_kernel(picked, pieces, left_ref, own_ref, peer_ref, after, *outs):
    depth = own_ref.shape[0]
    for out, blocks, span in zip(outs, picked, pieces):

        @pl.when(in_span(span))
        def _(out=out, blocks=blocks):
            wide = out.shape[0] // len(blocks)
            for n, block in enumerate(blocks):
                left = left_ref[block * wide : (block + 1) * wide]
                term = mm(left[:, :depth], own_ref[...]) + mm(left[:, depth:], peer_ref[...])
                out[n * wide : (n + 1) * wide] = term.astype(out.dtype)


def weight_terms(left, own, peer, picked, widths, kind, after):
    rows, pieces = left.shape[0] // 2, spans(widths)
    return pl.pallas_call(
        functools.partial(term_kernel, picked, pieces),
        grid=(own.shape[1] // GROUP,),
        in_specs=[whole(left), tile(own.shape[0]), tile(own.shape[0]), ORDER],
        out_specs=[tile(rows, *span) for span in pieces],
        out_shape=[jax.ShapeDtypeStruct((rows, width), kind) for width in widths],
        compiler_params=PARAMS,
        name="terms",
    )(left, own, peer, after)


def fold_kernel(pieces, join, final, after, *refs):
    given, outs = refs[: 2 * len(pieces)], refs[2 * len(pieces) :]
    for n, span in enumerate(pieces):
        stay_ref, got_ref = given[2 * n : 2 * n + 2]
        mine = outs if join else outs[2 * n : 2 * n + 2]

        @pl.when(in_span(span))
        def _(stay_ref=stay_ref, got_ref=got_ref, mine=mine):
            total = stay_ref[...] + got_ref[...].astype(F32)
            if final:
                mine[0][...] = total.astype(BF)
            else:
                rows = stay_ref.shape[0] // 2
                mine[0][...] = total[:rows]
                mine[1][...] = total[rows:].astype(BF)


def fold(parts, turn, join=False, final=False):
    height = parts[0][0].shape[0]
    rows = height if final else height // 2
    widths = [stay.shape[1] for stay, _ in parts]
    pieces = spans(widths)
    kinds = [BF] if final else [F32, BF]
    total = sum(widths)
    outs = pl.pallas_call(
        functools.partial(fold_kernel, pieces, join, final),
        grid=(total // GROUP,),
        in_specs=[ORDER] + [tile(height, *span) for span in pieces for _ in range(2)],
        out_specs=[tile(rows) for _ in kinds]
        if join
        else [tile(rows, *span) for span in pieces for _ in kinds],
        out_shape=[
            jax.ShapeDtypeStruct((rows, width), kind)
            for width in ([total] if join else widths)
            for kind in kinds
        ],
        compiler_params=PARAMS,
        name="fold",
    )(turn[0], *[a for part in parts for a in part])
    turn[0] = outs[0]
    return outs[0] if final else [outs[n : n + 2] for n in range(0, len(outs), 2)]


def summing(stays, came, orders, turn):
    dps = lax.axis_size("dp")
    dp_bits = bits_of(dps)
    for n in range(1, len(orders[0])):
        parts = fold(list(zip(stays, came)), turn)
        stays = [stay for stay, _ in parts]
        came = yield [send(go, "ctx", 2 * bits[n]) for (_, go), bits in zip(parts, orders)]
    parts = fold(list(zip(stays, came)), turn, join=True)
    for n, bit in enumerate(dp_bits):
        stay, go = parts[0]
        came = yield [send(go, "dp", bit)]
        parts = fold([(stay, came[0])], turn, join=True, final=n == len(dp_bits) - 1)
    held, came = parts, []
    for bit in dp_bits[::-1]:
        held = jnp.concatenate([held, *came])
        came = yield [send(held, "dp", bit)]
    yield (held, *came)


def together(*groups):
    flat = lax.optimization_barrier([part for group in groups for part in group])
    return [[flat.pop(0) for _ in group] for group in groups]


def place_kernel(chips, where_ref, *refs):
    given, (grad_x_ref, grad_small_ref) = refs[:-2], refs[-2:]
    dps = where_ref.shape[0] - chips
    thin = grad_x_ref.shape[0] // dps
    columns = grad_x_ref.shape[1]
    for k in range(dps):
        target = pl.ds(pl.multiple_of(where_ref[chips + k] * thin, thin), thin)
        column = 0
        for n in range(0, len(given), 2):
            ref, at = (given[n], k) if k < dps // 2 else (given[n + 1], k - dps // 2)
            piece = ref[at * thin : (at + 1) * thin].astype(F32)
            width = min(piece.shape[1], columns - column)
            grad_x_ref[target, column : column + width] = piece[:, :width]
            column += width
            if piece.shape[1] > width:
                grad_small_ref[target, :] = piece[:, width : width + grad_small_ref.shape[1]]


def placed(chips, where, given, wide, channels, small):
    vmem = pl.BlockSpec(memory_space=pltpu.VMEM)
    return pl.pallas_call(
        functools.partial(place_kernel, chips),
        in_specs=[SCALARS] + [vmem] * len(given),
        out_shape=[
            jax.ShapeDtypeStruct((wide, channels), F32),
            jax.ShapeDtypeStruct((wide, small), F32),
        ],
        compiler_params=PARAMS,
        name="placed",
    )(where, *given)


def cut_groups(groups):
    sizes = [groups // 2, groups - groups // 2]
    return [(sum(sizes[:n]), size) for n, size in enumerate(sizes)]


def shards(hidden, x_weight, state_weight, log_rates, step_bias, out_gain, cotangent):
    h, cot = hidden[0], cotangent[0]
    rows, channels = h.shape
    chips = lax.axis_size("ctx") // 2
    place = lax.axis_index("ctx")
    dps, dp_place = lax.axis_size("dp"), lax.axis_index("dp")
    scalars = Scalars(chips).made()
    where = (place ^ (2 * jnp.arange(chips)), dp_place ^ jnp.array(by_bits(dps, bits_of(dps))))
    where = jnp.concatenate(where).astype(jnp.int32)
    peer_h = send(h, "ctx", 1)
    both, nat, lines, cg3, bf3, bt, weight3, tot3 = project_small(
        h, state_weight, log_rates, step_bias
    )
    x, ends = project(both, x_weight, bt, weight3, tot3)
    near = send(ends, "ctx", 1)
    raw_fwd = inner(0, x, nat, lines, ends)
    sums = merge(chips, scalars, raw_fwd, ends, near)
    arrived = exchange(chips, sums)
    left = turned(h, peer_h, where, chips, sums[0])
    raw_rc = inner(1, x, nat, lines, left)
    mixed, draw, ry, adj, dc0, s_in, tots, starts = normed(
        (raw_fwd, raw_rc), x, nat, cg3, out_gain, cot, scalars, ends, near, arrived
    )
    near = send(adj, "ctx", 1)
    sums = merge(chips, scalars, adj, adj, near, tots)
    arrived = exchange(chips, sums)
    edges = jnp.stack([place == 0, place == 2 * chips - 1]).astype(jnp.int32)
    u, db, dc = inner_back(x, draw, nat, lines, starts, edges, sums[0])

    bits = bits_of(chips)
    orders = [bits[n:] + bits[:n] for n in range(2)]
    blocks = [by_bits(chips, order) for order in orders]
    staying, going = [b[: chips // 2] for b in blocks], [b[chips // 2 :] for b in blocks]
    more = [nat, db, dc, dc0, ry, log_rates[None]]
    before = []

    def finished(first, groups, after):
        own, *partial = finish(
            first, groups, x, u, bf3, s_in, ends, tots, scalars, near, arrived, after, more, before
        )
        before.extend(partial)
        return own

    def terms(own, peer, size, picked, kind):
        cuts = [size * GROUP // 2, own.shape[1] - size * GROUP // 2]
        outs = weight_terms(left, own, peer, picked, cuts, kind, turn[0])
        turn[0] = outs[0]
        return outs

    def first_hop(go):
        return [send(part, "ctx", 2 * order[0]) for part, order in zip(go, orders)]

    (start, size), (start_next, size_next) = cut_groups(channels // GROUP)
    own = finished(start, size, db)
    turn = [before[-1]]
    peer = send(own, "ctx", 1)
    came = first_hop(terms(own, peer, size, going, BF))
    own_next = finished(start_next, size_next, turn[0])
    (own_next,), came = together([own_next], came)
    turn[0] = own_next
    peer_next = send(own_next, "ctx", 1)
    ahead = summing(terms(own, peer, size, staying, F32), came, orders, turn)
    hop = next(ahead)
    go, hop = together(terms(own_next, peer_next, size_next, going, BF), hop)
    came = first_hop(go)
    hop = ahead.send(hop)
    stay = terms(own_next, peer_next, size_next, staying, F32)
    hop, came = together(hop, came)
    behind = summing(stay, came, orders, turn)
    hop, hop_next = ahead.send(hop), next(behind)
    while isinstance(hop, list):
        hop, hop_next = together(hop, hop_next)
        hop, hop_next = ahead.send(hop), behind.send(hop_next)
    while isinstance(hop_next, list):
        hop_next = behind.send(hop_next)
    done = [*hop, *hop_next]
    wide = channels // (2 * chips)
    grad_x, grad_small = placed(chips, where, done, wide, channels, state_weight.shape[1])
    return (mixed[None], grad_x, grad_small)


def solution(mesh):
    return jax.shard_map(
        shards,
        mesh=mesh,
        in_specs=(P("dp", "ctx", None), P(), P(), P(), P(), P(), P("dp", "ctx", None)),
        out_specs=(P("dp", "ctx", None), P("ctx", None), P("ctx", None)),
        check_vma=False,
    )
```

```python
import functools

import jax
import jax.numpy as jnp
from jax import lax
from jax.experimental import pallas as pl
from jax.experimental.pallas import tpu as pltpu
from jax.sharding import PartitionSpec as P

STATE = 64
GROUP = 256
LANES = 128
PROJECTED = 512
BF = jnp.bfloat16
F32 = jnp.float32
precise = lax.Precision.HIGHEST
ORDER = pl.BlockSpec(memory_space=pl.ANY)
SCALARS = pl.BlockSpec(memory_space=pltpu.SMEM)
PARAMS = pltpu.CompilerParams(vmem_limit_bytes=48 * 2**20)


def send(array, axis, mask):
    return lax.ppermute(array, axis, [(i, i ^ mask) for i in range(lax.axis_size(axis))])


def mm(a, b, ca=1, cb=0):
    return lax.dot_general(a, b, (((ca,), (cb,)), ((), ())), preferred_element_type=F32)


def exact(a, b, ca=1, cb=0):
    dims = (((ca,), (cb,)), ((), ()))
    return lax.dot_general(a, b, dims, precision=precise, preferred_element_type=F32)


def split(a):
    high = a.astype(BF)
    return high, (a - high.astype(F32)).astype(BF)


def split_three(a, axis):
    high, rest = split(a)
    middle, low = split(a - high.astype(F32))
    return jnp.concatenate([high, middle, low], axis=axis)


def iota(shape, axis):
    return lax.broadcasted_iota(jnp.int32, shape, axis)


def ordered(rows, branch, strict_after=False):
    t, s = iota((rows, rows), 0), iota((rows, rows), 1)
    return (t >= s) if (branch == 0) != strict_after else (t <= s)


def mirror(width):
    return (iota((width, width), 0) + iota((width, width), 1) == width - 1).astype(BF)


def spread(heads, channels, start, copies):
    head = iota((heads, GROUP if start is not None else channels), 0)
    lane = iota((heads, GROUP if start is not None else channels), 1)
    size = channels // heads
    first = 0 if start is None else start
    one = (head == lane // size + first).astype(BF)
    return jnp.concatenate([one] * copies, axis=0)


def flip_lanes(a, eye):
    parts = [mm(a[:, k : k + GROUP], eye).astype(BF) for k in range(0, a.shape[1], GROUP)]
    return jnp.concatenate(parts[::-1], axis=1)


def softplus(a):
    return jnp.maximum(a, 0.0) + jnp.log1p(jnp.exp(-jnp.abs(a)))


def whole(a):
    return pl.BlockSpec(a.shape, lambda *_: (0,) * a.ndim)


def padded(a):
    return jnp.concatenate([a, jnp.zeros((a.shape[0], LANES - a.shape[1]), a.dtype)], axis=1)


CUM, STEP = LANES, 2 * LANES


def small_kernel(
    h_ref, ws_ref, rate_ref, bias_ref,
    both_ref, nat_ref, lines_ref, cg3_ref, bf3_ref, bt_ref, weight3_ref, tot3_ref,
):
    rows, channels = h_ref.shape
    heads = rate_ref.shape[1]
    eye = mirror(GROUP)
    both_ref[:rows] = h_ref[...]
    for k in range(0, channels, GROUP):
        both_ref[rows:, channels - k - GROUP : channels - k] = mm(
            h_ref[:, k : k + GROUP], eye
        ).astype(BF)
    projected = mm(both_ref[...], ws_ref[...], 1, 1)
    for branch in range(2):
        p = projected[branch * rows : (branch + 1) * rows]
        b, c = p[:, :STATE], p[:, STATE : 2 * STATE]
        pre = p[:, 2 * STATE :] + bias_ref[...]
        step = softplus(pre)
        la = -jnp.exp(rate_ref[...]) * step
        cum = exact(ordered(rows, branch).astype(F32), la)
        tot = cum[rows - 1 :] if branch == 0 else cum[:1]
        fade = jnp.exp(tot - cum)
        wide_step, wide_cum = padded(step), padded(cum)
        nat_ref[branch, :, :CUM] = p[:, : 2 * STATE]
        nat_ref[branch, :, CUM:STEP] = wide_cum
        nat_ref[branch, :, STEP:] = padded(jnp.concatenate([step, pre], axis=1))
        lines_ref[branch, :heads] = wide_cum.T[:heads]
        lines_ref[branch, heads:] = wide_step.T[:heads]
        b_high, b_low = split(b)
        c_high, c_low = split(c)
        grow3 = split_three(jnp.exp(cum), 1)
        cg3_ref[branch] = jnp.concatenate(
            [c_high, c_low, c_high, grow3, jnp.zeros_like(grow3)], axis=1
        )
        bf3_ref[branch] = jnp.concatenate(
            [b_high, b_low, b_high, split_three(fade, 1), split_three(step, 1)], axis=1
        )
        bt_ref[branch] = jnp.concatenate([b_high, b_low], axis=1).T
        weight3_ref[branch] = split_three(fade * step, 1)
        tot3_ref[branch] = split_three(jnp.broadcast_to(tot, (8, heads)), 1)


def project_small(h, ws, log_rates, step_bias):
    rows, channels = h.shape
    heads = log_rates.shape[0]
    f32 = lambda *shape: jax.ShapeDtypeStruct(shape, F32)
    bf16 = lambda *shape: jax.ShapeDtypeStruct(shape, BF)
    return pl.pallas_call(
        small_kernel,
        out_shape=[
            bf16(2 * rows, channels),
            f32(2, rows, 3 * LANES),
            f32(2, 2 * heads, rows),
            bf16(2, rows, 3 * STATE + 6 * heads),
            bf16(2, rows, 3 * STATE + 6 * heads),
            bf16(2, 2 * STATE, rows),
            bf16(2, rows, 3 * heads),
            bf16(2, 8, 3 * heads),
        ],
        compiler_params=PARAMS,
        name="small",
    )(h, ws.T, log_rates[None], step_bias[None])


def project_kernel(both_ref, w_ref, bt_ref, weight3_ref, tot3_ref, x_ref, end_ref):
    at = pl.program_id(0)
    rows = x_ref.shape[1]
    heads = weight3_ref.shape[2] // 3
    channels = both_ref.shape[1]
    values = mm(both_ref[...], w_ref[...]).astype(BF)
    for part in range(PROJECTED // GROUP):
        here = slice(part * GROUP, (part + 1) * GROUP)
        group = at * (PROJECTED // GROUP) + part
        copier = spread(heads, channels, group * (GROUP * heads // channels), 3)
        for branch in range(2):
            x = values[branch * rows : (branch + 1) * rows, here]
            x_ref[branch, :, here] = x
            weighted = mm(weight3_ref[branch], copier) * x.astype(F32)
            both = mm(bt_ref[branch], weighted.astype(BF))
            end_ref[branch, :STATE, here] = both[:STATE] + both[STATE:]
            end_ref[branch, STATE:, here] = mm(tot3_ref[branch], copier)


def project(both, w, bt, weight3, tot3):
    rows, channels = both.shape[0] // 2, both.shape[1]
    return pl.pallas_call(
        project_kernel,
        grid=(channels // PROJECTED,),
        in_specs=[
            whole(both),
            pl.BlockSpec((channels, PROJECTED), lambda j: (0, j)),
            whole(bt),
            whole(weight3),
            whole(tot3),
        ],
        out_specs=[
            pl.BlockSpec((2, rows, PROJECTED), lambda j: (0, 0, j)),
            pl.BlockSpec((2, STATE + 8, PROJECTED), lambda j: (0, 0, j)),
        ],
        out_shape=[
            jax.ShapeDtypeStruct((2, rows, channels), BF),
            jax.ShapeDtypeStruct((2, STATE + 8, channels), F32),
        ],
        compiler_params=PARAMS,
        name="project",
    )(both, w, bt, weight3, tot3)


def own_lanes(a, k, size):
    lane = iota(a.shape, 1) // size
    return jnp.where(lane == k, a.astype(F32), 0.0).astype(BF)


def inner_kernel(branch, x_ref, nat_ref, lines_ref, after, raw_ref, score):
    at = pl.program_id(0)
    rows = x_ref.shape[1]
    heads = lines_ref.shape[1] // 2
    size = x_ref.shape[2] * pl.num_programs(0) // heads
    half = rows // 2
    per = GROUP // size

    @pl.when(at == 0)
    def _():
        b, c = nat_ref[0, :, :STATE], nat_ref[0, :, STATE : 2 * STATE]
        score[...] = jnp.where(ordered(rows, branch), exact(c, b, 1, 1), 0.0)

    alone, later = (0, half) if branch == 0 else (half, 0)
    columns = pltpu.roll(nat_ref[0, :, CUM:STEP], -(at * per) % LANES, 1)
    tops, bottoms = 0.0, 0.0
    for k in range(per):
        line = lines_ref[0, pl.ds(at * per + k, 1), :]
        step = lines_ref[0, pl.ds(heads + at * per + k, 1), :]
        xk = own_lanes(x_ref[0], k, size)
        own = pl.ds(alone, half)
        gap = columns[alone : alone + half, k : k + 1] - line[:, alone : alone + half]
        m = jnp.exp(jnp.minimum(gap, 0.0)) * score[own, own] * step[:, alone : alone + half]
        tops = tops + mm(m.astype(BF), xk[alone : alone + half])
        gap = columns[later : later + half, k : k + 1] - line
        m = jnp.exp(jnp.minimum(gap, 0.0)) * score[pl.ds(later, half), :] * step
        bottoms = bottoms + mm(m.astype(BF), xk)
    raw_ref[pl.ds(alone, half), :] = tops
    raw_ref[pl.ds(later, half), :] = bottoms


def inner(branch, x, nat, lines, after):
    _, rows, channels = x.shape
    one = lambda a: pl.BlockSpec((1, *a.shape[1:]), lambda j: (branch, 0, 0))
    return pl.pallas_call(
        functools.partial(inner_kernel, branch),
        grid=(channels // GROUP,),
        in_specs=[
            pl.BlockSpec((1, rows, GROUP), lambda j: (branch, 0, j)),
            one(nat),
            one(lines),
            ORDER,
        ],
        out_specs=pl.BlockSpec((rows, GROUP), lambda j: (0, j)),
        out_shape=jax.ShapeDtypeStruct((rows, channels), F32),
        scratch_shapes=[pltpu.VMEM((rows, rows), F32)],
        compiler_params=PARAMS,
        name="inner",
    )(x, nat, lines, after)


class Scalars:
    def __init__(self, chips, ref=None):
        self.chips, self.ref = chips, ref
        self.bits = bits_of(chips)

    def made(self):
        place = lax.axis_index("ctx")
        chip, core = place // 2, place % 2
        at = chip ^ jnp.arange(1, self.chips)
        up = (chip ^ jnp.array(self.bits)) > chip
        reach = jnp.concatenate([at < chip, at > chip])
        left = (at[None] > at[:, None]) & (at[None] < chip)
        right = (at[None] > chip) & (at[None] < at[:, None])
        parts = [jnp.stack([core == 0, core == 1]), up, reach, left.ravel(), right.ravel()]
        return jnp.concatenate(parts).astype(F32)

    def first(self, slot):
        return self.ref[slot]

    def up(self, n):
        return self.ref[2 + n]

    def reach(self, slot, m):
        return self.ref[2 + len(self.bits) + slot * (self.chips - 1) + m]

    def between(self, slot, m, k):
        most = self.chips - 1
        return self.ref[2 + len(self.bits) + 2 * most + (slot * most + m) * most + k]


def merge_kernel(chips, turned, scalars_ref, after, *refs):
    scalars = Scalars(chips, scalars_ref)
    if turned:
        tots_ref, own_ref, near_ref, *outs = refs
    else:
        own_ref, near_ref, *outs = refs
    sums, tots = [], []
    for slot in range(2):
        if turned:
            own, other = tots_ref[1 - slot : 2 - slot], tots_ref[3 - slot : 4 - slot]
        else:
            own, other = (ref[slot, STATE : STATE + 1] for ref in (own_ref, near_ref))
            tots.append(own + other)
        first = scalars.first(slot)
        a = first * jnp.exp(other) + (1.0 - first)
        p = first + (1.0 - first) * jnp.exp(own)
        sums.append(a * own_ref[slot, :STATE] + p * near_ref[slot, :STATE])
    for n, out in enumerate(outs):
        up = scalars.up(n)
        out[:STATE] = (up * sums[0] + (1.0 - up) * sums[1]).astype(BF)
        if not turned:
            rows = []
            for tot in tots:
                high, rest = split(tot)
                middle, low = split(tot - high.astype(F32))
                rows += [part.astype(F32) for part in (high, middle, low)]
            rows.append(jnp.zeros((16 - len(rows), rows[0].shape[1]), F32))
            out[STATE:] = jnp.concatenate(rows, axis=0).astype(BF)


def merge(chips, scalars, after, own, near, tots=None):
    channels = own.shape[2]
    rows = STATE if tots is not None else STATE + 16
    given = [own, near] if tots is None else [tots, own, near]
    bits = bits_of(chips)
    return pl.pallas_call(
        functools.partial(merge_kernel, chips, tots is not None),
        in_specs=[SCALARS, ORDER] + [pl.BlockSpec(memory_space=pltpu.VMEM)] * len(given),
        out_shape=[jax.ShapeDtypeStruct((rows, channels), BF) for _ in bits],
        compiler_params=PARAMS,
        name="merge",
    )(scalars, after, *given)


def exchange(chips, sums):
    return [send(sums[m.bit_length() - 1], "ctx", 2 * m) for m in range(1, chips)]


def gather_states(scalars, tot, near_ref, arrived, out):
    for slot in range(2):
        last = 1.0 - scalars.first(slot)
        total = last * near_ref[slot, :STATE]
        for m, ref in enumerate(arrived):
            weight = last * tot(1, slot)
            for k in range(len(arrived)):
                weight = weight + scalars.between(slot, m, k) * tot(2 + k, slot)
            weight = scalars.reach(slot, m) * jnp.exp(weight)
            total = total + weight * ref[:STATE].astype(F32)
        out(slot, total)


TILE = 128


def normed_kernel(
    count, heads, raw_fwd_ref, raw_rc_ref, cg3_ref, gain_ref, cot_ref, scalars_ref,
    x_fwd_ref, x_rc_ref, nat_fwd_ref, nat_rc_ref, own_ref, near_ref, *refs,
):
    arrived, refs = refs[:count], refs[count:]
    mixed_ref, draw_ref, ry_ref, adj_ref, dc_ref, s_ref, tots_ref, start_ref, s3 = refs
    at = pl.program_id(0)
    channels = raw_fwd_ref.shape[1]
    copier = spread(heads, channels, None, 3)

    @pl.when(at == 0)
    def _():
        rows = [own_ref[0, :1], own_ref[1, :1]]
        rows += [near_ref[0, STATE : STATE + 1], near_ref[1, STATE : STATE + 1]]
        for ref in arrived:
            parts = ref[STATE:].astype(F32)
            rows += [parts[n : n + 1] + parts[n + 1 : n + 2] + parts[n + 2 : n + 3] for n in (0, 3)]
        fill = tots_ref.shape[0] - len(rows)
        tots_ref[...] = jnp.concatenate(rows + [jnp.zeros((fill, channels), F32)], axis=0)

        def out(slot, total):
            s_ref[slot] = total
            high, low = split(total)
            s3[slot, :STATE] = high
            s3[slot, STATE : 2 * STATE] = high
            s3[slot, 2 * STATE :] = low

        scalars = Scalars(count + 1, scalars_ref)
        gather_states(scalars, lambda n, slot: rows[2 * n + slot], near_ref, arrived, out)
        adj_ref[...] = jnp.zeros_like(adj_ref)

    eye = mirror(GROUP)
    one = spread(heads, channels, None, 1)
    ys = []
    for branch in range(2):
        c3 = cg3_ref[branch, :, : 3 * STATE]
        grow = mm(cg3_ref[branch, :, 3 * STATE : 3 * STATE + 3 * heads], copier)
        raw_ref = raw_fwd_ref if branch == 0 else raw_rc_ref
        r = raw_ref[...] + grow * mm(c3, s3[branch])
        scale = lax.rsqrt(jnp.sum(r * r, axis=1, keepdims=True) * (1.0 / channels) + 1e-05)
        n = r * scale
        ys.append(n * gain_ref[...])
        cot = cot_ref[...] if branch == 0 else flip_lanes(cot_ref[...], eye)
        dz = cot.astype(F32) * gain_ref[...]
        mean = jnp.sum(dz * n, axis=1, keepdims=True) * (1.0 / channels)
        draw = scale * (dz - n * mean)
        draw_ref[branch] = draw.astype(BF)

        x_ref, nat_ref = ((x_fwd_ref, nat_fwd_ref), (x_rc_ref, nat_rc_ref))[branch]
        row, edge = (0, 0) if branch == 0 else (TILE - 1, x_ref.shape[1] - 1)

        @pl.when(at == (0 if branch == 0 else pl.num_programs(0) - 1))
        def _(branch=branch, x_ref=x_ref, nat_ref=nat_ref, row=row, edge=edge, scale=scale, dz=dz):
            step = mm(split_three(nat_ref[0, :, STEP : STEP + heads], 1), copier)
            step = step[0:1] if branch == 0 else step[7:8]
            x = x_ref[0].astype(F32)[edge : edge + 1]
            total = jnp.sum(step * x * dz[row : row + 1], axis=1, keepdims=True)
            value = 1e-05 * scale[row : row + 1] ** 3 * total
            start_ref[branch] = jnp.broadcast_to(value, start_ref.shape[1:])

        high, low = split(draw * r)
        ry_ref[branch] = mm(high, one, 1, 1) + mm(low, one, 1, 1)
        grown = (grow * draw).astype(BF)
        both = mm(c3[:, : 2 * STATE].T, grown)
        adj_ref[1 - branch] += both[:STATE] + both[STATE:]
        both = mm(grown, s3[branch, STATE:], 1, 1)
        dc_ref[branch] = both[:, :STATE] + both[:, STATE:]
    back = flip_lanes(ys[1].astype(BF), eye)
    mixed_ref[...] = (ys[0] + back.astype(F32)).astype(BF)


def normed(raws, x, nat, cg3, gain, cot, scalars, ends, near, arrived):
    rows, channels = raws[0].shape
    heads = (cg3.shape[2] - 3 * STATE) // 6
    band = lambda n: pl.BlockSpec((2, TILE, n), lambda j: (0, j, 0))
    flat = pl.BlockSpec((TILE, channels), lambda j: (j, 0))
    gain = gain[None]
    state = pl.BlockSpec((2, STATE, channels), lambda j: (0, 0, 0))
    tots = -(-2 * (len(arrived) + 2) // 8) * 8
    return pl.pallas_call(
        functools.partial(normed_kernel, len(arrived), heads),
        grid=(rows // TILE,),
        in_specs=[flat, flat, band(cg3.shape[2]), whole(gain), flat, SCALARS]
        + [
            pl.BlockSpec((1, 16, channels), lambda j: (0, 0, 0)),
            pl.BlockSpec((1, 16, channels), lambda j: (1, rows // 16 - 1, 0)),
            pl.BlockSpec((1, 8, nat.shape[2]), lambda j: (0, 0, 0)),
            pl.BlockSpec((1, 8, nat.shape[2]), lambda j: (1, rows // 8 - 1, 0)),
            pl.BlockSpec((2, 8, channels), lambda j: (0, STATE // 8, 0)),
        ]
        + [whole(a) for a in (near, *arrived)],
        out_specs=[flat, band(channels), band(heads), state, band(STATE), state]
        + [
            pl.BlockSpec((tots, channels), lambda j: (0, 0)),
            pl.BlockSpec((2, 8, LANES), lambda j: (0, 0, 0)),
        ],
        out_shape=[
            jax.ShapeDtypeStruct((rows, channels), BF),
            jax.ShapeDtypeStruct((2, rows, channels), BF),
            jax.ShapeDtypeStruct((2, rows, heads), F32),
            jax.ShapeDtypeStruct((2, STATE, channels), F32),
            jax.ShapeDtypeStruct((2, rows, STATE), F32),
            jax.ShapeDtypeStruct((2, STATE, channels), F32),
            jax.ShapeDtypeStruct((tots, channels), F32),
            jax.ShapeDtypeStruct((2, 8, LANES), F32),
        ],
        scratch_shapes=[pltpu.VMEM((2, 3 * STATE, channels), BF)],
        compiler_params=PARAMS,
        name="normed",
    )(*raws, cg3, gain, cot, scalars, x, x, nat, nat, ends, near, *arrived)


def inner_back_kernel(
    x_ref, draw_ref, nat_ref, lines_ref, start_ref, edges_ref, after, u_ref, db_ref, dc_ref, score, ds_all, ds_own,
):
    at = pl.program_id(0)
    rows = x_ref.shape[1]
    heads = lines_ref.shape[1] // 2
    size = x_ref.shape[2] * pl.num_programs(0) // heads
    half = rows // 2
    per = GROUP // size

    @pl.when(at == 0)
    def _():
        for branch in range(2):
            b, c = nat_ref[branch, :, :STATE], nat_ref[branch, :, STATE : 2 * STATE]
            full = exact(b, c, 1, 1)
            score[branch] = jnp.where(ordered(rows, 1 - branch), full, 0.0)
        ds_all[...] = jnp.zeros_like(ds_all)
        ds_own[...] = jnp.zeros_like(ds_own)

    for branch in range(2):
        alone, first = (half, 0) if branch == 0 else (0, half)
        columns = pltpu.roll(nat_ref[branch, :, CUM:STEP], -(at * per) % LANES, 1)
        steps = pltpu.roll(nat_ref[branch, :, STEP:], -(at * per) % LANES, 1)
        draw = draw_ref[branch]
        tops, bottoms = 0.0, 0.0
        for k in range(per):
            line = lines_ref[branch, pl.ds(at * per + k, 1), :]
            dk = own_lanes(draw, k, size)
            xk = own_lanes(x_ref[branch], k, size)
            gap = line[:, alone : alone + half] - columns[alone : alone + half, k : k + 1]
            d = jnp.exp(jnp.minimum(gap, 0.0))
            m = d * score[branch, pl.ds(alone, half), pl.ds(alone, half)]
            bottoms = bottoms + mm(m.astype(BF), dk[alone : alone + half])
            xd = mm(xk[alone : alone + half], draw[alone : alone + half], 1, 1)
            ds_own[branch] += d * xd * steps[alone : alone + half, k : k + 1]
            gap = line - columns[first : first + half, k : k + 1]
            d = jnp.exp(jnp.minimum(gap, 0.0))
            m = d * score[branch, pl.ds(first, half), :]
            tops = tops + mm(m.astype(BF), dk)
            xd = mm(xk[first : first + half], draw, 1, 1)
            ds_all[branch] += d * xd * steps[first : first + half, k : k + 1]
        u_ref[branch, pl.ds(alone, half), :] = bottoms
        u_ref[branch, pl.ds(first, half), :] = tops

    @pl.when(at == pl.num_programs(0) - 1)
    def _():
        for branch in range(2):
            alone, first = (half, 0) if branch == 0 else (0, half)
            place, column = iota((half, rows), 0) + first, iota((half, rows), 1)
            seen = (place <= column) if branch == 0 else (place >= column)
            corner = 0 if branch == 0 else rows - 1
            corner = (place == corner) & (column == corner) & (edges_ref[branch] > 0)
            all_part = jnp.where(corner, start_ref[branch, :1, :1], ds_all[branch])
            all_part = jnp.where(seen, all_part, 0.0)
            own_part = jnp.where(ordered(half, 1 - branch), ds_own[branch], 0.0)
            b, c = nat_ref[branch, :, :STATE], nat_ref[branch, :, STATE : 2 * STATE]
            db_ref[branch, pl.ds(first, half), :] = exact(all_part, c)
            db_ref[branch, pl.ds(alone, half), :] = exact(own_part, c[alone : alone + half])
            dc = exact(all_part.T, b[first : first + half])
            dc_own = dc[alone : alone + half] + exact(own_part.T, b[alone : alone + half])
            dc_ref[branch, pl.ds(first, half), :] = dc[first : first + half]
            dc_ref[branch, pl.ds(alone, half), :] = dc_own


def inner_back(x, draw, nat, lines, starts, edges, after):
    _, rows, channels = x.shape
    block = pl.BlockSpec((2, rows, GROUP), lambda j: (0, 0, j))
    return pl.pallas_call(
        inner_back_kernel,
        grid=(channels // GROUP,),
        in_specs=[block, block, whole(nat), whole(lines), whole(starts), SCALARS, ORDER],
        out_specs=[block] + [pl.BlockSpec((2, rows, STATE), lambda j: (0, 0, 0))] * 2,
        out_shape=[
            jax.ShapeDtypeStruct(x.shape, F32),
            jax.ShapeDtypeStruct((2, rows, STATE), F32),
            jax.ShapeDtypeStruct((2, rows, STATE), F32),
        ],
        scratch_shapes=[
            pltpu.VMEM((2, rows, rows), F32),
            pltpu.VMEM((2, rows // 2, rows), F32),
            pltpu.VMEM((2, rows // 2, rows // 2), F32),
        ],
        compiler_params=PARAMS,
        name="inner_back",
    )(x, draw, nat, lines, starts, edges, after)


def finish_kernel(first, count, last, heads, channels, *refs):
    x_ref, u_ref, bf3_ref, s_ref, end_ref, tots_ref, scalars_ref, near_ref, *refs = refs
    arrived, refs = refs[:count], refs[count + 1 :]
    if last:
        nat_ref, db_ref, dc_ref, dc0_ref, ry_ref, rate_ref, *refs = refs
        before, refs = refs[: len(refs) - 4], refs[len(refs) - 4 :]
    out_ref, dbs_ref, direct_ref, dtot_ref = refs
    at = pl.program_id(0)
    start = (first + at) * (GROUP * heads // channels)
    one = spread(heads, channels, start, 1)
    copier = spread(heads, channels, start, 3)
    columns = pl.ds(pl.multiple_of(at * GROUP, GROUP), GROUP)
    rows = x_ref.shape[1]

    def per_head(a):
        high, low = split(a)
        return mm(high, one, 1, 1) + mm(low, one, 1, 1)

    @pl.when(at == 0)
    def _():
        dbs_ref[...] = jnp.zeros_like(dbs_ref)
        direct_ref[...] = jnp.zeros_like(direct_ref)
        dtot_ref[...] = jnp.zeros_like(dtot_ref)

    def tot(n, slot):
        at = 2 * n + 1 - slot
        return tots_ref[at : at + 1]

    def out(slot, g):
        branch = 1 - slot
        g_high, g_low = split(g)
        us = mm(bf3_ref[branch, :, : 3 * STATE], jnp.concatenate([g_high, g_high, g_low], axis=0))
        fade = mm(bf3_ref[branch, :, 3 * STATE : 3 * STATE + 3 * heads], copier)
        step = mm(bf3_ref[branch, :, 3 * STATE + 3 * heads :], copier)
        both = u_ref[branch] + fade * us
        xf = x_ref[branch].astype(F32)
        dx = (step * both).astype(BF)
        band = slice(branch * rows, (branch + 1) * rows)
        if last:
            out_ref[band, columns] = dx
        else:
            out_ref[band] = dx
        direct_ref[branch] += per_head(xf * both)
        weighted = (fade * step * xf).astype(BF)
        sums = mm(weighted, jnp.concatenate([g_high, g_low], axis=0), 1, 1)
        dbs_ref[branch] += sums[:, :STATE] + sums[:, STATE:]
        ended = jnp.exp(tot(0, slot)) * s_ref[branch] + end_ref[branch]
        kept = jnp.sum(g * ended, axis=0, keepdims=True)
        kept = jnp.concatenate([kept, jnp.zeros((7, GROUP), F32)], axis=0)
        dtot_ref[branch] += per_head(kept)[:1]

    gather_states(Scalars(count + 1, scalars_ref), tot, near_ref, arrived, out)

    if last:

        @pl.when(at == pl.num_programs(0) - 1)
        def _():
            width = out_ref.shape[1] - GROUP
            for branch in range(2):
                dbs, direct, dtot = dbs_ref[branch], direct_ref[branch], dtot_ref[branch]
                for n in range(0, len(before), 3):
                    dbs = dbs + before[n][branch]
                    direct = direct + before[n + 1][branch]
                    dtot = dtot + before[n + 2][branch]
                step = nat_ref[branch, :, STEP : STEP + heads]
                pre = nat_ref[branch, :, STEP + heads : STEP + 2 * heads]
                dcum = ry_ref[branch] - step * direct
                dla = exact(ordered(rows, 1 - branch).astype(F32), dcum) + dtot
                dpre = (direct - jnp.exp(rate_ref[...]) * dla) * jax.nn.sigmoid(pre)
                fill = jnp.zeros((rows, GROUP - 2 * STATE - heads), F32)
                small = [db_ref[branch] + dbs, dc_ref[branch] + dc0_ref[branch], dpre, fill]
                small = jnp.concatenate(small, axis=1).astype(BF)
                out_ref[branch * rows : (branch + 1) * rows, width:] = small


def finish(first, groups, x, u, bf3, s_in, ends, tots, scalars, near, arrived, after, more, before):
    _, rows, channels = x.shape
    heads = (bf3.shape[2] - 3 * STATE) // 6
    last = (first + groups) * GROUP == channels
    block = pl.BlockSpec((2, rows, GROUP), lambda j: (0, 0, first + j))
    state = pl.BlockSpec((2, STATE, GROUP), lambda j: (0, 0, first + j))
    flat = lambda n: pl.BlockSpec((n, GROUP), lambda j: (0, first + j))
    extra = [*more, *before] if last else []
    width = (groups + 1 if last else groups) * GROUP
    sums = [(2, rows, STATE), (2, rows, heads), (2, 1, heads)]
    return pl.pallas_call(
        functools.partial(finish_kernel, first, len(arrived), last, heads, channels),
        grid=(groups,),
        in_specs=[block, block, whole(bf3), state, state, flat(tots.shape[0]), SCALARS, state]
        + [flat(STATE)] * len(arrived)
        + [ORDER]
        + [whole(a) for a in extra],
        out_specs=[
            pl.BlockSpec((2 * rows, width), lambda j: (0, 0))
            if last
            else pl.BlockSpec((2 * rows, GROUP), lambda j: (0, j))
        ]
        + [pl.BlockSpec(shape, lambda j: (0, 0, 0)) for shape in sums],
        out_shape=[jax.ShapeDtypeStruct((2 * rows, width), BF)]
        + [jax.ShapeDtypeStruct(shape, F32) for shape in sums],
        compiler_params=PARAMS,
        name="finish",
    )(x, u, bf3, s_in, ends, tots, scalars, near, *arrived, after, *extra)


def turned_kernel(
    chips, where_ref, own_ref, own_mirror_ref, peer_ref, peer_mirror_ref, after, out_ref, held
):
    parts = where_ref.shape[0] - chips
    wide, rows = held.shape[1], held.shape[2]
    thin = wide // parts
    eye = (iota((wide, wide), 0) == iota((wide, wide), 1)).astype(BF)
    back = mirror(wide)
    sources = [(own_ref, eye), (own_mirror_ref, back), (peer_ref, eye), (peer_mirror_ref, back)]
    for n, (ref, turn) in enumerate(sources):
        held[n] = mm(turn, ref[...], 1, 1).astype(BF)
    for n in range(4):
        for k in range(parts):
            start = pl.multiple_of(where_ref[chips + k] * thin, thin)
            out_ref[k * thin : (k + 1) * thin, n * rows : (n + 1) * rows] = held[
                n, pl.ds(start, thin), :
            ]


def turned(h, peer, where, chips, after):
    rows, channels = h.shape
    wide = channels // (2 * chips)
    plain = pl.BlockSpec((rows, wide), lambda m, where: (0, where[m]))
    other = pl.BlockSpec((rows, wide), lambda m, where: (0, 2 * chips - 1 - where[m]))
    return pl.pallas_call(
        functools.partial(turned_kernel, chips),
        grid_spec=pltpu.PrefetchScalarGridSpec(
            num_scalar_prefetch=1,
            grid=(chips,),
            in_specs=[plain, other, plain, other, ORDER],
            out_specs=pl.BlockSpec((wide, 4 * rows), lambda m, where: (m, 0)),
            scratch_shapes=[pltpu.VMEM((4, wide, rows), BF)],
        ),
        out_shape=jax.ShapeDtypeStruct((chips * wide, 4 * rows), BF),
        compiler_params=PARAMS,
        name="turned",
    )(where, h, h, peer, peer, after)


def by_bits(size, bits):
    return sorted(range(size), key=lambda k: [k & bit for bit in bits])


def bits_of(size):
    return [1 << k for k in range(size.bit_length() - 1)]


def tile(rows, start=0, count=None):
    if count is None:
        return pl.BlockSpec((rows, GROUP), lambda j: (0, j))
    return pl.BlockSpec((rows, GROUP), lambda j: (0, jnp.clip(j - start, 0, count - 1)))


def spans(widths):
    counts = [width // GROUP for width in widths]
    return [(sum(counts[:n]), count) for n, count in enumerate(counts)]


def in_span(span):
    at = pl.program_id(0)
    return (at >= span[0]) & (at < span[0] + span[1])


def term_kernel(picked, pieces, left_ref, own_ref, peer_ref, after, *outs):
    depth = own_ref.shape[0]
    for out, blocks, span in zip(outs, picked, pieces):

        @pl.when(in_span(span))
        def _(out=out, blocks=blocks):
            wide = out.shape[0] // len(blocks)
            for n, block in enumerate(blocks):
                left = left_ref[block * wide : (block + 1) * wide]
                term = mm(left[:, :depth], own_ref[...]) + mm(left[:, depth:], peer_ref[...])
                out[n * wide : (n + 1) * wide] = term.astype(out.dtype)


def weight_terms(left, own, peer, picked, widths, kind, after):
    rows, pieces = left.shape[0] // 2, spans(widths)
    return pl.pallas_call(
        functools.partial(term_kernel, picked, pieces),
        grid=(own.shape[1] // GROUP,),
        in_specs=[whole(left), tile(own.shape[0]), tile(own.shape[0]), ORDER],
        out_specs=[tile(rows, *span) for span in pieces],
        out_shape=[jax.ShapeDtypeStruct((rows, width), kind) for width in widths],
        compiler_params=PARAMS,
        name="terms",
    )(left, own, peer, after)


def fold_kernel(pieces, join, final, after, *refs):
    given, outs = refs[: 2 * len(pieces)], refs[2 * len(pieces) :]
    for n, span in enumerate(pieces):
        stay_ref, got_ref = given[2 * n : 2 * n + 2]
        mine = outs if join else outs[2 * n : 2 * n + 2]

        @pl.when(in_span(span))
        def _(stay_ref=stay_ref, got_ref=got_ref, mine=mine):
            total = stay_ref[...] + got_ref[...].astype(F32)
            if final:
                mine[0][...] = total.astype(BF)
            else:
                rows = stay_ref.shape[0] // 2
                mine[0][...] = total[:rows]
                mine[1][...] = total[rows:].astype(BF)


def fold(parts, turn, join=False, final=False):
    height = parts[0][0].shape[0]
    rows = height if final else height // 2
    widths = [stay.shape[1] for stay, _ in parts]
    pieces = spans(widths)
    kinds = [BF] if final else [F32, BF]
    total = sum(widths)
    outs = pl.pallas_call(
        functools.partial(fold_kernel, pieces, join, final),
        grid=(total // GROUP,),
        in_specs=[ORDER] + [tile(height, *span) for span in pieces for _ in range(2)],
        out_specs=[tile(rows) for _ in kinds]
        if join
        else [tile(rows, *span) for span in pieces for _ in kinds],
        out_shape=[
            jax.ShapeDtypeStruct((rows, width), kind)
            for width in ([total] if join else widths)
            for kind in kinds
        ],
        compiler_params=PARAMS,
        name="fold",
    )(turn[0], *[a for part in parts for a in part])
    turn[0] = outs[0]
    return outs[0] if final else [outs[n : n + 2] for n in range(0, len(outs), 2)]


def summing(stays, came, orders, turn):
    dps = lax.axis_size("dp")
    dp_bits = bits_of(dps)
    for n in range(1, len(orders[0])):
        parts = fold(list(zip(stays, came)), turn)
        stays = [stay for stay, _ in parts]
        came = yield [send(go, "ctx", 2 * bits[n]) for (_, go), bits in zip(parts, orders)]
    parts = fold(list(zip(stays, came)), turn, join=True)
    for n, bit in enumerate(dp_bits):
        stay, go = parts[0]
        came = yield [send(go, "dp", bit)]
        parts = fold([(stay, came[0])], turn, join=True, final=n == len(dp_bits) - 1)
    held, came = parts, []
    for bit in dp_bits[::-1]:
        held = jnp.concatenate([held, *came])
        came = yield [send(held, "dp", bit)]
    yield (held, *came)


def together(*groups):
    flat = lax.optimization_barrier([part for group in groups for part in group])
    return [[flat.pop(0) for _ in group] for group in groups]


def place_kernel(chips, where_ref, *refs):
    given, (grad_x_ref, grad_small_ref) = refs[:-2], refs[-2:]
    dps = where_ref.shape[0] - chips
    thin = grad_x_ref.shape[0] // dps
    columns = grad_x_ref.shape[1]
    for k in range(dps):
        target = pl.ds(pl.multiple_of(where_ref[chips + k] * thin, thin), thin)
        column = 0
        for n in range(0, len(given), 2):
            ref, at = (given[n], k) if k < dps // 2 else (given[n + 1], k - dps // 2)
            piece = ref[at * thin : (at + 1) * thin].astype(F32)
            width = min(piece.shape[1], columns - column)
            grad_x_ref[target, column : column + width] = piece[:, :width]
            column += width
            if piece.shape[1] > width:
                grad_small_ref[target, :] = piece[:, width : width + grad_small_ref.shape[1]]


def placed(chips, where, given, wide, channels, small):
    vmem = pl.BlockSpec(memory_space=pltpu.VMEM)
    return pl.pallas_call(
        functools.partial(place_kernel, chips),
        in_specs=[SCALARS] + [vmem] * len(given),
        out_shape=[
            jax.ShapeDtypeStruct((wide, channels), F32),
            jax.ShapeDtypeStruct((wide, small), F32),
        ],
        compiler_params=PARAMS,
        name="placed",
    )(where, *given)


def cut_groups(groups):
    sizes = [groups // 2, groups - groups // 2]
    return [(sum(sizes[:n]), size) for n, size in enumerate(sizes)]


def shards(hidden, x_weight, state_weight, log_rates, step_bias, out_gain, cotangent):
    h, cot = hidden[0], cotangent[0]
    rows, channels = h.shape
    chips = lax.axis_size("ctx") // 2
    place = lax.axis_index("ctx")
    dps, dp_place = lax.axis_size("dp"), lax.axis_index("dp")
    scalars = Scalars(chips).made()
    where = (place ^ (2 * jnp.arange(chips)), dp_place ^ jnp.array(by_bits(dps, bits_of(dps))))
    where = jnp.concatenate(where).astype(jnp.int32)
    peer_h = send(h, "ctx", 1)
    both, nat, lines, cg3, bf3, bt, weight3, tot3 = project_small(
        h, state_weight, log_rates, step_bias
    )
    x, ends = project(both, x_weight, bt, weight3, tot3)
    near = send(ends, "ctx", 1)
    raw_fwd = inner(0, x, nat, lines, ends)
    sums = merge(chips, scalars, raw_fwd, ends, near)
    arrived = exchange(chips, sums)
    left = turned(h, peer_h, where, chips, sums[0])
    raw_rc = inner(1, x, nat, lines, left)
    mixed, draw, ry, adj, dc0, s_in, tots, starts = normed(
        (raw_fwd, raw_rc), x, nat, cg3, out_gain, cot, scalars, ends, near, arrived
    )
    near = send(adj, "ctx", 1)
    sums = merge(chips, scalars, adj, adj, near, tots)
    arrived = exchange(chips, sums)
    edges = jnp.stack([place == 0, place == 2 * chips - 1]).astype(jnp.int32)
    u, db, dc = inner_back(x, draw, nat, lines, starts, edges, sums[0])

    bits = bits_of(chips)
    orders = [bits[n:] + bits[:n] for n in range(2)]
    blocks = [by_bits(chips, order) for order in orders]
    staying, going = [b[: chips // 2] for b in blocks], [b[chips // 2 :] for b in blocks]
    more = [nat, db, dc, dc0, ry, log_rates[None]]
    before = []

    def finished(first, groups, after):
        own, *partial = finish(
            first, groups, x, u, bf3, s_in, ends, tots, scalars, near, arrived, after, more, before
        )
        before.extend(partial)
        return own

    def terms(own, peer, size, picked, kind):
        cuts = [size * GROUP // 2, own.shape[1] - size * GROUP // 2]
        outs = weight_terms(left, own, peer, picked, cuts, kind, turn[0])
        turn[0] = outs[0]
        return outs

    def first_hop(go):
        return [send(part, "ctx", 2 * order[0]) for part, order in zip(go, orders)]

    (start, size), (start_next, size_next) = cut_groups(channels // GROUP)
    own = finished(start, size, db)
    turn = [before[-1]]
    peer = send(own, "ctx", 1)
    came = first_hop(terms(own, peer, size, going, BF))
    stay = terms(own, peer, size, staying, F32)
    own_next = finished(start_next, size_next, turn[0])
    (own_next,), came = together([own_next], came)
    turn[0] = own_next
    peer_next = send(own_next, "ctx", 1)
    ahead = summing(stay, came, orders, turn)
    hop = next(ahead)
    go, hop = together(terms(own_next, peer_next, size_next, going, BF), hop)
    came = first_hop(go)
    hop = ahead.send(hop)
    stay = terms(own_next, peer_next, size_next, staying, F32)
    hop, came = together(hop, came)
    behind = summing(stay, came, orders, turn)
    hop, hop_next = ahead.send(hop), next(behind)
    while isinstance(hop, list):
        hop, hop_next = together(hop, hop_next)
        hop, hop_next = ahead.send(hop), behind.send(hop_next)
    while isinstance(hop_next, list):
        hop_next = behind.send(hop_next)
    done = [*hop, *hop_next]
    wide = channels // (2 * chips)
    grad_x, grad_small = placed(chips, where, done, wide, channels, state_weight.shape[1])
    return (mixed[None], grad_x, grad_small)


def solution(mesh):
    return jax.shard_map(
        shards,
        mesh=mesh,
        in_specs=(P("dp", "ctx", None), P(), P(), P(), P(), P(), P("dp", "ctx", None)),
        out_specs=(P("dp", "ctx", None), P("ctx", None), P("ctx", None)),
        check_vma=False,
    )
```

```python
import functools

import jax
import jax.numpy as jnp
from jax import lax
from jax.experimental import pallas as pl
from jax.experimental.pallas import tpu as pltpu
from jax.sharding import PartitionSpec as P

STATE = 64
GROUP = 256
LANES = 128
PROJECTED = 512
BF = jnp.bfloat16
F32 = jnp.float32
precise = lax.Precision.HIGHEST
ORDER = pl.BlockSpec(memory_space=pl.ANY)
SCALARS = pl.BlockSpec(memory_space=pltpu.SMEM)
PARAMS = pltpu.CompilerParams(vmem_limit_bytes=48 * 2**20)


def send(array, axis, mask):
    return lax.ppermute(array, axis, [(i, i ^ mask) for i in range(lax.axis_size(axis))])


def mm(a, b, ca=1, cb=0):
    return lax.dot_general(a, b, (((ca,), (cb,)), ((), ())), preferred_element_type=F32)


def exact(a, b, ca=1, cb=0):
    dims = (((ca,), (cb,)), ((), ()))
    return lax.dot_general(a, b, dims, precision=precise, preferred_element_type=F32)


def split(a):
    high = a.astype(BF)
    return high, (a - high.astype(F32)).astype(BF)


def split_three(a, axis):
    high, rest = split(a)
    middle, low = split(a - high.astype(F32))
    return jnp.concatenate([high, middle, low], axis=axis)


def iota(shape, axis):
    return lax.broadcasted_iota(jnp.int32, shape, axis)


def ordered(rows, branch, strict_after=False):
    t, s = iota((rows, rows), 0), iota((rows, rows), 1)
    return (t >= s) if (branch == 0) != strict_after else (t <= s)


def mirror(width):
    return (iota((width, width), 0) + iota((width, width), 1) == width - 1).astype(BF)


def spread(heads, channels, start, copies):
    head = iota((heads, GROUP if start is not None else channels), 0)
    lane = iota((heads, GROUP if start is not None else channels), 1)
    size = channels // heads
    first = 0 if start is None else start
    one = (head == lane // size + first).astype(BF)
    return jnp.concatenate([one] * copies, axis=0)


def flip_lanes(a, eye):
    parts = [mm(a[:, k : k + GROUP], eye).astype(BF) for k in range(0, a.shape[1], GROUP)]
    return jnp.concatenate(parts[::-1], axis=1)


def softplus(a):
    return jnp.maximum(a, 0.0) + jnp.log1p(jnp.exp(-jnp.abs(a)))


def whole(a):
    return pl.BlockSpec(a.shape, lambda *_: (0,) * a.ndim)


def padded(a):
    return jnp.concatenate([a, jnp.zeros((a.shape[0], LANES - a.shape[1]), a.dtype)], axis=1)


CUM, STEP = LANES, 2 * LANES


def small_kernel(
    h_ref, ws_ref, rate_ref, bias_ref,
    both_ref, nat_ref, lines_ref, cg3_ref, bf3_ref, bt_ref, weight3_ref, tot3_ref,
):
    rows, channels = h_ref.shape
    heads = rate_ref.shape[1]
    eye = mirror(GROUP)
    both_ref[:rows] = h_ref[...]
    for k in range(0, channels, GROUP):
        both_ref[rows:, channels - k - GROUP : channels - k] = mm(
            h_ref[:, k : k + GROUP], eye
        ).astype(BF)
    projected = mm(both_ref[...], ws_ref[...], 1, 1)
    for branch in range(2):
        p = projected[branch * rows : (branch + 1) * rows]
        b, c = p[:, :STATE], p[:, STATE : 2 * STATE]
        pre = p[:, 2 * STATE :] + bias_ref[...]
        step = softplus(pre)
        la = -jnp.exp(rate_ref[...]) * step
        cum = exact(ordered(rows, branch).astype(F32), la)
        tot = cum[rows - 1 :] if branch == 0 else cum[:1]
        fade = jnp.exp(tot - cum)
        wide_step, wide_cum = padded(step), padded(cum)
        nat_ref[branch, :, :CUM] = p[:, : 2 * STATE]
        nat_ref[branch, :, CUM:STEP] = wide_cum
        nat_ref[branch, :, STEP:] = padded(jnp.concatenate([step, pre], axis=1))
        lines_ref[branch, :heads] = wide_cum.T[:heads]
        lines_ref[branch, heads:] = wide_step.T[:heads]
        b_high, b_low = split(b)
        c_high, c_low = split(c)
        grow3 = split_three(jnp.exp(cum), 1)
        cg3_ref[branch] = jnp.concatenate(
            [c_high, c_low, c_high, grow3, jnp.zeros_like(grow3)], axis=1
        )
        bf3_ref[branch] = jnp.concatenate(
            [b_high, b_low, b_high, split_three(fade, 1), split_three(step, 1)], axis=1
        )
        bt_ref[branch] = jnp.concatenate([b_high, b_low], axis=1).T
        weight3_ref[branch] = split_three(fade * step, 1)
        tot3_ref[branch] = split_three(jnp.broadcast_to(tot, (8, heads)), 1)


def project_small(h, ws, log_rates, step_bias):
    rows, channels = h.shape
    heads = log_rates.shape[0]
    f32 = lambda *shape: jax.ShapeDtypeStruct(shape, F32)
    bf16 = lambda *shape: jax.ShapeDtypeStruct(shape, BF)
    return pl.pallas_call(
        small_kernel,
        out_shape=[
            bf16(2 * rows, channels),
            f32(2, rows, 3 * LANES),
            f32(2, 2 * heads, rows),
            bf16(2, rows, 3 * STATE + 6 * heads),
            bf16(2, rows, 3 * STATE + 6 * heads),
            bf16(2, 2 * STATE, rows),
            bf16(2, rows, 3 * heads),
            bf16(2, 8, 3 * heads),
        ],
        compiler_params=PARAMS,
        name="small",
    )(h, ws.T, log_rates[None], step_bias[None])


def project_kernel(both_ref, w_ref, bt_ref, weight3_ref, tot3_ref, x_ref, end_ref):
    at = pl.program_id(0)
    rows = x_ref.shape[1]
    heads = weight3_ref.shape[2] // 3
    channels = both_ref.shape[1]
    values = mm(both_ref[...], w_ref[...]).astype(BF)
    for part in range(PROJECTED // GROUP):
        here = slice(part * GROUP, (part + 1) * GROUP)
        group = at * (PROJECTED // GROUP) + part
        copier = spread(heads, channels, group * (GROUP * heads // channels), 3)
        for branch in range(2):
            x = values[branch * rows : (branch + 1) * rows, here]
            x_ref[branch, :, here] = x
            weighted = mm(weight3_ref[branch], copier) * x.astype(F32)
            both = mm(bt_ref[branch], weighted.astype(BF))
            end_ref[branch, :STATE, here] = both[:STATE] + both[STATE:]
            end_ref[branch, STATE:, here] = mm(tot3_ref[branch], copier)


def project(both, w, bt, weight3, tot3):
    rows, channels = both.shape[0] // 2, both.shape[1]
    return pl.pallas_call(
        project_kernel,
        grid=(channels // PROJECTED,),
        in_specs=[
            whole(both),
            pl.BlockSpec((channels, PROJECTED), lambda j: (0, j)),
            whole(bt),
            whole(weight3),
            whole(tot3),
        ],
        out_specs=[
            pl.BlockSpec((2, rows, PROJECTED), lambda j: (0, 0, j)),
            pl.BlockSpec((2, STATE + 8, PROJECTED), lambda j: (0, 0, j)),
        ],
        out_shape=[
            jax.ShapeDtypeStruct((2, rows, channels), BF),
            jax.ShapeDtypeStruct((2, STATE + 8, channels), F32),
        ],
        compiler_params=PARAMS,
        name="project",
    )(both, w, bt, weight3, tot3)


def own_lanes(a, k, size):
    lane = iota(a.shape, 1) // size
    return jnp.where(lane == k, a.astype(F32), 0.0).astype(BF)


def inner_kernel(branch, x_ref, nat_ref, lines_ref, after, raw_ref, score):
    at = pl.program_id(0)
    rows = x_ref.shape[1]
    heads = lines_ref.shape[1] // 2
    size = x_ref.shape[2] * pl.num_programs(0) // heads
    half = rows // 2
    per = GROUP // size

    @pl.when(at == 0)
    def _():
        b, c = nat_ref[0, :, :STATE], nat_ref[0, :, STATE : 2 * STATE]
        score[...] = jnp.where(ordered(rows, branch), exact(c, b, 1, 1), 0.0)

    alone, later = (0, half) if branch == 0 else (half, 0)
    columns = pltpu.roll(nat_ref[0, :, CUM:STEP], -(at * per) % LANES, 1)
    tops, bottoms = 0.0, 0.0
    for k in range(per):
        line = lines_ref[0, pl.ds(at * per + k, 1), :]
        step = lines_ref[0, pl.ds(heads + at * per + k, 1), :]
        xk = own_lanes(x_ref[0], k, size)
        own = pl.ds(alone, half)
        gap = columns[alone : alone + half, k : k + 1] - line[:, alone : alone + half]
        m = jnp.exp(jnp.minimum(gap, 0.0)) * score[own, own] * step[:, alone : alone + half]
        tops = tops + mm(m.astype(BF), xk[alone : alone + half])
        gap = columns[later : later + half, k : k + 1] - line
        m = jnp.exp(jnp.minimum(gap, 0.0)) * score[pl.ds(later, half), :] * step
        bottoms = bottoms + mm(m.astype(BF), xk)
    raw_ref[pl.ds(alone, half), :] = tops
    raw_ref[pl.ds(later, half), :] = bottoms


def inner(branch, x, nat, lines, after):
    _, rows, channels = x.shape
    one = lambda a: pl.BlockSpec((1, *a.shape[1:]), lambda j: (branch, 0, 0))
    return pl.pallas_call(
        functools.partial(inner_kernel, branch),
        grid=(channels // GROUP,),
        in_specs=[
            pl.BlockSpec((1, rows, GROUP), lambda j: (branch, 0, j)),
            one(nat),
            one(lines),
            ORDER,
        ],
        out_specs=pl.BlockSpec((rows, GROUP), lambda j: (0, j)),
        out_shape=jax.ShapeDtypeStruct((rows, channels), F32),
        scratch_shapes=[pltpu.VMEM((rows, rows), F32)],
        compiler_params=PARAMS,
        name="inner",
    )(x, nat, lines, after)


class Scalars:
    def __init__(self, chips, ref=None):
        self.chips, self.ref = chips, ref
        self.bits = bits_of(chips)

    def made(self):
        place = lax.axis_index("ctx")
        chip, core = place // 2, place % 2
        at = chip ^ jnp.arange(1, self.chips)
        up = (chip ^ jnp.array(self.bits)) > chip
        reach = jnp.concatenate([at < chip, at > chip])
        left = (at[None] > at[:, None]) & (at[None] < chip)
        right = (at[None] > chip) & (at[None] < at[:, None])
        parts = [jnp.stack([core == 0, core == 1]), up, reach, left.ravel(), right.ravel()]
        return jnp.concatenate(parts).astype(F32)

    def first(self, slot):
        return self.ref[slot]

    def up(self, n):
        return self.ref[2 + n]

    def reach(self, slot, m):
        return self.ref[2 + len(self.bits) + slot * (self.chips - 1) + m]

    def between(self, slot, m, k):
        most = self.chips - 1
        return self.ref[2 + len(self.bits) + 2 * most + (slot * most + m) * most + k]


def merge_kernel(chips, turned, scalars_ref, after, *refs):
    scalars = Scalars(chips, scalars_ref)
    if turned:
        tots_ref, own_ref, near_ref, *outs = refs
    else:
        own_ref, near_ref, *outs = refs
    sums, tots = [], []
    for slot in range(2):
        if turned:
            own, other = tots_ref[1 - slot : 2 - slot], tots_ref[3 - slot : 4 - slot]
        else:
            own, other = (ref[slot, STATE : STATE + 1] for ref in (own_ref, near_ref))
            tots.append(own + other)
        first = scalars.first(slot)
        a = first * jnp.exp(other) + (1.0 - first)
        p = first + (1.0 - first) * jnp.exp(own)
        sums.append(a * own_ref[slot, :STATE] + p * near_ref[slot, :STATE])
    for n, out in enumerate(outs):
        up = scalars.up(n)
        out[:STATE] = (up * sums[0] + (1.0 - up) * sums[1]).astype(BF)
        if not turned:
            rows = []
            for tot in tots:
                high, rest = split(tot)
                middle, low = split(tot - high.astype(F32))
                rows += [part.astype(F32) for part in (high, middle, low)]
            rows.append(jnp.zeros((16 - len(rows), rows[0].shape[1]), F32))
            out[STATE:] = jnp.concatenate(rows, axis=0).astype(BF)


def merge(chips, scalars, after, own, near, tots=None):
    channels = own.shape[2]
    rows = STATE if tots is not None else STATE + 16
    given = [own, near] if tots is None else [tots, own, near]
    bits = bits_of(chips)
    return pl.pallas_call(
        functools.partial(merge_kernel, chips, tots is not None),
        in_specs=[SCALARS, ORDER] + [pl.BlockSpec(memory_space=pltpu.VMEM)] * len(given),
        out_shape=[jax.ShapeDtypeStruct((rows, channels), BF) for _ in bits],
        compiler_params=PARAMS,
        name="merge",
    )(scalars, after, *given)


def exchange(chips, sums):
    return [send(sums[m.bit_length() - 1], "ctx", 2 * m) for m in range(1, chips)]


def gather_states(scalars, tot, near_ref, arrived, out):
    for slot in range(2):
        last = 1.0 - scalars.first(slot)
        total = last * near_ref[slot, :STATE]
        for m, ref in enumerate(arrived):
            weight = last * tot(1, slot)
            for k in range(len(arrived)):
                weight = weight + scalars.between(slot, m, k) * tot(2 + k, slot)
            weight = scalars.reach(slot, m) * jnp.exp(weight)
            total = total + weight * ref[:STATE].astype(F32)
        out(slot, total)


TILE = 256


def normed_kernel(
    count, heads, raw_fwd_ref, raw_rc_ref, cg3_ref, gain_ref, cot_ref, scalars_ref,
    x_fwd_ref, x_rc_ref, nat_fwd_ref, nat_rc_ref, own_ref, near_ref, *refs,
):
    arrived, refs = refs[:count], refs[count:]
    mixed_ref, draw_ref, ry_ref, adj_ref, dc_ref, s_ref, tots_ref, start_ref, s3 = refs
    at = pl.program_id(0)
    channels = raw_fwd_ref.shape[1]
    copier = spread(heads, channels, None, 3)

    @pl.when(at == 0)
    def _():
        rows = [own_ref[0, :1], own_ref[1, :1]]
        rows += [near_ref[0, STATE : STATE + 1], near_ref[1, STATE : STATE + 1]]
        for ref in arrived:
            parts = ref[STATE:].astype(F32)
            rows += [parts[n : n + 1] + parts[n + 1 : n + 2] + parts[n + 2 : n + 3] for n in (0, 3)]
        fill = tots_ref.shape[0] - len(rows)
        tots_ref[...] = jnp.concatenate(rows + [jnp.zeros((fill, channels), F32)], axis=0)

        def out(slot, total):
            s_ref[slot] = total
            high, low = split(total)
            s3[slot, :STATE] = high
            s3[slot, STATE : 2 * STATE] = high
            s3[slot, 2 * STATE :] = low

        scalars = Scalars(count + 1, scalars_ref)
        gather_states(scalars, lambda n, slot: rows[2 * n + slot], near_ref, arrived, out)
        adj_ref[...] = jnp.zeros_like(adj_ref)

    eye = mirror(GROUP)
    one = spread(heads, channels, None, 1)
    ys = []
    for branch in range(2):
        c3 = cg3_ref[branch, :, : 3 * STATE]
        grow = mm(cg3_ref[branch, :, 3 * STATE : 3 * STATE + 3 * heads], copier)
        raw_ref = raw_fwd_ref if branch == 0 else raw_rc_ref
        r = raw_ref[...] + grow * mm(c3, s3[branch])
        scale = lax.rsqrt(jnp.sum(r * r, axis=1, keepdims=True) * (1.0 / channels) + 1e-05)
        n = r * scale
        ys.append(n * gain_ref[...])
        cot = cot_ref[...] if branch == 0 else flip_lanes(cot_ref[...], eye)
        dz = cot.astype(F32) * gain_ref[...]
        mean = jnp.sum(dz * n, axis=1, keepdims=True) * (1.0 / channels)
        draw = scale * (dz - n * mean)
        draw_ref[branch] = draw.astype(BF)

        x_ref, nat_ref = ((x_fwd_ref, nat_fwd_ref), (x_rc_ref, nat_rc_ref))[branch]
        row, edge = (0, 0) if branch == 0 else (TILE - 1, x_ref.shape[1] - 1)

        @pl.when(at == (0 if branch == 0 else pl.num_programs(0) - 1))
        def _(branch=branch, x_ref=x_ref, nat_ref=nat_ref, row=row, edge=edge, scale=scale, dz=dz):
            step = mm(split_three(nat_ref[0, :, STEP : STEP + heads], 1), copier)
            step = step[0:1] if branch == 0 else step[7:8]
            x = x_ref[0].astype(F32)[edge : edge + 1]
            total = jnp.sum(step * x * dz[row : row + 1], axis=1, keepdims=True)
            value = 1e-05 * scale[row : row + 1] ** 3 * total
            start_ref[branch] = jnp.broadcast_to(value, start_ref.shape[1:])

        high, low = split(draw * r)
        ry_ref[branch] = mm(high, one, 1, 1) + mm(low, one, 1, 1)
        grown = (grow * draw).astype(BF)
        both = mm(c3[:, : 2 * STATE].T, grown)
        adj_ref[1 - branch] += both[:STATE] + both[STATE:]
        both = mm(grown, s3[branch, STATE:], 1, 1)
        dc_ref[branch] = both[:, :STATE] + both[:, STATE:]
    back = flip_lanes(ys[1].astype(BF), eye)
    mixed_ref[...] = (ys[0] + back.astype(F32)).astype(BF)


def normed(raws, x, nat, cg3, gain, cot, scalars, ends, near, arrived):
    rows, channels = raws[0].shape
    heads = (cg3.shape[2] - 3 * STATE) // 6
    band = lambda n: pl.BlockSpec((2, TILE, n), lambda j: (0, j, 0))
    flat = pl.BlockSpec((TILE, channels), lambda j: (j, 0))
    gain = gain[None]
    state = pl.BlockSpec((2, STATE, channels), lambda j: (0, 0, 0))
    tots = -(-2 * (len(arrived) + 2) // 8) * 8
    return pl.pallas_call(
        functools.partial(normed_kernel, len(arrived), heads),
        grid=(rows // TILE,),
        in_specs=[flat, flat, band(cg3.shape[2]), whole(gain), flat, SCALARS]
        + [
            pl.BlockSpec((1, 16, channels), lambda j: (0, 0, 0)),
            pl.BlockSpec((1, 16, channels), lambda j: (1, rows // 16 - 1, 0)),
            pl.BlockSpec((1, 8, nat.shape[2]), lambda j: (0, 0, 0)),
            pl.BlockSpec((1, 8, nat.shape[2]), lambda j: (1, rows // 8 - 1, 0)),
            pl.BlockSpec((2, 8, channels), lambda j: (0, STATE // 8, 0)),
        ]
        + [whole(a) for a in (near, *arrived)],
        out_specs=[flat, band(channels), band(heads), state, band(STATE), state]
        + [
            pl.BlockSpec((tots, channels), lambda j: (0, 0)),
            pl.BlockSpec((2, 8, LANES), lambda j: (0, 0, 0)),
        ],
        out_shape=[
            jax.ShapeDtypeStruct((rows, channels), BF),
            jax.ShapeDtypeStruct((2, rows, channels), BF),
            jax.ShapeDtypeStruct((2, rows, heads), F32),
            jax.ShapeDtypeStruct((2, STATE, channels), F32),
            jax.ShapeDtypeStruct((2, rows, STATE), F32),
            jax.ShapeDtypeStruct((2, STATE, channels), F32),
            jax.ShapeDtypeStruct((tots, channels), F32),
            jax.ShapeDtypeStruct((2, 8, LANES), F32),
        ],
        scratch_shapes=[pltpu.VMEM((2, 3 * STATE, channels), BF)],
        compiler_params=PARAMS,
        name="normed",
    )(*raws, cg3, gain, cot, scalars, x, x, nat, nat, ends, near, *arrived)


def inner_back_kernel(
    x_ref, draw_ref, nat_ref, lines_ref, start_ref, edges_ref, after, u_ref, db_ref, dc_ref, score, ds_all, ds_own,
):
    at = pl.program_id(0)
    rows = x_ref.shape[1]
    heads = lines_ref.shape[1] // 2
    size = x_ref.shape[2] * pl.num_programs(0) // heads
    half = rows // 2
    per = GROUP // size

    @pl.when(at == 0)
    def _():
        for branch in range(2):
            b, c = nat_ref[branch, :, :STATE], nat_ref[branch, :, STATE : 2 * STATE]
            full = exact(b, c, 1, 1)
            score[branch] = jnp.where(ordered(rows, 1 - branch), full, 0.0)
        ds_all[...] = jnp.zeros_like(ds_all)
        ds_own[...] = jnp.zeros_like(ds_own)

    for branch in range(2):
        alone, first = (half, 0) if branch == 0 else (0, half)
        columns = pltpu.roll(nat_ref[branch, :, CUM:STEP], -(at * per) % LANES, 1)
        steps = pltpu.roll(nat_ref[branch, :, STEP:], -(at * per) % LANES, 1)
        draw = draw_ref[branch]
        tops, bottoms = 0.0, 0.0
        for k in range(per):
            line = lines_ref[branch, pl.ds(at * per + k, 1), :]
            dk = own_lanes(draw, k, size)
            xk = own_lanes(x_ref[branch], k, size)
            gap = line[:, alone : alone + half] - columns[alone : alone + half, k : k + 1]
            d = jnp.exp(jnp.minimum(gap, 0.0))
            m = d * score[branch, pl.ds(alone, half), pl.ds(alone, half)]
            bottoms = bottoms + mm(m.astype(BF), dk[alone : alone + half])
            xd = mm(xk[alone : alone + half], draw[alone : alone + half], 1, 1)
            ds_own[branch] += d * xd * steps[alone : alone + half, k : k + 1]
            gap = line - columns[first : first + half, k : k + 1]
            d = jnp.exp(jnp.minimum(gap, 0.0))
            m = d * score[branch, pl.ds(first, half), :]
            tops = tops + mm(m.astype(BF), dk)
            xd = mm(xk[first : first + half], draw, 1, 1)
            ds_all[branch] += d * xd * steps[first : first + half, k : k + 1]
        u_ref[branch, pl.ds(alone, half), :] = bottoms
        u_ref[branch, pl.ds(first, half), :] = tops

    @pl.when(at == pl.num_programs(0) - 1)
    def _():
        for branch in range(2):
            alone, first = (half, 0) if branch == 0 else (0, half)
            place, column = iota((half, rows), 0) + first, iota((half, rows), 1)
            seen = (place <= column) if branch == 0 else (place >= column)
            corner = 0 if branch == 0 else rows - 1
            corner = (place == corner) & (column == corner) & (edges_ref[branch] > 0)
            all_part = jnp.where(corner, start_ref[branch, :1, :1], ds_all[branch])
            all_part = jnp.where(seen, all_part, 0.0)
            own_part = jnp.where(ordered(half, 1 - branch), ds_own[branch], 0.0)
            b, c = nat_ref[branch, :, :STATE], nat_ref[branch, :, STATE : 2 * STATE]
            db_ref[branch, pl.ds(first, half), :] = exact(all_part, c)
            db_ref[branch, pl.ds(alone, half), :] = exact(own_part, c[alone : alone + half])
            dc = exact(all_part.T, b[first : first + half])
            dc_own = dc[alone : alone + half] + exact(own_part.T, b[alone : alone + half])
            dc_ref[branch, pl.ds(first, half), :] = dc[first : first + half]
            dc_ref[branch, pl.ds(alone, half), :] = dc_own


def inner_back(x, draw, nat, lines, starts, edges, after):
    _, rows, channels = x.shape
    block = pl.BlockSpec((2, rows, GROUP), lambda j: (0, 0, j))
    return pl.pallas_call(
        inner_back_kernel,
        grid=(channels // GROUP,),
        in_specs=[block, block, whole(nat), whole(lines), whole(starts), SCALARS, ORDER],
        out_specs=[block] + [pl.BlockSpec((2, rows, STATE), lambda j: (0, 0, 0))] * 2,
        out_shape=[
            jax.ShapeDtypeStruct(x.shape, F32),
            jax.ShapeDtypeStruct((2, rows, STATE), F32),
            jax.ShapeDtypeStruct((2, rows, STATE), F32),
        ],
        scratch_shapes=[
            pltpu.VMEM((2, rows, rows), F32),
            pltpu.VMEM((2, rows // 2, rows), F32),
            pltpu.VMEM((2, rows // 2, rows // 2), F32),
        ],
        compiler_params=PARAMS,
        name="inner_back",
    )(x, draw, nat, lines, starts, edges, after)


def finish_kernel(first, count, last, heads, channels, *refs):
    x_ref, u_ref, bf3_ref, s_ref, end_ref, tots_ref, scalars_ref, near_ref, *refs = refs
    arrived, refs = refs[:count], refs[count + 1 :]
    if last:
        nat_ref, db_ref, dc_ref, dc0_ref, ry_ref, rate_ref, *refs = refs
        before, refs = refs[: len(refs) - 4], refs[len(refs) - 4 :]
    out_ref, dbs_ref, direct_ref, dtot_ref = refs
    at = pl.program_id(0)
    start = (first + at) * (GROUP * heads // channels)
    one = spread(heads, channels, start, 1)
    copier = spread(heads, channels, start, 3)
    columns = pl.ds(pl.multiple_of(at * GROUP, GROUP), GROUP)
    rows = x_ref.shape[1]

    def per_head(a):
        high, low = split(a)
        return mm(high, one, 1, 1) + mm(low, one, 1, 1)

    @pl.when(at == 0)
    def _():
        dbs_ref[...] = jnp.zeros_like(dbs_ref)
        direct_ref[...] = jnp.zeros_like(direct_ref)
        dtot_ref[...] = jnp.zeros_like(dtot_ref)

    def tot(n, slot):
        at = 2 * n + 1 - slot
        return tots_ref[at : at + 1]

    def out(slot, g):
        branch = 1 - slot
        g_high, g_low = split(g)
        us = mm(bf3_ref[branch, :, : 3 * STATE], jnp.concatenate([g_high, g_high, g_low], axis=0))
        fade = mm(bf3_ref[branch, :, 3 * STATE : 3 * STATE + 3 * heads], copier)
        step = mm(bf3_ref[branch, :, 3 * STATE + 3 * heads :], copier)
        both = u_ref[branch] + fade * us
        xf = x_ref[branch].astype(F32)
        dx = (step * both).astype(BF)
        band = slice(branch * rows, (branch + 1) * rows)
        if last:
            out_ref[band, columns] = dx
        else:
            out_ref[band] = dx
        direct_ref[branch] += per_head(xf * both)
        weighted = (fade * step * xf).astype(BF)
        sums = mm(weighted, jnp.concatenate([g_high, g_low], axis=0), 1, 1)
        dbs_ref[branch] += sums[:, :STATE] + sums[:, STATE:]
        ended = jnp.exp(tot(0, slot)) * s_ref[branch] + end_ref[branch]
        kept = jnp.sum(g * ended, axis=0, keepdims=True)
        kept = jnp.concatenate([kept, jnp.zeros((7, GROUP), F32)], axis=0)
        dtot_ref[branch] += per_head(kept)[:1]

    gather_states(Scalars(count + 1, scalars_ref), tot, near_ref, arrived, out)

    if last:

        @pl.when(at == pl.num_programs(0) - 1)
        def _():
            width = out_ref.shape[1] - GROUP
            for branch in range(2):
                dbs, direct, dtot = dbs_ref[branch], direct_ref[branch], dtot_ref[branch]
                for n in range(0, len(before), 3):
                    dbs = dbs + before[n][branch]
                    direct = direct + before[n + 1][branch]
                    dtot = dtot + before[n + 2][branch]
                step = nat_ref[branch, :, STEP : STEP + heads]
                pre = nat_ref[branch, :, STEP + heads : STEP + 2 * heads]
                dcum = ry_ref[branch] - step * direct
                dla = exact(ordered(rows, 1 - branch).astype(F32), dcum) + dtot
                dpre = (direct - jnp.exp(rate_ref[...]) * dla) * jax.nn.sigmoid(pre)
                fill = jnp.zeros((rows, GROUP - 2 * STATE - heads), F32)
                small = [db_ref[branch] + dbs, dc_ref[branch] + dc0_ref[branch], dpre, fill]
                small = jnp.concatenate(small, axis=1).astype(BF)
                out_ref[branch * rows : (branch + 1) * rows, width:] = small


def finish(first, groups, x, u, bf3, s_in, ends, tots, scalars, near, arrived, after, more, before):
    _, rows, channels = x.shape
    heads = (bf3.shape[2] - 3 * STATE) // 6
    last = (first + groups) * GROUP == channels
    block = pl.BlockSpec((2, rows, GROUP), lambda j: (0, 0, first + j))
    state = pl.BlockSpec((2, STATE, GROUP), lambda j: (0, 0, first + j))
    flat = lambda n: pl.BlockSpec((n, GROUP), lambda j: (0, first + j))
    extra = [*more, *before] if last else []
    width = (groups + 1 if last else groups) * GROUP
    sums = [(2, rows, STATE), (2, rows, heads), (2, 1, heads)]
    return pl.pallas_call(
        functools.partial(finish_kernel, first, len(arrived), last, heads, channels),
        grid=(groups,),
        in_specs=[block, block, whole(bf3), state, state, flat(tots.shape[0]), SCALARS, state]
        + [flat(STATE)] * len(arrived)
        + [ORDER]
        + [whole(a) for a in extra],
        out_specs=[
            pl.BlockSpec((2 * rows, width), lambda j: (0, 0))
            if last
            else pl.BlockSpec((2 * rows, GROUP), lambda j: (0, j))
        ]
        + [pl.BlockSpec(shape, lambda j: (0, 0, 0)) for shape in sums],
        out_shape=[jax.ShapeDtypeStruct((2 * rows, width), BF)]
        + [jax.ShapeDtypeStruct(shape, F32) for shape in sums],
        compiler_params=PARAMS,
        name="finish",
    )(x, u, bf3, s_in, ends, tots, scalars, near, *arrived, after, *extra)


def turned_kernel(
    chips, where_ref, own_ref, own_mirror_ref, peer_ref, peer_mirror_ref, after, out_ref, held
):
    parts = where_ref.shape[0] - chips
    wide, rows = held.shape[1], held.shape[2]
    thin = wide // parts
    eye = (iota((wide, wide), 0) == iota((wide, wide), 1)).astype(BF)
    back = mirror(wide)
    sources = [(own_ref, eye), (own_mirror_ref, back), (peer_ref, eye), (peer_mirror_ref, back)]
    for n, (ref, turn) in enumerate(sources):
        held[n] = mm(turn, ref[...], 1, 1).astype(BF)
    for n in range(4):
        for k in range(parts):
            start = pl.multiple_of(where_ref[chips + k] * thin, thin)
            out_ref[k * thin : (k + 1) * thin, n * rows : (n + 1) * rows] = held[
                n, pl.ds(start, thin), :
            ]


def turned(h, peer, where, chips, after):
    rows, channels = h.shape
    wide = channels // (2 * chips)
    plain = pl.BlockSpec((rows, wide), lambda m, where: (0, where[m]))
    other = pl.BlockSpec((rows, wide), lambda m, where: (0, 2 * chips - 1 - where[m]))
    return pl.pallas_call(
        functools.partial(turned_kernel, chips),
        grid_spec=pltpu.PrefetchScalarGridSpec(
            num_scalar_prefetch=1,
            grid=(chips,),
            in_specs=[plain, other, plain, other, ORDER],
            out_specs=pl.BlockSpec((wide, 4 * rows), lambda m, where: (m, 0)),
            scratch_shapes=[pltpu.VMEM((4, wide, rows), BF)],
        ),
        out_shape=jax.ShapeDtypeStruct((chips * wide, 4 * rows), BF),
        compiler_params=PARAMS,
        name="turned",
    )(where, h, h, peer, peer, after)


def by_bits(size, bits):
    return sorted(range(size), key=lambda k: [k & bit for bit in bits])


def bits_of(size):
    return [1 << k for k in range(size.bit_length() - 1)]


def tile(rows, start=0, count=None):
    if count is None:
        return pl.BlockSpec((rows, GROUP), lambda j: (0, j))
    return pl.BlockSpec((rows, GROUP), lambda j: (0, jnp.clip(j - start, 0, count - 1)))


def spans(widths):
    counts = [width // GROUP for width in widths]
    return [(sum(counts[:n]), count) for n, count in enumerate(counts)]


def in_span(span):
    at = pl.program_id(0)
    return (at >= span[0]) & (at < span[0] + span[1])


def term_kernel(picked, pieces, left_ref, own_ref, peer_ref, after, *outs):
    depth = own_ref.shape[0]
    for out, blocks, span in zip(outs, picked, pieces):

        @pl.when(in_span(span))
        def _(out=out, blocks=blocks):
            wide = out.shape[0] // len(blocks)
            for n, block in enumerate(blocks):
                left = left_ref[block * wide : (block + 1) * wide]
                term = mm(left[:, :depth], own_ref[...]) + mm(left[:, depth:], peer_ref[...])
                out[n * wide : (n + 1) * wide] = term.astype(out.dtype)


def weight_terms(left, own, peer, picked, widths, kind, after):
    rows, pieces = left.shape[0] // 2, spans(widths)
    return pl.pallas_call(
        functools.partial(term_kernel, picked, pieces),
        grid=(own.shape[1] // GROUP,),
        in_specs=[whole(left), tile(own.shape[0]), tile(own.shape[0]), ORDER],
        out_specs=[tile(rows, *span) for span in pieces],
        out_shape=[jax.ShapeDtypeStruct((rows, width), kind) for width in widths],
        compiler_params=PARAMS,
        name="terms",
    )(left, own, peer, after)


def fold_kernel(pieces, join, final, after, *refs):
    given, outs = refs[: 2 * len(pieces)], refs[2 * len(pieces) :]
    for n, span in enumerate(pieces):
        stay_ref, got_ref = given[2 * n : 2 * n + 2]
        mine = outs if join else outs[2 * n : 2 * n + 2]

        @pl.when(in_span(span))
        def _(stay_ref=stay_ref, got_ref=got_ref, mine=mine):
            total = stay_ref[...] + got_ref[...].astype(F32)
            if final:
                mine[0][...] = total.astype(BF)
            else:
                rows = stay_ref.shape[0] // 2
                mine[0][...] = total[:rows]
                mine[1][...] = total[rows:].astype(BF)


def fold(parts, turn, join=False, final=False):
    height = parts[0][0].shape[0]
    rows = height if final else height // 2
    widths = [stay.shape[1] for stay, _ in parts]
    pieces = spans(widths)
    kinds = [BF] if final else [F32, BF]
    total = sum(widths)
    outs = pl.pallas_call(
        functools.partial(fold_kernel, pieces, join, final),
        grid=(total // GROUP,),
        in_specs=[ORDER] + [tile(height, *span) for span in pieces for _ in range(2)],
        out_specs=[tile(rows) for _ in kinds]
        if join
        else [tile(rows, *span) for span in pieces for _ in kinds],
        out_shape=[
            jax.ShapeDtypeStruct((rows, width), kind)
            for width in ([total] if join else widths)
            for kind in kinds
        ],
        compiler_params=PARAMS,
        name="fold",
    )(turn[0], *[a for part in parts for a in part])
    turn[0] = outs[0]
    return outs[0] if final else [outs[n : n + 2] for n in range(0, len(outs), 2)]


def summing(stays, came, orders, turn):
    dps = lax.axis_size("dp")
    dp_bits = bits_of(dps)
    for n in range(1, len(orders[0])):
        parts = fold(list(zip(stays, came)), turn)
        stays = [stay for stay, _ in parts]
        came = yield [send(go, "ctx", 2 * bits[n]) for (_, go), bits in zip(parts, orders)]
    parts = fold(list(zip(stays, came)), turn, join=True)
    for n, bit in enumerate(dp_bits):
        stay, go = parts[0]
        came = yield [send(go, "dp", bit)]
        parts = fold([(stay, came[0])], turn, join=True, final=n == len(dp_bits) - 1)
    held, came = parts, []
    for bit in dp_bits[::-1]:
        held = jnp.concatenate([held, *came])
        came = yield [send(held, "dp", bit)]
    yield (held, *came)


def together(*groups):
    flat = lax.optimization_barrier([part for group in groups for part in group])
    return [[flat.pop(0) for _ in group] for group in groups]


def place_kernel(chips, where_ref, *refs):
    given, (grad_x_ref, grad_small_ref) = refs[:-2], refs[-2:]
    dps = where_ref.shape[0] - chips
    thin = grad_x_ref.shape[0] // dps
    columns = grad_x_ref.shape[1]
    for k in range(dps):
        target = pl.ds(pl.multiple_of(where_ref[chips + k] * thin, thin), thin)
        column = 0
        for n in range(0, len(given), 2):
            ref, at = (given[n], k) if k < dps // 2 else (given[n + 1], k - dps // 2)
            piece = ref[at * thin : (at + 1) * thin].astype(F32)
            width = min(piece.shape[1], columns - column)
            grad_x_ref[target, column : column + width] = piece[:, :width]
            column += width
            if piece.shape[1] > width:
                grad_small_ref[target, :] = piece[:, width : width + grad_small_ref.shape[1]]


def placed(chips, where, given, wide, channels, small):
    vmem = pl.BlockSpec(memory_space=pltpu.VMEM)
    return pl.pallas_call(
        functools.partial(place_kernel, chips),
        in_specs=[SCALARS] + [vmem] * len(given),
        out_shape=[
            jax.ShapeDtypeStruct((wide, channels), F32),
            jax.ShapeDtypeStruct((wide, small), F32),
        ],
        compiler_params=PARAMS,
        name="placed",
    )(where, *given)


def cut_groups(groups):
    sizes = [groups // 2, groups - groups // 2]
    return [(sum(sizes[:n]), size) for n, size in enumerate(sizes)]


def shards(hidden, x_weight, state_weight, log_rates, step_bias, out_gain, cotangent):
    h, cot = hidden[0], cotangent[0]
    rows, channels = h.shape
    chips = lax.axis_size("ctx") // 2
    place = lax.axis_index("ctx")
    dps, dp_place = lax.axis_size("dp"), lax.axis_index("dp")
    scalars = Scalars(chips).made()
    where = (place ^ (2 * jnp.arange(chips)), dp_place ^ jnp.array(by_bits(dps, bits_of(dps))))
    where = jnp.concatenate(where).astype(jnp.int32)
    peer_h = send(h, "ctx", 1)
    both, nat, lines, cg3, bf3, bt, weight3, tot3 = project_small(
        h, state_weight, log_rates, step_bias
    )
    x, ends = project(both, x_weight, bt, weight3, tot3)
    near = send(ends, "ctx", 1)
    raw_fwd = inner(0, x, nat, lines, ends)
    sums = merge(chips, scalars, raw_fwd, ends, near)
    arrived = exchange(chips, sums)
    left = turned(h, peer_h, where, chips, sums[0])
    raw_rc = inner(1, x, nat, lines, left)
    mixed, draw, ry, adj, dc0, s_in, tots, starts = normed(
        (raw_fwd, raw_rc), x, nat, cg3, out_gain, cot, scalars, ends, near, arrived
    )
    near = send(adj, "ctx", 1)
    sums = merge(chips, scalars, adj, adj, near, tots)
    arrived = exchange(chips, sums)
    edges = jnp.stack([place == 0, place == 2 * chips - 1]).astype(jnp.int32)
    u, db, dc = inner_back(x, draw, nat, lines, starts, edges, sums[0])

    bits = bits_of(chips)
    orders = [bits[n:] + bits[:n] for n in range(2)]
    blocks = [by_bits(chips, order) for order in orders]
    staying, going = [b[: chips // 2] for b in blocks], [b[chips // 2 :] for b in blocks]
    more = [nat, db, dc, dc0, ry, log_rates[None]]
    before = []

    def finished(first, groups, after):
        own, *partial = finish(
            first, groups, x, u, bf3, s_in, ends, tots, scalars, near, arrived, after, more, before
        )
        before.extend(partial)
        return own

    def terms(own, peer, size, picked, kind):
        cuts = [size * GROUP // 2, own.shape[1] - size * GROUP // 2]
        outs = weight_terms(left, own, peer, picked, cuts, kind, turn[0])
        turn[0] = outs[0]
        return outs

    def first_hop(go):
        return [send(part, "ctx", 2 * order[0]) for part, order in zip(go, orders)]

    (start, size), (start_next, size_next) = cut_groups(channels // GROUP)
    own = finished(start, size, db)
    turn = [before[-1]]
    peer = send(own, "ctx", 1)
    came = first_hop(terms(own, peer, size, going, BF))
    stay = terms(own, peer, size, staying, F32)
    own_next = finished(start_next, size_next, turn[0])
    (own_next,), came = together([own_next], came)
    turn[0] = own_next
    peer_next = send(own_next, "ctx", 1)
    ahead = summing(stay, came, orders, turn)
    hop = next(ahead)
    go, hop = together(terms(own_next, peer_next, size_next, going, BF), hop)
    came = first_hop(go)
    hop = ahead.send(hop)
    stay = terms(own_next, peer_next, size_next, staying, F32)
    hop, came = together(hop, came)
    behind = summing(stay, came, orders, turn)
    hop, hop_next = ahead.send(hop), next(behind)
    while isinstance(hop, list):
        hop, hop_next = together(hop, hop_next)
        hop, hop_next = ahead.send(hop), behind.send(hop_next)
    while isinstance(hop_next, list):
        hop_next = behind.send(hop_next)
    done = [*hop, *hop_next]
    wide = channels // (2 * chips)
    grad_x, grad_small = placed(chips, where, done, wide, channels, state_weight.shape[1])
    return (mixed[None], grad_x, grad_small)


def solution(mesh):
    return jax.shard_map(
        shards,
        mesh=mesh,
        in_specs=(P("dp", "ctx", None), P(), P(), P(), P(), P(), P("dp", "ctx", None)),
        out_specs=(P("dp", "ctx", None), P("ctx", None), P("ctx", None)),
        check_vma=False,
    )
```
